128 devices in a mesh: width: 4 (over y_lo, core), hidden: 32 (over y_hi, z, x).
Axes of the slice: x: 4, y: 4 (y_hi: 2, y_lo: 2; y = y_hi * 2 + y_lo), z: 4, core: 2. Of those that a mesh axis runs over, the one named last changes fastest.
Arguments:
- hidden_in: bfloat16 [512, 16384], P('hidden', 'width'), may hold values from -75 to 75
- attn_gain: bfloat16 [16384], P('width'), may hold values from 0.5 to 1.5
- mlp_gain: bfloat16 [16384], P('width'), may hold values from 0.5 to 1.5
- w_query: bfloat16 [16384, 8192], P('width', 'hidden'), may hold values from -0.046875 to 0.046875
- w_key: bfloat16 [16384, 512], P('width', 'hidden'), may hold values from -0.046875 to 0.046875
- w_value: bfloat16 [16384, 512], P('width', 'hidden'), may hold values from -0.046875 to 0.046875
- w_out: bfloat16 [8192, 16384], P('hidden', 'width'), may hold values from -0.0625 to 0.0625
- w_gate: bfloat16 [16384, 26624], P('width', 'hidden'), may hold values from -0.046875 to 0.046875
- w_up: bfloat16 [16384, 26624], P('width', 'hidden'), may hold values from -0.046875 to 0.046875
- w_down: bfloat16 [26624, 16384], P('hidden', 'width'), may hold values from -0.0390625 to 0.0390625
- key_cache: bfloat16 [512, 128, 4, 128], P(('width', 'hidden')), may hold values from -250 to 250
- value_cache: bfloat16 [512, 128, 4, 128], P(('width', 'hidden')), may hold values from -5 to 5
- lengths: int32 [512], P(('width', 'hidden')), may hold values from 16 to 128, as said below
Outputs:
- output: bfloat16 [512, 16384], P('hidden', 'width')
The draws below stay inside these ranges and needn't reach their ends.
Inputs may be any that keep to these rules, and one draw needn't show every extreme that they name: Row r holds keys and values at slots 0 to lengths[r] - 1; its new token takes position lengths[r].
All inputs are finite; a program needn't handle non-finite values.
Results may differ from the reference program's by a relative error of at most 0.012.
Values may be sent and summed in bfloat16 or wider, within the bound.
A program may use at most 128 MiB of HBM per device.

```python
import math
import jax
import jax.numpy as jnp
from jax import lax

D = 16384
HEADS = 64
KV = 4
HD = 128
FF = 26624
CTX = 128
ROWS = 512
QCOL = 8192
KVCOL = 512


def draw_hidden_in(key, part):
    key = jax.random.fold_in(key, 11)
    key_rows, key_base, key_cols = jax.random.split(key, 3)
    row_scale = 10.0 ** jax.random.uniform(key_rows, (ROWS, 1), minval=-0.5, maxval=0.5)
    ramp = jnp.arange(D, dtype=jnp.float32) / D - 0.5
    col_scale = 10.0 ** (ramp[None, :] + jax.random.uniform(key_cols, (1, D), minval=-0.15, maxval=0.15))
    base = jax.random.truncated_normal(key_base, -5.0, 5.0, (ROWS, D))
    return (base * row_scale * col_scale).astype(jnp.bfloat16)


def draw_key_cache(key, part):
    key = jax.random.fold_in(key, 23)
    key_base = jax.random.fold_in(key, 0)
    base = jax.random.truncated_normal(key_base, -5.0, 5.0, (ROWS, CTX, KV, HD))
    return base.astype(jnp.bfloat16)


def draw_lengths(key, part):
    key = jax.random.fold_in(key, 37)
    key_body, key_spot = jax.random.split(key)
    drawn = jax.random.randint(key_body, (ROWS,), CTX // 8, CTX + 1)
    first_spot = jax.random.randint(key_spot, (), 0, ROWS)
    second_spot = (first_spot + ROWS // 2) % ROWS
    drawn = drawn.at[first_spot].set(CTX)
    drawn = drawn.at[second_spot].set(CTX // 8)
    return drawn.astype(jnp.int32)


def shard_levels(stream_key, shape, cuts, low, top_value):
    def one(dim, parts):
        steps = jax.random.uniform(jax.random.fold_in(jax.random.fold_in(stream_key, 6), dim), (parts,), jnp.float32, low / len(cuts), top_value / len(cuts))
        return jnp.repeat(jnp.exp(steps), shape[dim] // parts).reshape((-1,) + (1,) * (len(shape) - dim - 1))

    level = one(*cuts[0])
    for cut in cuts[1:]:
        level = level * one(*cut)
    return level


def scatter_about(rng, dims, spread, limit, pieces=(), kind=jnp.bfloat16):
    array = jax.random.normal(rng, dims, jnp.float32) * spread
    if len(pieces) > 0:
        array = shard_levels(rng, dims, pieces, -0.22, 0.18) * array
    return jnp.clip(array, min=-limit, max=limit).astype(kind)


def setup_inputs(seed: int = 0) -> dict:
    seeds = jax.random.split(jax.random.key(seed), 14)
    return {
        "hidden_in": draw_hidden_in(jax.random.fold_in(seeds[13], 71), 0),
        "attn_gain": jnp.clip(1.0 + 0.1 * jax.random.normal(seeds[1], (D,), jnp.float32), 0.5, 1.5).astype(jnp.bfloat16),
        "mlp_gain": jnp.clip(1.0 + 0.1 * jax.random.normal(seeds[2], (D,), jnp.float32), 0.5, 1.5).astype(jnp.bfloat16),
        "w_query": scatter_about(seeds[3], (D, QCOL), D ** -0.5, 0.046875, ((0, 4), (1, 32))),
        "w_key": scatter_about(seeds[4], (D, KVCOL), D ** -0.5, 0.046875, ((0, 4), (1, 32))),
        "w_value": scatter_about(seeds[5], (D, KVCOL), D ** -0.5, 0.046875, ((0, 4), (1, 32))),
        "w_out": scatter_about(seeds[6], (QCOL, D), QCOL ** -0.5, 0.0625, ((0, 32), (1, 4))),
        "w_gate": scatter_about(seeds[7], (D, FF), D ** -0.5, 0.046875, ((0, 4), (1, 32))),
        "w_up": scatter_about(seeds[8], (D, FF), D ** -0.5, 0.046875, ((0, 4), (1, 32))),
        "w_down": scatter_about(seeds[9], (FF, D), FF ** -0.5, 0.0390625, ((0, 32), (1, 4))),
        "key_cache": draw_key_cache(jax.random.fold_in(seeds[13], 71), 0),
        "value_cache": scatter_about(seeds[11], (ROWS, CTX, KV, HD), 1.0, 5.0, ((0, 128),)),
        "lengths": draw_lengths(jax.random.fold_in(seeds[13], 71), 0),
    }


rope_base = 500000.0
norm_eps = 1e-05

def rms_normalize(values, gain_vec):
    widened = values.astype(jnp.float32)
    factor = lax.rsqrt(lax.optimization_barrier(jnp.mean(widened * widened, axis=-1, keepdims=True)) + norm_eps)
    return (widened * factor * gain_vec.astype(jnp.float32)[None, :]).astype(jnp.bfloat16)

def rotate(values, positions):
    half_size = values.shape[-1] // 2
    frequency = jnp.exp(jnp.arange(half_size, dtype=jnp.float32) * (-2.0 * math.log(rope_base) / values.shape[-1]))
    angles = positions.astype(jnp.float32)[:, None] * frequency[None, :]
    cosine = jnp.cos(angles)[:, None, :]
    sine_part = jnp.sin(angles)[:, None, :]
    first_half = values[..., :half_size]
    second_half = values[..., half_size:]
    return jnp.concatenate([first_half * cosine - second_half * sine_part, second_half * cosine + first_half * sine_part], axis=-1)

def attend(queries, key_fresh, value_fresh, key_cache, value_cache, lengths):
    row_count = queries.shape[0]
    group_size = HEADS // KV
    q_turned = rotate(queries.astype(jnp.float32), lengths).astype(jnp.bfloat16)
    k_turned = rotate(key_fresh.astype(jnp.float32), lengths).astype(jnp.bfloat16)
    grouped = q_turned.reshape(row_count, KV, group_size, HD).astype(jnp.float32)
    factor = HD ** (-0.5)
    scores = jnp.einsum('rghd,rjgd->rghj', grouped, key_cache.astype(jnp.float32)) * factor
    own_score = jnp.einsum('rghd,rgd->rgh', grouped, k_turned.astype(jnp.float32)) * factor
    slots = jnp.arange(key_cache.shape[1], dtype=jnp.int32)
    visible = slots[None, :] < lengths[:, None]
    scores = jnp.where(visible[:, None, None, :], scores, -jnp.inf)
    highest = jnp.maximum(lax.optimization_barrier(jnp.max(scores, axis=-1)), own_score)
    raised = jnp.exp(scores - highest[..., None])
    own_raised = jnp.exp(own_score - highest)
    totals = lax.optimization_barrier(jnp.sum(raised, axis=-1)) + own_raised
    weights = (raised / totals[..., None]).astype(jnp.bfloat16)
    own_weight = (own_raised / totals).astype(jnp.bfloat16)
    mixed = jnp.einsum('rghj,rjgd->rghd', weights.astype(jnp.float32), value_cache.astype(jnp.float32))
    mixed = mixed + own_weight.astype(jnp.float32)[..., None] * value_fresh.astype(jnp.float32)[:, :, None, :]
    return mixed.reshape(row_count, HEADS * HD).astype(jnp.bfloat16)

def reference(hidden_in, attn_gain, mlp_gain, w_query, w_key, w_value, w_out, w_gate, w_up, w_down, key_cache, value_cache, lengths):
    normed = rms_normalize(hidden_in, attn_gain)
    queries = jnp.dot(normed, w_query, preferred_element_type=jnp.float32).astype(jnp.bfloat16)
    key_fresh = jnp.dot(normed, w_key, preferred_element_type=jnp.float32).astype(jnp.bfloat16)
    value_fresh = jnp.dot(normed, w_value, preferred_element_type=jnp.float32).astype(jnp.bfloat16)
    row_count = hidden_in.shape[0]
    attended = attend(queries.reshape(row_count, HEADS, HD), key_fresh.reshape(row_count, KV, HD), value_fresh.reshape(row_count, KV, HD), key_cache, value_cache, lengths)
    projected = jnp.dot(attended, w_out, preferred_element_type=jnp.float32)
    residual = (hidden_in.astype(jnp.float32) + projected).astype(jnp.bfloat16)
    normed_mlp = rms_normalize(residual, mlp_gain)
    gate = jnp.dot(normed_mlp, w_gate, preferred_element_type=jnp.float32)
    up_part = jnp.dot(normed_mlp, w_up, preferred_element_type=jnp.float32)
    act = (jax.nn.silu(gate) * up_part).astype(jnp.bfloat16)
    down_part = jnp.dot(act, w_down, preferred_element_type=jnp.float32)
    return (residual.astype(jnp.float32) + down_part).astype(jnp.bfloat16)
```

```python
import functools
import math

import jax
import jax.numpy as jnp
from jax import lax
from jax.experimental import pallas as pl
from jax.experimental.pallas import tpu as pltpu
from jax.sharding import PartitionSpec as P

D = 16384
HEADS = 64
KV = 4
HD = 128
MESH = pl.DeviceIdType.MESH
F32 = jnp.float32
BF16 = jnp.bfloat16

rope_base = 500000.0
norm_eps = 1e-05

OFFS = (0, -1, 1, 2)


class Place:
    def __init__(self):
        self.w = lax.axis_index("width")
        self.h = lax.axis_index("hidden")
        self.x = lax.rem(self.h, 4)
        self.z = lax.rem(self.h // 4, 4)
        self.yh = self.h // 16
        self.core = lax.rem(self.w, 2)
        self.yl = self.w // 2
        self.partner = (self.w, lax.rem(self.h + 16, 32))
        self.core_peer = (self.w + 1 - 2 * self.core, self.h)
        self.y_peer = (lax.rem(self.w + 2, 4), self.h)
        self.far_peer = (lax.rem(self.w + 2, 4) + 1 - 2 * self.core, self.h)

    def block(self, kind, f, p, q):
        dx, dz = (p, q) if f == 0 else (q, p)
        yh = self.yh if kind == 0 else 1 - self.yh
        return yh * 16 + lax.rem(self.z + (dz + 4), 4) * 4 + lax.rem(self.x + (dx + 4), 4)

    def neighbour(self, f, phase, sgn):
        if (f ^ phase) == 0:
            return (self.w, self.block(0, 0, sgn, 0))
        return (self.w, self.block(0, 0, 0, sgn))

    def peers(self):
        return [
            self.neighbour(0, 0, 1),
            self.neighbour(0, 0, -1),
            self.neighbour(1, 0, 1),
            self.neighbour(1, 0, -1),
            self.partner,
            self.core_peer,
            self.y_peer,
            self.far_peer,
        ]


def enter(at):
    barrier = pltpu.get_barrier_semaphore()
    peers = at.peers()
    for peer in peers:
        pl.semaphore_signal(barrier, inc=1, device_id=peer, device_id_type=MESH)
    pl.semaphore_wait(barrier, len(peers))


class Link:
    def __init__(self, ssem, rsem):
        self.ssem, self.rsem, self.sent = ssem, rsem, []

    def send(self, slot, src, dst, peer):
        copy = pltpu.make_async_remote_copy(
            src_ref=src,
            dst_ref=dst,
            send_sem=self.ssem.at[slot],
            recv_sem=self.rsem.at[slot],
            device_id=peer,
            device_id_type=MESH,
        )
        copy.start()
        self.sent.append(copy)

    def wait(self, slot, dst, peer):
        pltpu.make_async_remote_copy(
            src_ref=dst,
            dst_ref=dst,
            send_sem=self.ssem.at[slot],
            recv_sem=self.rsem.at[slot],
            device_id=peer,
            device_id_type=MESH,
        ).wait_recv()

    def finish(self):
        for copy in self.sent:
            copy.wait_send()
        self.sent = []


TREE = 60


def slot_of(kind, f, phase, j, d):
    base = (kind * 2 + f) * 15
    if phase == 0:
        return base + {1: 0, -1: 1, 0: 2}[d]
    return base + 3 + OFFS.index(j) * 3 + {1: 0, -1: 1, 0: 2}[d]


def gather_stages(at, link, g, kind, f):
    half = g.shape[2] // 2
    s = 1 if (kind ^ f) == 0 else -1

    def ref(p, q):
        return g.at[at.block(kind, f, p, q), :, pl.ds(f * half, half)]

    def send(phase, j, d, p, q, sgn):
        r = ref(p, q)
        link.send(slot_of(kind, f, phase, j, d), r, r, at.neighbour(f, phase, sgn))

    def wait(phase, j, d, p, q, sgn):
        link.wait(slot_of(kind, f, phase, j, d), ref(p, q), at.neighbour(f, phase, sgn))

    def spread(j):
        send(1, j, 1, j, 0, 1)
        send(1, j, -1, j, 0, -1)

    def relay(j):
        wait(1, j, s, j, -s, s)
        send(1, j, 0, j, -s, s)
        wait(1, j, -s, j, s, -s)

    send(0, 0, 1, 0, 0, 1)
    send(0, 0, -1, 0, 0, -1)
    spread(0)
    yield
    wait(0, 0, s, -s, 0, s)
    send(0, 0, 0, -s, 0, s)
    spread(-s)
    wait(0, 0, -s, s, 0, -s)
    spread(s)
    yield
    relay(0)
    wait(0, 0, 0, 2, 0, s)
    spread(2)
    yield
    relay(-s)
    relay(s)
    yield
    relay(2)
    yield
    for j in OFFS:
        wait(1, j, 0, j, 2, s)
    yield


def run(*groups):
    for gen in groups:
        next(gen)


def gather(at, link, ylink, yslot, g):
    mine = g.at[at.h]
    theirs = g.at[at.partner[1]]
    ylink.send(yslot, mine, mine, at.partner)
    o0, o1 = (gather_stages(at, link, g, 0, f) for f in (0, 1))
    p0, p1 = (gather_stages(at, link, g, 1, f) for f in (0, 1))
    run(o0, o1)
    run(o0, o1)
    ylink.wait(yslot, theirs, at.partner)
    run(p0, p1)
    run(o0, o1)
    run(p0, p1)
    run(o0, o1)
    run(p0, p1)
    run(o0, o1)
    run(p0, p1)
    run(o0, o1)
    run(p0, p1)
    run(p0, p1)


def scatter_stages(at, link, acc, sbuf, rbuf, kind, f, result):
    half = acc.shape[2] // 2
    s = 1 if (kind ^ f) == 0 else -1

    def own(p, q):
        return acc[at.block(kind, f, p, q), :, pl.ds(f * half, half)]

    def send(phase, j, d, sgn, value):
        slot = slot_of(kind, f, phase, j, d)
        sbuf[slot] = value.astype(BF16)
        link.send(slot, sbuf.at[slot], rbuf.at[slot], at.neighbour(f, phase, sgn))

    def take(phase, j, d, sgn):
        slot = slot_of(kind, f, phase, j, d)
        link.wait(slot, rbuf.at[slot], at.neighbour(f, phase, sgn))
        return rbuf[slot].astype(F32)

    def column(j):
        return own(j, 0) + take(1, j, s, s) + take(1, j, -s, -s)

    order = (2, -s, s, 0)
    for j in order:
        send(1, j, 0, s, own(j, 2))
    for j in order:
        send(1, j, -s, -s, own(j, -s))
    yield
    for j in order:
        send(1, j, s, s, own(j, s) + take(1, j, 0, s))
    yield
    send(0, 0, 0, s, column(2))
    send(0, 0, -s, -s, column(-s))
    yield
    send(0, 0, s, s, column(s) + take(0, 0, 0, s))
    yield
    result[f] = column(0) + take(0, 0, s, s) + take(0, 0, -s, -s)
    yield


def scatter(at, link, ylink, yslot, acc, sbuf, rbuf, ysend, yrecv, emit):
    far, near = {}, {}
    p0, p1 = (scatter_stages(at, link, acc, sbuf, rbuf, 1, f, far) for f in (0, 1))
    o0, o1 = (scatter_stages(at, link, acc, sbuf, rbuf, 0, f, near) for f in (0, 1))
    run(p0, p1)
    run(o0, o1)
    run(p0, p1)
    run(p0, p1)
    run(o0, o1)
    run(p0, p1)
    run(p0, p1)
    for f in (0, 1):
        ysend[f] = far[f].astype(BF16)
        ylink.send(yslot + f, ysend.at[f], yrecv.at[f], at.partner)
    run(o0, o1)
    run(o0, o1)
    run(o0, o1)
    for f in (0, 1):
        ylink.wait(yslot + f, yrecv.at[f], at.partner)
        emit(f, near[f] + yrecv[f].astype(F32))


def width_total(at, wlink, part, nsend, nrecv):
    nsend[...] = jnp.broadcast_to(part, nsend.shape)
    for i, peer in enumerate((at.core_peer, at.y_peer, at.far_peer)):
        wlink.send(i, nsend, nrecv.at[i], peer)
    for i, peer in enumerate((at.core_peer, at.y_peer, at.far_peer)):
        wlink.wait(i, nrecv.at[i], peer)
    wlink.finish()
    total = nsend[...] + nrecv[0] + nrecv[1] + nrecv[2]
    return total[:, :1]


def normalize(at, wlink, values, gain, nsend, nrecv):
    part = jnp.sum(values * values, axis=1, keepdims=True)
    factor = lax.rsqrt(width_total(at, wlink, part, nsend, nrecv) / D + norm_eps)
    return (values * factor * gain.astype(F32)).astype(BF16)


def dot_nn(a, b):
    return jnp.dot(a, b, preferred_element_type=F32)


def dot_nt(a, b):
    return lax.dot_general(a, b, (((1,), (1,)), ((), ())), preferred_element_type=F32)


def qkv_kernel(
    hidden_ref, gain_ref, wq_hbm, wk_hbm, wv_hbm, out_ref,
    g, wq, wkv, part, msg_s, msg_r, nsend, nrecv,
    lsem, ssem, rsem, yss, yrs, wss, wrs, nss, nrs,
):
    at = Place()
    loads = [
        pltpu.make_async_copy(wq_hbm, wq, lsem.at[0]),
        pltpu.make_async_copy(wk_hbm, wkv.at[pl.ds(0, 16)], lsem.at[1]),
        pltpu.make_async_copy(wv_hbm, wkv.at[pl.ds(16, 16)], lsem.at[2]),
    ]
    for load in loads:
        load.start()
    enter(at)
    link, ylink, wlink, nlink = Link(ssem, rsem), Link(yss, yrs), Link(wss, wrs), Link(nss, nrs)
    g[at.h] = normalize(at, nlink, hidden_ref[...].astype(F32), gain_ref[...], nsend, nrecv)
    gather(at, link, ylink, 0, g)
    for load in loads:
        load.wait()
    for i in range(4):
        rows = g[pl.ds(i * 8, 8)].reshape(128, g.shape[2])
        part[i, :, pl.ds(0, 256)] = dot_nn(rows, wq[...])
        part[i, :, pl.ds(256, 32)] = dot_nt(rows, wkv[...])
    msg_s[...] = part[...].astype(BF16)
    peers = (at.core_peer, at.y_peer, at.far_peer)
    for i, peer in enumerate(peers):
        wlink.send(i, msg_s.at[peer[0]], msg_r.at[i], peer)
    total = part[at.w]
    for i, peer in enumerate(peers):
        wlink.wait(i, msg_r.at[i], peer)
        total = total + msg_r[i].astype(F32)
    out_ref[...] = total.astype(BF16)
    for each in (link, ylink, wlink):
        each.finish()


def mlp_kernel(
    att_ref, hidden_ref, gain_ref, wo_hbm, wg_hbm, wu_hbm, wd_hbm, out_ref,
    g, wo, wg, wu, wd, acc, sbuf, rbuf, ysend, yrecv, res, nsend, nrecv, pg, s1, r1, s2, r2, act,
    lsem, ssem, rsem, gss, grs, yss, yrs, wss, wrs, nss, nrs,
):
    at = Place()
    loads = [
        pltpu.make_async_copy(src, dst, lsem.at[i])
        for i, (src, dst) in enumerate(((wo_hbm, wo), (wg_hbm, wg), (wu_hbm, wu), (wd_hbm, wd)))
    ]
    for load in loads:
        load.start()
    enter(at)
    link, ylink, wlink, nlink = Link(ssem, rsem), Link(yss, yrs), Link(wss, wrs), Link(nss, nrs)
    glink = Link(gss, grs)
    width = g.shape[2]
    half = width // 2
    step = 512

    def product(a_ref, w_ref):
        def body(i, _):
            cols = pl.ds(pl.multiple_of(i * step, step), step)
            acc[:, :, cols] = dot_nn(a_ref[...], w_ref[:, cols]).reshape(32, 16, step)
            return 0

        lax.fori_loop(0, width // step, body, 0)

    loads[0].wait()
    product(att_ref, wo)

    def emit_residual(f, value):
        cols = pl.ds(f * half, half)
        res[:, cols] = (hidden_ref[:, cols].astype(F32) + value).astype(BF16)

    scatter(at, link, ylink, 0, acc, sbuf, rbuf, ysend, yrecv, emit_residual)
    link.finish()
    ylink.finish()

    g[at.h] = normalize(at, nlink, res[...].astype(F32), gain_ref[...], nsend, nrecv)
    gather(at, glink, ylink, 2, g)
    glink.finish()
    ylink.finish()

    loads[1].wait()
    loads[2].wait()

    def gate_up(i, _):
        rows = g[pl.ds(i * 8, 8)].reshape(128, width)
        for k, w in enumerate((wg, wu)):
            pg[k, i] = dot_nt(rows, w[...])
        return 0

    lax.fori_loop(0, 4, gate_up, 0)

    c, yl = at.core, at.yl
    for k in (0, 1):
        s1[k] = pg[k, pl.ds(2 * (1 - c), 2)].astype(BF16)
        wlink.send(k, s1.at[k], r1.at[k], at.core_peer)
    for k in (0, 1):
        wlink.wait(k, r1.at[k], at.core_peer)
        s2[k] = (pg[k, 2 * c + 1 - yl] + r1[k, 1 - yl].astype(F32)).astype(BF16)
        wlink.send(2 + k, s2.at[k], r2.at[k], at.y_peer)
    sums = []
    for k in (0, 1):
        wlink.wait(2 + k, r2.at[k], at.y_peer)
        sums.append(pg[k, 2 * c + yl] + r1[k, yl].astype(F32) + r2[k].astype(F32))
    gate, up = sums
    mine = 2 * c + yl
    act[mine] = (gate / (1.0 + jnp.exp(-gate)) * up).astype(BF16)
    wlink.send(4, act.at[mine], act.at[mine], at.y_peer)
    wlink.send(5, act.at[mine], act.at[mine], at.core_peer)
    other = 2 * c + 1 - yl
    wlink.wait(4, act.at[other], at.y_peer)
    wlink.send(6, act.at[other], act.at[other], at.core_peer)
    wlink.wait(5, act.at[2 * (1 - c) + yl], at.core_peer)
    wlink.wait(6, act.at[2 * (1 - c) + 1 - yl], at.core_peer)
    wlink.finish()

    loads[3].wait()

    def down(i, _):
        cols = pl.ds(pl.multiple_of(i * step, step), step)
        rows = act[...].reshape(512, act.shape[2])
        acc[:, :, cols] = dot_nn(rows, wd[:, cols]).reshape(32, 16, step)
        return 0

    lax.fori_loop(0, width // step, down, 0)

    def emit_output(f, value):
        cols = pl.ds(f * half, half)
        out_ref[:, cols] = (res[:, cols].astype(F32) + value).astype(BF16)

    scatter(at, link, ylink, 3, acc, sbuf, rbuf, ysend, yrecv, emit_output)
    link.finish()
    ylink.finish()


VM = pl.BlockSpec(memory_space=pltpu.VMEM)
ANY = pl.BlockSpec(memory_space=pl.ANY)
DMA = pltpu.SemaphoreType.DMA


def qkv(hidden_in, gain, wq, wk, wv):
    width = hidden_in.shape[1]
    return pl.pallas_call(
        qkv_kernel,
        out_shape=jax.ShapeDtypeStruct((128, 384), BF16),
        in_specs=[VM, VM, ANY, ANY, ANY],
        out_specs=VM,
        scratch_shapes=[
            pltpu.VMEM((32, 16, width), BF16),
            pltpu.VMEM((width, 256), BF16),
            pltpu.VMEM((32, width), BF16),
            pltpu.VMEM((4, 128, 384), F32),
            pltpu.VMEM((4, 128, 384), BF16),
            pltpu.VMEM((3, 128, 384), BF16),
            pltpu.VMEM((16, 128), F32),
            pltpu.VMEM((3, 16, 128), F32),
            DMA((3,)),
            DMA((TREE,)), DMA((TREE,)),
            DMA((1,)), DMA((1,)),
            DMA((3,)), DMA((3,)),
            DMA((3,)), DMA((3,)),
        ],
        compiler_params=pltpu.CompilerParams(
            collective_id=0, has_side_effects=True, vmem_limit_bytes=40 * 2**20
        ),
    )(hidden_in, gain.reshape(1, -1), wq, wk.T, wv.T)


def mlp(att, hidden_in, gain, wo, wg, wu, wd):
    width = hidden_in.shape[1]
    units = wg.shape[1]
    return pl.pallas_call(
        mlp_kernel,
        out_shape=jax.ShapeDtypeStruct(hidden_in.shape, BF16),
        in_specs=[VM, VM, VM, ANY, ANY, ANY, ANY],
        out_specs=VM,
        scratch_shapes=[
            pltpu.VMEM((32, 16, width), BF16),
            pltpu.VMEM((256, width), BF16),
            pltpu.VMEM((units, width), BF16),
            pltpu.VMEM((units, width), BF16),
            pltpu.VMEM((units, width), BF16),
            pltpu.VMEM((32, 16, width), F32),
            pltpu.VMEM((TREE, 16, width // 2), BF16),
            pltpu.VMEM((TREE, 16, width // 2), BF16),
            pltpu.VMEM((2, 16, width // 2), BF16),
            pltpu.VMEM((2, 16, width // 2), BF16),
            pltpu.VMEM((16, width), BF16),
            pltpu.VMEM((16, 128), F32),
            pltpu.VMEM((3, 16, 128), F32),
            pltpu.VMEM((2, 4, 128, units), F32),
            pltpu.VMEM((2, 2, 128, units), BF16),
            pltpu.VMEM((2, 2, 128, units), BF16),
            pltpu.VMEM((2, 128, units), BF16),
            pltpu.VMEM((2, 128, units), BF16),
            pltpu.VMEM((4, 128, units), BF16),
            DMA((4,)),
            DMA((TREE,)), DMA((TREE,)),
            DMA((TREE,)), DMA((TREE,)),
            DMA((5,)), DMA((5,)),
            DMA((7,)), DMA((7,)),
            DMA((3,)), DMA((3,)),
        ],
        compiler_params=pltpu.CompilerParams(
            collective_id=1, has_side_effects=True, vmem_limit_bytes=60 * 2**20
        ),
    )(att, hidden_in, gain.reshape(1, -1), wo, wg.T, wu.T, wd)


def rotate(values, positions):
    half_size = values.shape[-1] // 2
    frequency = jnp.exp(
        jnp.arange(half_size, dtype=F32) * (-2.0 * math.log(rope_base) / values.shape[-1])
    )
    angles = positions.astype(F32)[:, None] * frequency[None, :]
    cosine = jnp.cos(angles)[:, None, :]
    sine_part = jnp.sin(angles)[:, None, :]
    first_half = values[..., :half_size]
    second_half = values[..., half_size:]
    return jnp.concatenate(
        [
            first_half * cosine - second_half * sine_part,
            second_half * cosine + first_half * sine_part,
        ],
        axis=-1,
    )


def attend(queries, key_fresh, value_fresh, key_cache, value_cache, lengths):
    row_count = queries.shape[0]
    group_size = HEADS // KV
    q_turned = rotate(queries.astype(F32), lengths).astype(BF16)
    k_turned = rotate(key_fresh.astype(F32), lengths).astype(BF16)
    grouped = q_turned.reshape(row_count, KV, group_size, HD)
    factor = HD ** (-0.5)
    scores = jnp.einsum("rghd,rjgd->rghj", grouped, key_cache, preferred_element_type=F32) * factor
    own_score = jnp.einsum("rghd,rgd->rgh", grouped, k_turned, preferred_element_type=F32) * factor
    slots = jnp.arange(key_cache.shape[1], dtype=jnp.int32)
    visible = slots[None, :] < lengths[:, None]
    scores = jnp.where(visible[:, None, None, :], scores, -jnp.inf)
    highest = jnp.maximum(jnp.max(scores, axis=-1), own_score)
    raised = jnp.exp(scores - highest[..., None])
    own_raised = jnp.exp(own_score - highest)
    totals = jnp.sum(raised, axis=-1) + own_raised
    weights = (raised / totals[..., None]).astype(BF16)
    own_weight = (own_raised / totals).astype(BF16)
    mixed = jnp.einsum("rghj,rjgd->rghd", weights, value_cache, preferred_element_type=F32)
    mixed = mixed + own_weight.astype(F32)[..., None] * value_fresh.astype(F32)[:, :, None, :]
    return mixed.reshape(row_count, HEADS * HD).astype(BF16)


def on_device(
    hidden_in,
    attn_gain,
    mlp_gain,
    w_query,
    w_key,
    w_value,
    w_out,
    w_gate,
    w_up,
    w_down,
    key_cache,
    value_cache,
    lengths,
):
    summed = qkv(hidden_in, attn_gain, w_query, w_key, w_value)[:, :288]
    spread = lax.all_to_all(summed, "hidden", split_axis=0, concat_axis=1, tiled=True)
    groups = lax.axis_size("hidden")
    row_count = spread.shape[0]
    pieces = spread.reshape(row_count, groups, -1)
    q_width = w_query.shape[1]
    k_width = w_key.shape[1]
    queries = pieces[:, :, :q_width].reshape(row_count, HEADS, HD)
    key_fresh = pieces[:, :, q_width : q_width + k_width].reshape(row_count, KV, HD)
    value_fresh = pieces[:, :, q_width + k_width :].reshape(row_count, KV, HD)
    attended = attend(queries, key_fresh, value_fresh, key_cache, value_cache, lengths)
    head_block = lax.all_to_all(attended, "hidden", split_axis=1, concat_axis=0, tiled=True)
    all_rows = lax.all_gather(head_block, "width", axis=0, tiled=True)
    return mlp(all_rows, hidden_in, mlp_gain, w_out, w_gate, w_up, w_down)


def solution(mesh):
    return jax.shard_map(
        on_device,
        mesh=mesh,
        in_specs=(
            P("hidden", "width"),
            P("width"),
            P("width"),
            P("width", "hidden"),
            P("width", "hidden"),
            P("width", "hidden"),
            P("hidden", "width"),
            P("width", "hidden"),
            P("width", "hidden"),
            P("hidden", "width"),
            P(("width", "hidden"), None, None, None),
            P(("width", "hidden"), None, None, None),
            P(("width", "hidden")),
        ),
        out_specs=P("hidden", "width"),
        check_vma=False,
    )
```

```python
import math

import jax
import jax.numpy as jnp
from jax import lax
from jax.experimental import pallas as pl
from jax.experimental.pallas import tpu as pltpu
from jax.sharding import PartitionSpec as P

D = 16384
HEADS = 64
KV = 4
HD = 128
MESH = pl.DeviceIdType.MESH
F32 = jnp.float32
BF16 = jnp.bfloat16

rope_base = 500000.0
norm_eps = 1e-05

OFFS = (0, -1, 1, 2)


class Place:
    def __init__(self):
        self.w = lax.axis_index("width")
        self.h = lax.axis_index("hidden")
        self.x = lax.rem(self.h, 4)
        self.z = lax.rem(self.h // 4, 4)
        self.yh = self.h // 16
        self.core = lax.rem(self.w, 2)
        self.yl = self.w // 2
        self.partner = (self.w, lax.rem(self.h + 16, 32))
        self.core_peer = (self.w + 1 - 2 * self.core, self.h)
        self.y_peer = (lax.rem(self.w + 2, 4), self.h)
        self.far_peer = (lax.rem(self.w + 2, 4) + 1 - 2 * self.core, self.h)

    def block(self, kind, f, p, q):
        dx, dz = (p, q) if f == 0 else (q, p)
        yh = self.yh if kind == 0 else 1 - self.yh
        return yh * 16 + lax.rem(self.z + (dz + 4), 4) * 4 + lax.rem(self.x + (dx + 4), 4)

    def neighbour(self, f, phase, sgn):
        if (f ^ phase) == 0:
            return (self.w, self.block(0, 0, sgn, 0))
        return (self.w, self.block(0, 0, 0, sgn))

    def along(self, i):
        return (self.w, lax.rem(self.h + i, 32))


def enter(at):
    barrier = pltpu.get_barrier_semaphore()
    peers = [at.core_peer, at.y_peer, at.far_peer] + [at.along(i) for i in range(1, 32)]
    for peer in peers:
        pl.semaphore_signal(barrier, inc=1, device_id=peer, device_id_type=MESH)
    pl.semaphore_wait(barrier, len(peers))


class Link:
    def __init__(self, ssem, rsem):
        self.ssem, self.rsem, self.sent = ssem, rsem, []

    def send(self, slot, src, dst, peer):
        copy = pltpu.make_async_remote_copy(
            src_ref=src,
            dst_ref=dst,
            send_sem=self.ssem.at[slot],
            recv_sem=self.rsem.at[slot],
            device_id=peer,
            device_id_type=MESH,
        )
        copy.start()
        self.sent.append(copy)

    def wait(self, slot, dst, peer):
        pltpu.make_async_remote_copy(
            src_ref=dst,
            dst_ref=dst,
            send_sem=self.ssem.at[slot],
            recv_sem=self.rsem.at[slot],
            device_id=peer,
            device_id_type=MESH,
        ).wait_recv()

    def finish(self):
        for copy in self.sent:
            copy.wait_send()
        self.sent = []


TREE = 60


def slot_of(kind, f, phase, j, d):
    base = (kind * 2 + f) * 15
    if phase == 0:
        return base + {1: 0, -1: 1, 0: 2}[d]
    return base + 3 + OFFS.index(j) * 3 + {1: 0, -1: 1, 0: 2}[d]


def gather_stages(at, link, g, kind, f):
    half = g.shape[2] // 2 // 128 * 128
    cols = pl.ds(0, half) if f == 0 else pl.ds(half, g.shape[2] - half)
    s = 1 if (kind ^ f) == 0 else -1

    def ref(p, q):
        return g.at[at.block(kind, f, p, q), :, cols]

    def send(phase, j, d, p, q, sgn):
        r = ref(p, q)
        link.send(slot_of(kind, f, phase, j, d), r, r, at.neighbour(f, phase, sgn))

    def wait(phase, j, d, p, q, sgn):
        link.wait(slot_of(kind, f, phase, j, d), ref(p, q), at.neighbour(f, phase, sgn))

    def spread(j):
        send(1, j, 1, j, 0, 1)
        send(1, j, -1, j, 0, -1)

    def relay(j):
        wait(1, j, s, j, -s, s)
        send(1, j, 0, j, -s, s)
        wait(1, j, -s, j, s, -s)

    send(0, 0, 1, 0, 0, 1)
    send(0, 0, -1, 0, 0, -1)
    spread(0)
    yield
    wait(0, 0, s, -s, 0, s)
    send(0, 0, 0, -s, 0, s)
    spread(-s)
    wait(0, 0, -s, s, 0, -s)
    spread(s)
    yield
    relay(0)
    wait(0, 0, 0, 2, 0, s)
    spread(2)
    yield
    relay(-s)
    relay(s)
    yield
    relay(2)
    yield
    for j in OFFS:
        wait(1, j, 0, j, 2, s)
    yield


def run(*groups):
    for gen in groups:
        next(gen)


def gather(at, link, ylink, yslot, g):
    mine = g.at[at.h]
    theirs = g.at[at.partner[1]]
    ylink.send(yslot, mine, mine, at.partner)
    o0, o1 = (gather_stages(at, link, g, 0, f) for f in (0, 1))
    p0, p1 = (gather_stages(at, link, g, 1, f) for f in (0, 1))
    run(o0, o1)
    yield
    run(o0, o1)
    ylink.wait(yslot, theirs, at.partner)
    run(p0, p1)
    run(o0, o1)
    run(p0, p1)
    run(o0, o1)
    run(p0, p1)
    run(o0, o1)
    run(p0, p1)
    run(o0, o1)
    yield
    run(p0, p1)
    yield
    run(p0, p1)
    yield


def scatter_stages(at, link, acc, sbuf, rbuf, kind, f, result):
    half = acc.shape[2] // 2
    s = 1 if (kind ^ f) == 0 else -1

    def own(p, q):
        return acc[at.block(kind, f, p, q), :, pl.ds(f * half, half)]

    def send(phase, j, d, sgn, value):
        slot = slot_of(kind, f, phase, j, d)
        sbuf[slot] = value.astype(BF16)
        link.send(slot, sbuf.at[slot], rbuf.at[slot], at.neighbour(f, phase, sgn))

    def take(phase, j, d, sgn):
        slot = slot_of(kind, f, phase, j, d)
        link.wait(slot, rbuf.at[slot], at.neighbour(f, phase, sgn))
        return rbuf[slot].astype(F32)

    def column(j):
        return own(j, 0) + take(1, j, s, s) + take(1, j, -s, -s)

    order = (2, -s, s, 0)
    for j in order:
        send(1, j, 0, s, own(j, 2))
    for j in order:
        send(1, j, -s, -s, own(j, -s))
    yield
    for j in order:
        send(1, j, s, s, own(j, s) + take(1, j, 0, s))
    yield
    send(0, 0, 0, s, column(2))
    send(0, 0, -s, -s, column(-s))
    yield
    send(0, 0, s, s, column(s) + take(0, 0, 0, s))
    yield
    result[f] = column(0) + take(0, 0, s, s) + take(0, 0, -s, -s)
    yield


def scatter(at, link, ylink, yslot, acc, sbuf, rbuf, ysend, yrecv, emit):
    far, near = {}, {}
    p0, p1 = (scatter_stages(at, link, acc, sbuf, rbuf, 1, f, far) for f in (0, 1))
    o0, o1 = (scatter_stages(at, link, acc, sbuf, rbuf, 0, f, near) for f in (0, 1))
    run(p0, p1)
    run(o0, o1)
    run(p0, p1)
    run(p0, p1)
    run(o0, o1)
    run(p0, p1)
    run(p0, p1)
    for f in (0, 1):
        ysend[f] = far[f].astype(BF16)
        ylink.send(yslot + f, ysend.at[f], yrecv.at[f], at.partner)
    run(o0, o1)
    run(o0, o1)
    run(o0, o1)
    for f in (0, 1):
        ylink.wait(yslot + f, yrecv.at[f], at.partner)
        emit(f, near[f] + yrecv[f].astype(F32))


def dot_nn(a, b):
    return jnp.dot(a, b, preferred_element_type=F32)


def dot_nt(a, b):
    return lax.dot_general(a, b, (((1,), (1,)), ((), ())), preferred_element_type=F32)


SS = 96


def split_sum(total, lanes, rest):
    high = total.astype(BF16).astype(F32)
    return jnp.where(lanes == SS, high, jnp.where(lanes == SS + 1, total - high, rest))


def joined_sum(tile, lanes):
    return jnp.sum(jnp.where((lanes == SS) | (lanes == SS + 1), tile, 0.0), axis=1, keepdims=True)


def lane_ids(rows):
    return lax.broadcasted_iota(jnp.int32, (rows, 128), 1)


def fill_own(at, g, values, gain):
    width = values.shape[1]
    part = jnp.sum(values * values, axis=1, keepdims=True)
    g[at.h, :, pl.ds(0, width)] = (values * gain).astype(BF16)
    lanes = lane_ids(values.shape[0])
    g[at.h, :, pl.ds(width, 128)] = split_sum(part, lanes, jnp.zeros(lanes.shape, F32)).astype(BF16)


def exchange(at, link, src, dst):
    for i in range(1, 32):
        peer = at.along(i)
        link.send(i, src(peer[1]), dst(at.h), peer)


def exchanged(at, link, dst):
    for i in range(1, 32):
        peer = at.along(32 - i)
        link.wait(i, dst(peer[1]), peer)


def turn(values, cosine, sine):
    return values * cosine + pltpu.roll(values, HD // 2, 1) * sine


def attend(lengths, rqf, kc, vc, out):
    pairs = HEADS // 2
    lane = lax.broadcasted_iota(jnp.int32, (1, HD), 1)
    entry = lax.rem(lane, HD // 2).astype(F32)
    frequency = jnp.exp(entry * (-2.0 * math.log(rope_base) / HD))
    count = kc.shape[1]
    place = lax.broadcasted_iota(jnp.int32, (HEADS, count), 1)
    head_group = lax.rem(lax.broadcasted_iota(jnp.int32, (HEADS, count), 0), pairs) // (pairs // KV)
    same_group = lax.rem(place, KV) == head_group
    slot = place // KV
    factor = HD ** (-0.5)

    def widen(fresh):
        each = jnp.broadcast_to(fresh[:, None, :], (KV, pairs // KV, HD)).reshape(pairs, HD)
        return jnp.concatenate([each, each], axis=0)

    for r in range(4):
        def piece(t):
            return rqf[pl.ds(4 * t + r, pairs, stride=16), :]

        position = lengths[r]
        angle = frequency * position.astype(F32)
        cosine = jnp.cos(angle)
        sine = jnp.where(lane < HD // 2, -1.0, 1.0) * jnp.sin(angle)
        q = turn(jnp.concatenate([piece(0), piece(1)], axis=0), cosine, sine).astype(BF16)
        k_fresh = jnp.sum(piece(2).reshape(KV, pairs // KV, HD), axis=1)
        v_fresh = jnp.sum(piece(3).reshape(KV, pairs // KV, HD), axis=1)
        k_turned = turn(k_fresh, cosine, sine).astype(BF16).astype(F32)
        own = jnp.sum(q.astype(F32) * widen(k_turned), axis=1, keepdims=True) * factor
        visible = same_group & (slot < position)
        scores = jnp.where(visible, dot_nt(q, kc[r]) * factor, -jnp.inf)
        highest = jnp.maximum(jnp.max(scores, axis=1, keepdims=True), own)
        raised = jnp.exp(scores - highest)
        own_raised = jnp.exp(own - highest)
        total = jnp.sum(raised, axis=1, keepdims=True) + own_raised
        weights = (raised / total).astype(BF16)
        own_weight = (own_raised / total).astype(BF16).astype(F32)
        mixed = dot_nn(weights, vc[r]) + own_weight * widen(v_fresh)
        mixed = mixed.astype(BF16).astype(F32)
        for t in (0, 1):
            out[pl.ds(4 * t + r, pairs, stride=8), :] = mixed[t * pairs : (t + 1) * pairs]


def layer_kernel(
    hidden_ref, gains_ref, lengths, wq_hbm, wk_hbm, wv_hbm, wo_hbm, wg_hbm, wu_hbm, wd_hbm, kc_hbm, vc_hbm,
    out_ref,
    g, wq, wkv, wo, wgu, wd, kc, vc, acc, sbuf, rbuf, ysend, yrecv, res,
    qkv, qkv_s, qkv_r, heads, msgf, msg, rq, rqf, msg2, rq2, attf, att,
    pg, s1, r1, s2, r2, act,
    lsem, gss, grs, ssem, rsem, yss, yrs, wss, wrs, ass, ars, bss, brs,
):
    at = Place()
    width = hidden_ref.shape[1]
    units = wd.shape[0]
    half = width // 2
    loads = [
        pltpu.make_async_copy(src, dst, lsem.at[i])
        for i, (src, dst) in enumerate(
            (
                (wq_hbm, wq),
                (wk_hbm, wkv.at[pl.ds(0, 16)]),
                (wv_hbm, wkv.at[pl.ds(16, 16)]),
                (kc_hbm, kc),
                (vc_hbm, vc),
                (wo_hbm, wo),
                (wg_hbm, wgu.at[0, pl.ds(0, units)]),
                (wu_hbm, wgu.at[1, pl.ds(0, units)]),
                (wd_hbm, wd),
            )
        )
    ]
    for load in loads:
        load.start()
    fill_own(at, g, hidden_ref[...].astype(F32), gains_ref[0:1, :].astype(F32))
    enter(at)
    glink, link, ylink = Link(gss, grs), Link(ssem, rsem), Link(yss, yrs)
    wlink, alink, blink = Link(wss, wrs), Link(ass, ars), Link(bss, brs)
    mates = (at.core_peer, at.y_peer, at.far_peer)

    first = gather(at, glink, ylink, 0, g)
    next(first)
    wkv[pl.ds(32, 96), :] = jnp.zeros((96, width), BF16)
    for k in (0, 1):
        wgu[k, pl.ds(units, 64), :] = jnp.zeros((64, width), BF16)
    for load in loads[:3]:
        load.wait()
    for _ in first:
        pass
    glink.finish()
    ylink.finish()
    for i in range(4):
        rows = g[pl.ds(i * 8, 8), :, pl.ds(0, width)].reshape(128, width)
        tail = g[pl.ds(i * 8, 8), :, pl.ds(width, 128)].reshape(128, 128).astype(F32)
        qkv[i, :, pl.ds(0, 256)] = dot_nn(rows, wq[...])
        qkv[i, :, pl.ds(256, 128)] = dot_nt(rows, wkv[...]) + tail
    qkv_s[...] = qkv[...].astype(BF16)
    for i, peer in enumerate(mates):
        wlink.send(i, qkv_s.at[peer[0]], qkv_r.at[i], peer)
    total = qkv[at.w]
    for i, peer in enumerate(mates):
        wlink.wait(i, qkv_r.at[i], peer)
        total = total + qkv_r[i].astype(F32)
    norm = lax.rsqrt(joined_sum(total[:, 256:], lane_ids(128)) / D + norm_eps)
    scaled = (total * norm).astype(BF16)
    row = lax.broadcasted_iota(jnp.int32, (128, 256), 0)
    col = lax.broadcasted_iota(jnp.int32, (128, 256), 1)
    wanted = 16 * (col // 128) + lax.rem(col, 16)
    placed = (row == wanted) & (lax.rem(col, 128) // 16 == lax.rem(at.h, 8))
    fresh = dot_nn(scaled[:, 256:], jnp.where(placed, 1.0, 0.0).astype(BF16))
    heads[0] = scaled[:, :128].astype(F32)
    heads[1] = scaled[:, 128:256].astype(F32)
    heads[2] = fresh[:, :128]
    heads[3] = fresh[:, 128:]
    for t in range(4):
        for r in range(4):
            msgf[pl.ds(4 * t + r, 32, stride=16), :] = heads[t, pl.ds(r, 32, stride=4), :]
    msg[...] = msgf[...].astype(BF16).reshape(32, 16, 128)
    exchange(at, alink, lambda d: msg.at[d], lambda d: rq.at[d])
    rq[at.h] = msg[at.h]
    loads[3].wait()
    loads[4].wait()
    exchanged(at, alink, lambda d: rq.at[d])
    rqf[...] = rq[...].astype(F32).reshape(512, 128)
    attend(lengths, rqf, kc, vc, msg2)

    def eight(ref):
        return lambda d: ref.at[pl.ds(pl.multiple_of(d * 8, 8), 8)]

    exchange(at, blink, eight(msg2), eight(rq2))
    own8 = pl.ds(pl.multiple_of(at.h * 8, 8), 8)
    rq2[own8, :] = msg2[own8, :]
    exchanged(at, blink, eight(rq2))
    for t in (0, 1):
        for r in range(4):
            attf[t, pl.ds(r, 32, stride=4), :] = rq2[pl.ds(4 * t + r, 32, stride=8), :]
        att[at.w, :, pl.ds(t * 128, 128)] = attf[t].astype(BF16)
    for i, peer in enumerate(mates):
        wlink.send(3 + i, att.at[at.w], att.at[at.w], peer)
    loads[5].wait()
    for i, peer in enumerate(mates):
        wlink.wait(3 + i, att.at[peer[0]], peer)
    wlink.finish()
    alink.finish()
    blink.finish()
    for i in range(4):
        cols = pl.ds(i * 1024, 1024)
        acc[:, :, cols] = dot_nn(att[...].reshape(512, 256), wo[:, cols]).reshape(32, 16, 1024)

    def emit_residual(f, value):
        cols = pl.ds(f * half, half)
        res[:, cols] = (hidden_ref[:, cols].astype(F32) + value).astype(BF16)

    scatter(at, link, ylink, 1, acc, sbuf, rbuf, ysend, yrecv, emit_residual)
    link.finish()
    ylink.finish()

    fill_own(at, g, res[...].astype(F32), gains_ref[1:2, :].astype(F32))
    for load in loads[6:]:
        load.wait()
    c, yl = at.core, at.yl
    planes = (at.yh, 1 - at.yh)

    def plane(kind):
        return pl.ds(pl.multiple_of(planes[kind] * 16, 16), 16)

    def gate_up(kind, k):
        rows = g[plane(kind), :, pl.ds(0, width)].reshape(256, width)
        for start, size in ((0, 256), (256, 256), (512, 384)):
            value = dot_nt(rows, wgu[k, pl.ds(start, size), :])
            pg[k, kind, :, :, pl.ds(start, size)] = value.reshape(4, 64, size)
        if k == 0:
            tail = g[plane(kind), :, pl.ds(width, 128)].reshape(4, 64, 128).astype(F32)
            last = pl.ds(768, 128)
            pg[0, kind, :, :, last] = pg[0, kind, :, :, last] + tail
        s1[kind, k] = pg[k, kind, pl.ds(2 * (1 - c), 2)].astype(BF16)
        wlink.send(6 + kind * 7 + k, s1.at[kind, k], r1.at[kind, k], at.core_peer)

    def over_y(kind):
        for k in (0, 1):
            slot = 6 + kind * 7 + k
            wlink.wait(slot, r1.at[kind, k], at.core_peer)
            value = pg[k, kind, 2 * c + 1 - yl] + r1[kind, k, 1 - yl].astype(F32)
            s2[kind, k] = value.astype(BF16)
            if k == 0:
                lanes = lane_ids(64)
                tile = value[:, 768:]
                s2[kind, k, :, pl.ds(768, 128)] = split_sum(joined_sum(tile, lanes), lanes, tile).astype(BF16)
            wlink.send(slot + 2, s2.at[kind, k], r2.at[kind, k], at.y_peer)

    def activate(kind):
        base = 6 + kind * 7
        sums = []
        for k in (0, 1):
            wlink.wait(base + 2 + k, r2.at[kind, k], at.y_peer)
            sums.append(
                pg[k, kind, 2 * c + yl] + r1[kind, k, yl].astype(F32) + r2[kind, k].astype(F32)
            )
        scale = lax.rsqrt(joined_sum(sums[0][:, 768:], lane_ids(64)) / D + norm_eps)
        gate, up = sums[0][:, :units] * scale, sums[1][:, :units] * scale
        mine = act.at[kind, 2 * c + yl]
        act[kind, 2 * c + yl] = (gate / (1.0 + jnp.exp(-gate)) * up).astype(BF16)
        wlink.send(base + 4, mine, mine, at.y_peer)
        wlink.send(base + 5, mine, mine, at.core_peer)

    def pass_on(kind):
        base = 6 + kind * 7
        other = act.at[kind, 2 * c + 1 - yl]
        wlink.wait(base + 4, other, at.y_peer)
        wlink.send(base + 6, other, other, at.core_peer)

    def complete(kind):
        base = 6 + kind * 7
        wlink.wait(base + 5, act.at[kind, 2 * (1 - c) + yl], at.core_peer)
        wlink.wait(base + 6, act.at[kind, 2 * (1 - c) + 1 - yl], at.core_peer)

    def down(kind):
        rows = act[kind].reshape(256, units)
        for i in range(4):
            cols = pl.ds(i * 1024, 1024)
            acc[plane(kind), :, cols] = dot_nn(rows, wd[:, cols]).reshape(16, 16, 1024)

    near, far = {}, {}
    o0, o1 = (scatter_stages(at, link, acc, sbuf, rbuf, 0, f, near) for f in (0, 1))
    p0, p1 = (scatter_stages(at, link, acc, sbuf, rbuf, 1, f, far) for f in (0, 1))

    second = gather(at, glink, ylink, 3, g)
    next(second)
    next(second)
    gate_up(0, 0)
    next(second)
    gate_up(0, 1)
    over_y(0)
    next(second)
    gate_up(1, 0)
    activate(0)
    gate_up(1, 1)
    pass_on(0)
    over_y(1)
    complete(0)
    down(0)
    run(o0, o1)
    activate(1)
    run(o0, o1)
    pass_on(1)
    complete(1)
    down(1)
    run(p0, p1)
    run(o0, o1)
    run(p0, p1)
    run(o0, o1)
    run(p0, p1)
    run(o0, o1)
    run(p0, p1)
    run(p0, p1)
    for f in (0, 1):
        ysend[f] = far[f].astype(BF16)
        ylink.send(4 + f, ysend.at[f], yrecv.at[f], at.partner)
    for f in (0, 1):
        cols = pl.ds(f * half, half)
        ylink.wait(4 + f, yrecv.at[f], at.partner)
        value = res[:, cols].astype(F32) + near[f] + yrecv[f].astype(F32)
        out_ref[:, cols] = value.astype(BF16)
    for each in (glink, link, ylink, wlink):
        each.finish()


VM = pl.BlockSpec(memory_space=pltpu.VMEM)
ANY = pl.BlockSpec(memory_space=pl.ANY)
DMA = pltpu.SemaphoreType.DMA


def on_device(
    hidden_in,
    attn_gain,
    mlp_gain,
    w_query,
    w_key,
    w_value,
    w_out,
    w_gate,
    w_up,
    w_down,
    key_cache,
    value_cache,
    lengths,
):
    width = hidden_in.shape[1]
    units = w_gate.shape[1]
    padded = units + 64
    slots = key_cache.shape[1] * KV
    return pl.pallas_call(
        layer_kernel,
        out_shape=jax.ShapeDtypeStruct(hidden_in.shape, BF16),
        in_specs=[VM, VM, pl.BlockSpec(memory_space=pltpu.SMEM)] + [ANY] * 9,
        out_specs=VM,
        scratch_shapes=[
            pltpu.VMEM((32, 16, width + 128), BF16),
            pltpu.VMEM((width, 256), BF16),
            pltpu.VMEM((128, width), BF16),
            pltpu.VMEM((256, width), BF16),
            pltpu.VMEM((2, padded, width), BF16),
            pltpu.VMEM((units, width), BF16),
            pltpu.VMEM((4, slots, HD), BF16),
            pltpu.VMEM((4, slots, HD), BF16),
            pltpu.VMEM((32, 16, width), F32),
            pltpu.VMEM((TREE, 16, width // 2), BF16),
            pltpu.VMEM((TREE, 16, width // 2), BF16),
            pltpu.VMEM((2, 16, width // 2), BF16),
            pltpu.VMEM((2, 16, width // 2), BF16),
            pltpu.VMEM((16, width), BF16),
            pltpu.VMEM((4, 128, 384), F32),
            pltpu.VMEM((4, 128, 384), BF16),
            pltpu.VMEM((3, 128, 384), BF16),
            pltpu.VMEM((4, 128, 128), F32),
            pltpu.VMEM((512, 128), F32),
            pltpu.VMEM((32, 16, 128), BF16),
            pltpu.VMEM((32, 16, 128), BF16),
            pltpu.VMEM((512, 128), F32),
            pltpu.VMEM((256, 128), F32),
            pltpu.VMEM((256, 128), F32),
            pltpu.VMEM((2, 128, 128), F32),
            pltpu.VMEM((4, 128, 256), BF16),
            pltpu.VMEM((2, 2, 4, 64, padded), F32),
            pltpu.VMEM((2, 2, 2, 64, padded), BF16),
            pltpu.VMEM((2, 2, 2, 64, padded), BF16),
            pltpu.VMEM((2, 2, 64, padded), BF16),
            pltpu.VMEM((2, 2, 64, padded), BF16),
            pltpu.VMEM((2, 4, 64, units), BF16),
            DMA((9,)),
            DMA((TREE,)), DMA((TREE,)),
            DMA((TREE,)), DMA((TREE,)),
            DMA((6,)), DMA((6,)),
            DMA((20,)), DMA((20,)),
            DMA((32,)), DMA((32,)),
            DMA((32,)), DMA((32,)),
        ],
        compiler_params=pltpu.CompilerParams(
            collective_id=0, has_side_effects=True, vmem_limit_bytes=63 * 2**20
        ),
    )(
        hidden_in,
        jnp.stack([attn_gain, mlp_gain]),
        lengths,
        w_query,
        w_key.T,
        w_value.T,
        w_out,
        w_gate.T,
        w_up.T,
        w_down,
        key_cache.reshape(4, slots, HD),
        value_cache.reshape(4, slots, HD),
    )


def solution(mesh):
    return jax.shard_map(
        on_device,
        mesh=mesh,
        in_specs=(
            P("hidden", "width"),
            P("width"),
            P("width"),
            P("width", "hidden"),
            P("width", "hidden"),
            P("width", "hidden"),
            P("hidden", "width"),
            P("width", "hidden"),
            P("width", "hidden"),
            P("hidden", "width"),
            P(("width", "hidden"), None, None, None),
            P(("width", "hidden"), None, None, None),
            P(("width", "hidden")),
        ),
        out_specs=P("hidden", "width"),
        check_vma=False,
    )
```

```python
import functools
import math

import jax
import jax.numpy as jnp
from jax import lax
from jax.experimental import pallas as pl
from jax.experimental.pallas import tpu as pltpu
from jax.sharding import PartitionSpec as P

D = 16384
HEADS = 64
KV = 4
HD = 128
MESH = pl.DeviceIdType.MESH
F32 = jnp.float32
BF16 = jnp.bfloat16

rope_base = 500000.0
norm_eps = 1e-05

OFFS = (0, -1, 1, 2)


class Place:
    def __init__(self):
        self.w = lax.axis_index("width")
        self.h = lax.axis_index("hidden")
        self.x = lax.rem(self.h, 4)
        self.z = lax.rem(self.h // 4, 4)
        self.yh = self.h // 16
        self.core = lax.rem(self.w, 2)
        self.yl = self.w // 2
        self.partner = (self.w, lax.rem(self.h + 16, 32))
        self.core_peer = (self.w + 1 - 2 * self.core, self.h)
        self.y_peer = (lax.rem(self.w + 2, 4), self.h)
        self.far_peer = (lax.rem(self.w + 2, 4) + 1 - 2 * self.core, self.h)

    def block(self, c, f, p, q):
        dx, dz = (p, q) if f == 0 else (q, p)
        return c * 16 + lax.rem(self.z + (dz + 4), 4) * 4 + lax.rem(self.x + (dx + 4), 4)

    def neighbour(self, f, phase, sgn):
        p, q = (sgn, 0) if phase == 0 else (0, sgn)
        return (self.w, self.yh * 16 + self.block(0, f, p, q))

    def along(self, i):
        return (self.w, lax.rem(self.h + i, 32))


def enter(at):
    barrier = pltpu.get_barrier_semaphore()
    peers = [at.core_peer, at.y_peer, at.far_peer] + [at.along(i) for i in range(1, 32)]
    for peer in peers:
        pl.semaphore_signal(barrier, inc=1, device_id=peer, device_id_type=MESH)
    pl.semaphore_wait(barrier, len(peers))


class Link:
    def __init__(self, ssem, rsem, peer):
        self.ssem, self.rsem, self.peer, self.sent = ssem, rsem, peer, {}

    def copy(self, slot, src, dst, peer):
        return pltpu.make_async_remote_copy(
            src_ref=src,
            dst_ref=dst,
            send_sem=self.ssem.at[slot],
            recv_sem=self.rsem.at[slot],
            device_id=peer,
            device_id_type=MESH,
        )

    def send(self, slot, src, dst, peer, key=None, like=None):
        self.copy(slot, src, dst, peer).start()
        self.sent[(slot, key)] = like or (lambda: src)

    def wait(self, slot, dst, peer):
        self.copy(slot, dst, dst, peer).wait_recv()

    def finish(self, slots=None, key=None):
        for which in [w for w in self.sent if w[1] == key and (slots is None or w[0] in slots)]:
            like = self.sent.pop(which)()
            self.copy(which[0], like, like, self.peer).wait_send()


def only(flag, body):
    pl.when(flag[0] == flag[1])(body)


TREE = 60


def slots_of(c, f):
    return range((c * 2 + f) * 15, (c * 2 + f) * 15 + 15)


def slot_of(c, f, phase, j, d):
    base = (c * 2 + f) * 15
    if phase == 0:
        return base + {1: 0, -1: 1, 0: 2}[d]
    return base + 3 + OFFS.index(j) * 3 + {1: 0, -1: 1, 0: 2}[d]


class Gather:
    def __init__(self, at, link, g, c, f):
        half = g.shape[2] // 2 // 128 * 128
        self.cols = pl.ds(0, half) if f == 0 else pl.ds(half, g.shape[2] - half)
        self.at, self.link, self.g, self.c, self.f = at, link, g, c, f
        self.s = 1 if (c ^ f) == 0 else -1

    def ref(self, p, q):
        return self.g.at[self.at.block(self.c, self.f, p, q), :, self.cols]

    def send(self, phase, j, d, p, q, sgn):
        r = self.ref(p, q)
        slot = slot_of(self.c, self.f, phase, j, d)
        self.link.send(slot, r, r, self.at.neighbour(self.f, phase, sgn))

    def wait(self, phase, j, d, p, q, sgn):
        slot = slot_of(self.c, self.f, phase, j, d)
        self.link.wait(slot, self.ref(p, q), self.at.neighbour(self.f, phase, sgn))

    def spread(self, j):
        self.send(1, j, self.s, j, 0, self.s)
        self.send(1, j, -self.s, j, 0, -self.s)

    def start(self):
        self.send(0, 0, self.s, 0, 0, self.s)
        self.send(0, 0, -self.s, 0, 0, -self.s)
        self.spread(0)

    def first(self):
        s = self.s
        self.wait(0, 0, s, -s, 0, s)
        self.send(0, 0, 0, -s, 0, s)
        self.spread(-s)

    def second(self):
        s = self.s
        self.wait(0, 0, -s, s, 0, -s)
        self.spread(s)

    def third(self):
        self.wait(0, 0, 0, 2, 0, self.s)
        self.spread(2)

    def relay(self, j):
        s = self.s
        self.wait(1, j, s, j, -s, s)
        self.send(1, j, 0, j, -s, s)

    def end(self):
        for j in OFFS:
            self.wait(1, j, -self.s, j, self.s, -self.s)
        for j in OFFS:
            self.wait(1, j, 0, j, 2, self.s)

    def tasks(self, add, name):
        add(f"{name}.start", self.start)
        add(f"{name}.first", self.first)
        add(f"{name}.second", self.second)
        add(f"{name}.third", self.third)
        for j in (0, -self.s, self.s, 2):
            add(f"{name}.relay{j}", functools.partial(self.relay, j))


class Scatter:
    def __init__(self, at, link, acc, sbuf, rbuf, c, f):
        half = acc.shape[2] // 2
        self.cols = pl.ds(f * half, half)
        self.at, self.link, self.acc, self.sbuf, self.rbuf, self.c, self.f = at, link, acc, sbuf, rbuf, c, f
        self.s = 1 if (c ^ f) == 0 else -1

    def own(self, p, q):
        return self.acc[self.at.block(self.c, self.f, p, q), :, self.cols]

    def send(self, phase, j, d, sgn, value):
        slot = slot_of(self.c, self.f, phase, j, d)
        self.sbuf[slot] = value.astype(BF16)
        self.link.send(slot, self.sbuf.at[slot], self.rbuf.at[slot], self.at.neighbour(self.f, phase, sgn))

    def take(self, phase, j, d, sgn):
        slot = slot_of(self.c, self.f, phase, j, d)
        self.link.wait(slot, self.rbuf.at[slot], self.at.neighbour(self.f, phase, sgn))
        return self.rbuf[slot].astype(F32)

    def column(self, j):
        s = self.s
        return self.own(j, 0) + self.take(1, j, s, s) + self.take(1, j, -s, -s)

    def far(self, j):
        self.send(1, j, 0, self.s, self.own(j, 2))

    def back(self, j):
        self.send(1, j, -self.s, -self.s, self.own(j, -self.s))

    def on(self, j):
        self.send(1, j, self.s, self.s, self.own(j, self.s) + self.take(1, j, 0, self.s))

    def line_far(self):
        self.send(0, 0, 0, self.s, self.column(2))

    def line_back(self):
        self.send(0, 0, -self.s, -self.s, self.column(-self.s))

    def line_on(self):
        self.send(0, 0, self.s, self.s, self.column(self.s) + self.take(0, 0, 0, self.s))

    def total(self):
        return self.column(0) + self.take(0, 0, self.s, self.s) + self.take(0, 0, -self.s, -self.s)

    def tasks(self, add, name):
        order = (2, -self.s, self.s, 0)
        for j in order:
            add(f"{name}.far{j}", functools.partial(self.far, j), 0.06)
        for j in order:
            add(f"{name}.back{j}", functools.partial(self.back, j), 0.06)
        for j in order:
            add(f"{name}.on{j}", functools.partial(self.on, j), 0.08)
        add(f"{name}.line_far", self.line_far, 0.1)
        add(f"{name}.line_back", self.line_back, 0.1)
        add(f"{name}.line_on", self.line_on, 0.1)


def dot_nn(a, b):
    return jnp.dot(a, b, preferred_element_type=F32)


def dot_nt(a, b):
    return lax.dot_general(a, b, (((1,), (1,)), ((), ())), preferred_element_type=F32)


SS = 96


def split_sum(total, lanes, rest):
    high = total.astype(BF16).astype(F32)
    return jnp.where(lanes == SS, high, jnp.where(lanes == SS + 1, total - high, rest))


def joined_sum(tile, lanes):
    return jnp.sum(jnp.where((lanes == SS) | (lanes == SS + 1), tile, 0.0), axis=1, keepdims=True)


def lane_ids(rows):
    return lax.broadcasted_iota(jnp.int32, (rows, 128), 1)


def fill_own(at, g, values, gain):
    width = values.shape[1]
    part = jnp.sum(values * values, axis=1, keepdims=True)
    g[at.h, :, pl.ds(0, width)] = (values * gain).astype(BF16)
    lanes = lane_ids(values.shape[0])
    g[at.h, :, pl.ds(width, 128)] = split_sum(part, lanes, jnp.zeros(lanes.shape, F32)).astype(BF16)


def exchange(at, link, src, dst, key, like):
    for i in range(1, 32):
        peer = at.along(i)
        link.send(i, src(peer[1]), dst(at.h), peer, key, like)


def exchanged(at, link, dst):
    for i in range(1, 32):
        peer = at.along(32 - i)
        link.wait(i, dst(peer[1]), peer)


def turn(values, cosine, sine):
    return values * cosine + pltpu.roll(values, HD // 2, 1) * sine


def attend(lengths, rqf, kc, vc, out):
    pairs = HEADS // 2
    lane = lax.broadcasted_iota(jnp.int32, (1, HD), 1)
    entry = lax.rem(lane, HD // 2).astype(F32)
    frequency = jnp.exp(entry * (-2.0 * math.log(rope_base) / HD))
    count = kc.shape[1]
    place = lax.broadcasted_iota(jnp.int32, (HEADS, count), 1)
    head_group = lax.rem(lax.broadcasted_iota(jnp.int32, (HEADS, count), 0), pairs) // (pairs // KV)
    same_group = lax.rem(place, KV) == head_group
    slot = place // KV
    factor = HD ** (-0.5)

    def widen(fresh):
        each = jnp.broadcast_to(fresh[:, None, :], (KV, pairs // KV, HD)).reshape(pairs, HD)
        return jnp.concatenate([each, each], axis=0)

    for r in range(4):
        def piece(t):
            return rqf[pl.ds(4 * t + r, pairs, stride=16), :]

        position = lengths[r]
        angle = frequency * position.astype(F32)
        cosine = jnp.cos(angle)
        sine = jnp.where(lane < HD // 2, -1.0, 1.0) * jnp.sin(angle)
        q = turn(jnp.concatenate([piece(0), piece(1)], axis=0), cosine, sine).astype(BF16)
        k_fresh = jnp.sum(piece(2).reshape(KV, pairs // KV, HD), axis=1)
        v_fresh = jnp.sum(piece(3).reshape(KV, pairs // KV, HD), axis=1)
        k_turned = turn(k_fresh, cosine, sine).astype(BF16).astype(F32)
        own = jnp.sum(q.astype(F32) * widen(k_turned), axis=1, keepdims=True) * factor
        visible = same_group & (slot < position)
        scores = jnp.where(visible, dot_nt(q, kc[r]) * factor, -jnp.inf)
        highest = jnp.maximum(jnp.max(scores, axis=1, keepdims=True), own)
        raised = jnp.exp(scores - highest)
        own_raised = jnp.exp(own - highest)
        total = jnp.sum(raised, axis=1, keepdims=True) + own_raised
        weights = (raised / total).astype(BF16)
        own_weight = (own_raised / total).astype(BF16).astype(F32)
        mixed = dot_nn(weights, vc[r]) + own_weight * widen(v_fresh)
        mixed = mixed.astype(BF16).astype(F32)
        for t in (0, 1):
            out[pl.ds(4 * t + r, pairs, stride=8), :] = mixed[t * pairs : (t + 1) * pairs]


def layer_kernel(
    hidden_ref, gains_ref, lengths, wq_hbm, wk_hbm, wv_hbm, wo_hbm, wg_hbm, wu_hbm, wd_hbm, kc_hbm, vc_hbm,
    out_ref,
    g, wq, wkv, wo, wgu, wd, kc, vc, acc, sbuf, rbuf, near, ysend, yrecv, res,
    qkv, own_part, qkv_s, qkv_r, heads, msgf, msg, rq, rqf, msg2, rq2, attf, att,
    pg, s1, r1, s2, r2, act,
    lsem, gss, grs, ssem, rsem, yss, yrs, wss, wrs, ass, ars, bss, brs,
):
    at = Place()
    width = hidden_ref.shape[1]
    units = wd.shape[0]
    half = width // 2
    loads = [
        pltpu.make_async_copy(src, dst, lsem.at[i])
        for i, (src, dst) in enumerate(
            (
                (wq_hbm, wq),
                (wk_hbm, wkv.at[pl.ds(0, 16)]),
                (wv_hbm, wkv.at[pl.ds(16, 16)]),
                (kc_hbm, kc),
                (vc_hbm, vc),
                (wo_hbm, wo),
                (wg_hbm, wgu.at[0, pl.ds(0, units)]),
                (wu_hbm, wgu.at[1, pl.ds(0, units)]),
                (wd_hbm, wd),
            )
        )
    ]
    for load in loads:
        load.start()
    fill_own(at, g, hidden_ref[...].astype(F32), gains_ref[0:1, :].astype(F32))
    enter(at)
    pairs = ((gss, grs), (ssem, rsem), (yss, yrs), (wss, wrs), (ass, ars), (bss, brs))
    glink, link, ylink, wlink, alink, blink = (Link(a, b, at.partner) for a, b in pairs)
    mates = (at.core_peer, at.y_peer, at.far_peer)
    c_, yl = at.core, at.yl
    tasks = {}

    def add(name, body, cost=0.0):
        tasks[name] = (body, cost)

    def here(c):
        return (at.yh, c)

    def there(c):
        return (at.yh, 1 - c)

    def fresh_zeros():
        wkv[pl.ds(32, 96), :] = jnp.zeros((96, width), BF16)
        for k in (0, 1):
            wgu[k, pl.ds(units, 64), :] = jnp.zeros((64, width), BF16)

    add("zeros", fresh_zeros, 0.6)

    def add_loaded(name, which):
        def body():
            for load in which:
                load.wait()

        add(name, body)

    add_loaded("load_qkv", loads[:3])
    add_loaded("load_cache", loads[3:5])
    add_loaded("load_out", loads[5:6])
    add_loaded("load_mlp", loads[6:])

    def add_gather(turn, c):
        name = f"g{turn}{c}"
        halves = [Gather(at, glink, g, c, f) for f in (0, 1)]

        def slot(f):
            return turn * 4 + c * 2 + f

        def own_rows():
            if turn == 1:
                fill_own(at, g, res[...].astype(F32), gains_ref[1:2, :].astype(F32))
            for f in (0, 1):
                mine = g.at[at.h, :, halves[f].cols]
                like = lambda f=f: g.at[0, :, halves[f].cols]
                ylink.send(slot(f), mine, mine, at.partner, c, like)

        add(f"{name}.own", lambda: only(here(c), own_rows), 0.4 * turn)
        for f in (0, 1):
            def arrive(f=f):
                theirs = g.at[at.partner[1], :, halves[f].cols]
                only(there(c), lambda: ylink.wait(slot(f), theirs, at.partner))

            add(f"{name}.{f}.arrive", arrive)
            halves[f].tasks(add, f"{name}.{f}")

        def end():
            for each in halves:
                each.end()

        def finish():
            for f in (0, 1):
                glink.finish(slots_of(c, f))
            only(here(c), lambda: ylink.finish([slot(0), slot(1)], c))

        add(f"{name}.end", end)
        if turn == 0:
            add(f"{name}.finish", finish)

    def add_scatter(turn, c):
        name = f"s{turn}{c}"
        for f in (0, 1):
            one = Scatter(at, link, acc, sbuf, rbuf, c, f)
            one.tasks(add, f"{name}.{f}")
            slot = 8 + turn * 4 + c * 2 + f
            buf = turn * 2 + f

            def total(one=one, f=f, slot=slot, buf=buf):
                near[c, f] = one.total()

                def pass_over():
                    ysend[buf] = near[c, f].astype(BF16)
                    ylink.send(slot, ysend.at[buf], yrecv.at[buf], at.partner, 1 - c, lambda: ysend.at[buf])

                only(there(c), pass_over)

            def last(f=f, slot=slot, buf=buf):
                def body():
                    cols = pl.ds(f * half, half)
                    ylink.wait(slot, yrecv.at[buf], at.partner)
                    value = near[c, f] + yrecv[buf].astype(F32)
                    if turn == 0:
                        res[:, cols] = (hidden_ref[:, cols].astype(F32) + value).astype(BF16)
                    else:
                        out_ref[:, cols] = (res[:, cols].astype(F32) + value).astype(BF16)

                only(here(c), body)

            add(f"{name}.{f}.total", total, 0.15)
            add(f"{name}.{f}.last", last, 0.1)
            if turn == 0:
                add(f"{name}.{f}.finish", functools.partial(link.finish, slots_of(c, f)))

    def add_attention(c):
        active, passive = (at.yl, c), (at.yl, 1 - c)

        def project():
            rows = g[pl.ds(c * 16, 16), :, pl.ds(0, width)].reshape(256, width)
            extra = g[pl.ds(c * 16, 16), :, pl.ds(width, 128)].reshape(256, 128).astype(F32)
            qkv[:, :, pl.ds(0, 256)] = dot_nn(rows, wq[...]).reshape(2, 128, 256)
            qkv[:, :, pl.ds(256, 128)] = (dot_nt(rows, wkv[...]) + extra).reshape(2, 128, 128)
            buf, like = qkv_s.at[c], lambda: qkv_s.at[c, 0]
            qkv_s[c] = qkv[...].astype(BF16)

            def inside():
                wlink.send(0, buf.at[1 - c_], qkv_r.at[0], at.core_peer, c, like)

            def across():
                wlink.send(1, buf.at[c_], qkv_r.at[1], at.y_peer, 1 - c, like)
                wlink.send(2, buf.at[1 - c_], qkv_r.at[2], at.far_peer, 1 - c, like)

            only(active, inside)
            only(passive, across)
            only(active, lambda: own_part.__setitem__(Ellipsis, qkv[c_]))

        def sum_up():
            total = own_part[...]
            for i, peer in enumerate(mates):
                wlink.wait(i, qkv_r.at[i], peer)
                total = total + qkv_r[i].astype(F32)
            norm = lax.rsqrt(joined_sum(total[:, 256:], lane_ids(128)) / D + norm_eps)
            scaled = (total * norm).astype(BF16)
            row = lax.broadcasted_iota(jnp.int32, (128, 256), 0)
            col = lax.broadcasted_iota(jnp.int32, (128, 256), 1)
            wanted = 16 * (col // 128) + lax.rem(col, 16)
            placed = (row == wanted) & (lax.rem(col, 128) // 16 == lax.rem(at.h, 8))
            fresh = dot_nn(scaled[:, 256:], jnp.where(placed, 1.0, 0.0).astype(BF16))
            heads[0] = scaled[:, :128].astype(F32)
            heads[1] = scaled[:, 128:256].astype(F32)
            heads[2] = fresh[:, :128]
            heads[3] = fresh[:, 128:]
            for t in range(4):
                for r in range(4):
                    msgf[pl.ds(4 * t + r, 32, stride=16), :] = heads[t, pl.ds(r, 32, stride=4), :]
            msg[...] = msgf[...].astype(BF16).reshape(32, 16, 128)
            exchange(at, alink, lambda d: msg.at[d], lambda d: rq.at[d], c, lambda: msg.at[0])
            rq[at.h] = msg[at.h]

        def eight(ref):
            return lambda d: ref.at[pl.ds(pl.multiple_of(d * 8, 8), 8)]

        def attention():
            exchanged(at, alink, lambda d: rq.at[d])
            rqf[...] = rq[...].astype(F32).reshape(512, 128)
            attend(lengths, rqf, kc, vc, msg2)
            exchange(at, blink, eight(msg2), eight(rq2), c, lambda: msg2.at[pl.ds(0, 8)])
            own8 = pl.ds(pl.multiple_of(at.h * 8, 8), 8)
            rq2[own8, :] = msg2[own8, :]

        def hand_out():
            exchanged(at, blink, eight(rq2))
            for t in (0, 1):
                for r in range(4):
                    attf[t, pl.ds(r, 32, stride=4), :] = rq2[pl.ds(4 * t + r, 32, stride=8), :]
                att[at.w, :, pl.ds(t * 128, 128)] = attf[t].astype(BF16)
            for i, peer in enumerate(mates):
                wlink.send(3 + i, att.at[at.w], att.at[at.w], peer, c, lambda: att.at[0])
            alink.finish(None, c)
            blink.finish(None, c)

        def take_in():
            only(active, lambda: wlink.wait(3, att.at[at.core_peer[0]], at.core_peer))

            def across():
                wlink.wait(4, att.at[at.y_peer[0]], at.y_peer)
                wlink.wait(5, att.at[at.far_peer[0]], at.far_peer)

            only(passive, across)

        def out_product(f):
            rows = att[pl.ds(2 * c, 2)].reshape(256, 256)
            for i in (2 * f, 2 * f + 1):
                cols = pl.ds(i * 1024, 1024)
                acc[pl.ds(c * 16, 16), :, cols] = dot_nn(rows, wo[:, cols]).reshape(16, 16, 1024)

        add(f"a{c}.project", project, 0.2)
        add(f"a{c}.sum", lambda: only(active, sum_up), 1.0)
        add(f"a{c}.attend", lambda: only(active, attention), 1.2)
        add(f"a{c}.hand", lambda: only(active, hand_out), 0.3)
        add(f"a{c}.take", take_in)
        for f in (0, 1):
            add(f"a{c}.out{f}", functools.partial(out_product, f))

    def add_mlp(c):
        base = 6 + c * 7
        cuts = ((0, 256), (256, 256), (512, 384))

        def gate_up(k, i):
            start, size = cuts[i]
            rows = g[pl.ds(c * 16, 16), :, pl.ds(0, width)].reshape(256, width)
            value = dot_nt(rows, wgu[k, pl.ds(start, size), :])
            pg[k, c, :, :, pl.ds(start, size)] = value.reshape(4, 64, size)
            if i == 2:
                if k == 0:
                    extra = g[pl.ds(c * 16, 16), :, pl.ds(width, 128)].reshape(4, 64, 128).astype(F32)
                    end = pl.ds(768, 128)
                    pg[0, c, :, :, end] = pg[0, c, :, :, end] + extra
                s1[c, k] = pg[k, c, pl.ds(2 * (1 - c_), 2)].astype(BF16)
                wlink.send(base + k, s1.at[c, k], r1.at[c, k], at.core_peer)

        def over_y(k):
            wlink.wait(base + k, r1.at[c, k], at.core_peer)
            value = pg[k, c, 2 * c_ + 1 - yl] + r1[c, k, 1 - yl].astype(F32)
            s2[c, k] = value.astype(BF16)
            if k == 0:
                lanes = lane_ids(64)
                tile = value[:, 768:]
                s2[c, k, :, pl.ds(768, 128)] = split_sum(joined_sum(tile, lanes), lanes, tile).astype(BF16)
            wlink.send(base + 2 + k, s2.at[c, k], r2.at[c, k], at.y_peer)

        def activate():
            sums = []
            for k in (0, 1):
                wlink.wait(base + 2 + k, r2.at[c, k], at.y_peer)
                sums.append(pg[k, c, 2 * c_ + yl] + r1[c, k, yl].astype(F32) + r2[c, k].astype(F32))
            scale = lax.rsqrt(joined_sum(sums[0][:, 768:], lane_ids(64)) / D + norm_eps)
            gate, up = sums[0][:, :units] * scale, sums[1][:, :units] * scale
            mine = act.at[c, 2 * c_ + yl]
            act[c, 2 * c_ + yl] = (gate / (1.0 + jnp.exp(-gate)) * up).astype(BF16)
            wlink.send(base + 4, mine, mine, at.y_peer)
            wlink.send(base + 5, mine, mine, at.core_peer)

        def pass_on():
            other = act.at[c, 2 * c_ + 1 - yl]
            wlink.wait(base + 4, other, at.y_peer)
            wlink.send(base + 6, other, other, at.core_peer)

        def complete():
            wlink.wait(base + 5, act.at[c, 2 * (1 - c_) + yl], at.core_peer)
            wlink.wait(base + 6, act.at[c, 2 * (1 - c_) + 1 - yl], at.core_peer)

        def down(i):
            rows = act[c].reshape(256, units)
            cols = pl.ds(i * 1024, 1024)
            acc[pl.ds(c * 16, 16), :, cols] = dot_nn(rows, wd[:, cols]).reshape(16, 16, 1024)

        for k in (0, 1):
            for i in range(3):
                add(f"m{c}.gu{k}{i}", functools.partial(gate_up, k, i), 0.25 * (i == 2))
            add(f"m{c}.y{k}", functools.partial(over_y, k), 0.2)
        add(f"m{c}.act", activate, 0.5)
        add(f"m{c}.pass", pass_on)
        add(f"m{c}.complete", complete)
        for i in range(4):
            add(f"m{c}.down{i}", functools.partial(down, i))

    for c in (0, 1):
        add_gather(0, c)
        add_attention(c)
        add_scatter(0, c)
        add_gather(1, c)
        add_mlp(c)
        add_scatter(1, c)

    for name in order_of(tasks):
        enter_task(name, tasks[name][1])
        tasks[name][0]()
    for each in (glink, link, wlink):
        each.finish()
    for c in (0, 1):
        only(here(c), lambda c=c: ylink.finish(None, c))
        only((at.yl, c), lambda c=c: wlink.finish(None, c))


def enter_task(name, cost):
    pass


ORDER = [
    "g00.own", "g01.own", "g00.0.arrive", "g00.0.start", "g00.1.arrive", "g00.1.start", "g01.0.arrive",
    "g01.0.start", "g01.1.arrive", "g00.0.first", "g00.0.second", "g00.1.second", "g00.1.relay0", "zeros",
    "g00.1.first", "g01.1.start", "load_qkv", "g00.0.third", "g00.0.relay1", "g00.0.relay-1", "g00.1.third",
    "g00.0.relay2", "load_out", "g00.1.relay-1", "g00.1.relay1", "g00.0.relay0", "g00.1.relay2",
    "g01.0.first", "g01.1.second", "g01.1.first", "g01.1.relay0", "load_mlp", "g01.0.second", "load_cache",
    "g01.0.relay0", "g01.0.relay1", "g00.end", "g00.finish", "a0.project", "g01.1.third", "g01.1.relay1",
    "g01.0.third", "g01.1.relay-1", "g01.0.relay-1", "g01.1.relay2", "g01.0.relay2", "a0.sum", "g01.end",
    "a1.project", "a0.attend", "a1.sum", "g01.finish", "a0.hand", "a1.attend", "a0.take", "a0.out0",
    "s00.0.far2", "a0.out1", "s00.1.far1", "s00.1.back-1", "s00.0.back1", "s00.1.far2", "s00.0.back0",
    "s00.1.far0", "s00.1.back0", "s00.0.far-1", "s00.1.back2", "s00.1.far-1", "s00.0.back2", "s00.0.far0",
    "a1.hand", "s00.0.far1", "s00.1.back1", "s00.1.on2", "s00.0.back-1", "s00.0.on2", "s00.0.on-1",
    "s00.1.on1", "s00.1.on0", "s00.1.on-1", "s00.0.on1", "s00.0.on0", "s00.0.line_far", "a1.take",
    "s00.1.line_far", "a1.out0", "a1.out1", "s01.0.far2", "s00.0.line_back", "s01.1.far2", "s01.0.far1",
    "s00.0.line_on", "s01.1.back0", "s00.1.line_back", "s00.1.line_on", "s01.0.far-1", "s01.0.far0",
    "s01.1.back1", "s01.1.far1", "s01.0.back1", "s01.1.far-1", "s01.1.on2", "s01.0.back0", "s00.0.total",
    "s01.1.back2", "s01.0.on2", "s01.0.on1", "s01.0.back2", "s00.1.total", "s01.1.back-1", "s01.0.back-1",
    "s01.1.far0", "s01.0.on-1", "s01.1.on-1", "s01.0.on0", "s01.1.on1", "s01.0.line_far", "s01.1.on0",
    "s01.1.line_far", "s01.1.line_back", "s01.0.line_back", "s00.0.last", "s00.1.last", "g10.own",
    "s01.0.line_on", "g10.0.arrive", "g10.0.start", "s01.1.line_on", "g10.1.arrive", "g10.1.start",
    "s01.0.total", "g10.0.first", "s01.0.last", "s01.1.total", "g10.1.first", "s01.1.last", "g10.0.second",
    "g11.own", "g10.1.relay0", "g10.0.third", "s00.0.finish", "g10.1.second", "g10.0.relay-1", "g10.1.third",
    "g10.0.relay2", "g10.0.relay1", "g10.0.relay0", "g10.1.relay1", "g10.1.relay-1", "g10.1.relay2",
    "g11.0.arrive", "g11.1.arrive", "s00.1.finish", "g11.1.start", "g11.0.start", "g10.end", "m0.gu11",
    "m0.gu00", "g11.1.first", "m0.gu10", "g11.0.second", "g11.0.first", "g11.0.relay0", "g11.1.second",
    "m0.gu12", "g11.1.third", "m0.gu01", "m0.y1", "g11.1.relay0", "g11.0.third", "m0.gu02", "g11.0.relay1",
    "g11.1.relay1", "g11.1.relay-1", "m0.y0", "g11.0.relay-1", "g11.0.relay2", "g11.1.relay2", "m0.act",
    "g11.end", "m1.gu00", "m1.gu01", "m1.gu02", "m1.gu10", "m1.y0", "m0.pass", "m1.gu11", "m1.gu12",
    "m0.complete", "m0.down3", "m1.y1", "m0.down2", "s10.1.far2", "m0.down1", "s10.1.far-1", "m0.down0",
    "s10.0.back0", "s10.1.far0", "s10.0.far1", "s10.1.back2", "s10.0.far2", "s10.1.far1", "s10.0.back1",
    "s10.0.far-1", "m1.act", "s10.0.far0", "s10.0.back2", "s10.1.on2", "s10.1.on-1", "s10.1.back1",
    "s10.0.on2", "s10.0.back-1", "s10.1.back0", "s10.1.on1", "s01.0.finish", "s10.0.on1", "m1.pass",
    "s10.1.back-1", "s10.1.on0", "s10.0.on-1", "s10.1.line_far", "m1.complete", "s10.0.on0", "m1.down0",
    "m1.down1", "s11.0.far2", "s10.0.line_far", "s11.0.far-1", "m1.down3", "s01.1.finish", "m1.down2",
    "s11.1.back0", "s11.1.far2", "s10.0.line_back", "s11.1.far1", "s11.0.far1", "s11.0.on2", "s11.0.back0",
    "s11.0.back1", "s11.1.back-1", "s11.0.back2", "s11.1.far-1", "s11.0.far0", "s10.1.line_back",
    "s11.1.far0", "s11.1.on2", "s11.1.back2", "s11.0.on1", "s11.0.back-1", "s10.1.line_on", "s11.1.on-1",
    "s10.0.line_on", "s11.1.back1", "s11.1.on1", "s11.0.on-1", "s11.0.on0", "s11.0.line_far",
    "s11.0.line_back", "s11.1.on0", "s11.1.line_far", "s10.1.total", "s11.0.line_on", "s10.0.total",
    "s11.1.line_back", "s11.1.line_on", "s11.0.total", "s11.0.last", "s11.1.total", "s10.1.last",
    "s10.0.last", "s11.1.last",
]


def order_of(tasks):
    assert sorted(ORDER) == sorted(tasks)
    return ORDER


VM = pl.BlockSpec(memory_space=pltpu.VMEM)
ANY = pl.BlockSpec(memory_space=pl.ANY)
DMA = pltpu.SemaphoreType.DMA


def on_device(
    hidden_in,
    attn_gain,
    mlp_gain,
    w_query,
    w_key,
    w_value,
    w_out,
    w_gate,
    w_up,
    w_down,
    key_cache,
    value_cache,
    lengths,
):
    width = hidden_in.shape[1]
    units = w_gate.shape[1]
    padded = units + 64
    slots = key_cache.shape[1] * KV
    return pl.pallas_call(
        layer_kernel,
        out_shape=jax.ShapeDtypeStruct(hidden_in.shape, BF16),
        in_specs=[VM, VM, pl.BlockSpec(memory_space=pltpu.SMEM)] + [ANY] * 9,
        out_specs=VM,
        scratch_shapes=[
            pltpu.VMEM((32, 16, width + 128), BF16),
            pltpu.VMEM((width, 256), BF16),
            pltpu.VMEM((128, width), BF16),
            pltpu.VMEM((256, width), BF16),
            pltpu.VMEM((2, padded, width), BF16),
            pltpu.VMEM((units, width), BF16),
            pltpu.VMEM((4, slots, HD), BF16),
            pltpu.VMEM((4, slots, HD), BF16),
            pltpu.VMEM((32, 16, width), F32),
            pltpu.VMEM((TREE, 16, width // 2), BF16),
            pltpu.VMEM((TREE, 16, width // 2), BF16),
            pltpu.VMEM((2, 2, 16, width // 2), F32),
            pltpu.VMEM((4, 16, width // 2), BF16),
            pltpu.VMEM((4, 16, width // 2), BF16),
            pltpu.VMEM((16, width), BF16),
            pltpu.VMEM((2, 128, 384), F32),
            pltpu.VMEM((128, 384), F32),
            pltpu.VMEM((2, 2, 128, 384), BF16),
            pltpu.VMEM((3, 128, 384), BF16),
            pltpu.VMEM((4, 128, 128), F32),
            pltpu.VMEM((512, 128), F32),
            pltpu.VMEM((32, 16, 128), BF16),
            pltpu.VMEM((32, 16, 128), BF16),
            pltpu.VMEM((512, 128), F32),
            pltpu.VMEM((256, 128), F32),
            pltpu.VMEM((256, 128), F32),
            pltpu.VMEM((2, 128, 128), F32),
            pltpu.VMEM((4, 128, 256), BF16),
            pltpu.VMEM((2, 2, 4, 64, padded), F32),
            pltpu.VMEM((2, 2, 2, 64, padded), BF16),
            pltpu.VMEM((2, 2, 2, 64, padded), BF16),
            pltpu.VMEM((2, 2, 64, padded), BF16),
            pltpu.VMEM((2, 2, 64, padded), BF16),
            pltpu.VMEM((2, 4, 64, units), BF16),
            DMA((9,)),
            DMA((TREE,)), DMA((TREE,)),
            DMA((TREE,)), DMA((TREE,)),
            DMA((16,)), DMA((16,)),
            DMA((20,)), DMA((20,)),
            DMA((32,)), DMA((32,)),
            DMA((32,)), DMA((32,)),
        ],
        compiler_params=pltpu.CompilerParams(
            collective_id=0, has_side_effects=True, vmem_limit_bytes=63 * 2**20
        ),
    )(
        hidden_in,
        jnp.stack([attn_gain, mlp_gain]),
        lengths,
        w_query,
        w_key.T,
        w_value.T,
        w_out,
        w_gate.T,
        w_up.T,
        w_down,
        key_cache.reshape(4, slots, HD),
        value_cache.reshape(4, slots, HD),
    )


def solution(mesh):
    return jax.shard_map(
        on_device,
        mesh=mesh,
        in_specs=(
            P("hidden", "width"),
            P("width"),
            P("width"),
            P("width", "hidden"),
            P("width", "hidden"),
            P("width", "hidden"),
            P("hidden", "width"),
            P("width", "hidden"),
            P("width", "hidden"),
            P("hidden", "width"),
            P(("width", "hidden"), None, None, None),
            P(("width", "hidden"), None, None, None),
            P(("width", "hidden")),
        ),
        out_specs=P("hidden", "width"),
        check_vma=False,
    )
```

```python
import functools
import math

import jax
import jax.numpy as jnp
from jax import lax
from jax.experimental import pallas as pl
from jax.experimental.pallas import tpu as pltpu
from jax.sharding import PartitionSpec as P

D = 16384
HEADS = 64
KV = 4
HD = 128
MESH = pl.DeviceIdType.MESH
F32 = jnp.float32
BF16 = jnp.bfloat16

rope_base = 500000.0
norm_eps = 1e-05

OFFS = (0, -1, 1, 2)


class Place:
    def __init__(self):
        self.w = lax.axis_index("width")
        self.h = lax.axis_index("hidden")
        self.x = lax.rem(self.h, 4)
        self.z = lax.rem(self.h // 4, 4)
        self.yh = self.h // 16
        self.core = lax.rem(self.w, 2)
        self.yl = self.w // 2
        self.partner = (self.w, lax.rem(self.h + 16, 32))
        self.core_peer = (self.w + 1 - 2 * self.core, self.h)
        self.y_peer = (lax.rem(self.w + 2, 4), self.h)
        self.far_peer = (lax.rem(self.w + 2, 4) + 1 - 2 * self.core, self.h)

    def block(self, c, f, p, q):
        dx, dz = (p, q) if f == 0 else (q, p)
        return c * 16 + lax.rem(self.z + (dz + 4), 4) * 4 + lax.rem(self.x + (dx + 4), 4)

    def neighbour(self, f, phase, sgn):
        p, q = (sgn, 0) if phase == 0 else (0, sgn)
        return (self.w, self.yh * 16 + self.block(0, f, p, q))

    def along(self, i):
        return (self.w, lax.rem(self.h + i, 32))


def enter(at):
    barrier = pltpu.get_barrier_semaphore()
    peers = [at.core_peer, at.y_peer, at.far_peer] + [at.along(i) for i in range(1, 32)]
    for peer in peers:
        pl.semaphore_signal(barrier, inc=1, device_id=peer, device_id_type=MESH)
    pl.semaphore_wait(barrier, len(peers))


class Link:
    def __init__(self, ssem, rsem, peer):
        self.ssem, self.rsem, self.peer, self.sent = ssem, rsem, peer, {}

    def copy(self, slot, src, dst, peer):
        return pltpu.make_async_remote_copy(
            src_ref=src,
            dst_ref=dst,
            send_sem=self.ssem.at[slot],
            recv_sem=self.rsem.at[slot],
            device_id=peer,
            device_id_type=MESH,
        )

    def send(self, slot, src, dst, peer, key=None, like=None):
        self.copy(slot, src, dst, peer).start()
        self.sent[(slot, key)] = like or (lambda: src)

    def wait(self, slot, dst, peer):
        self.copy(slot, dst, dst, peer).wait_recv()

    def finish(self, slots=None, key=None):
        for which in [w for w in self.sent if w[1] == key and (slots is None or w[0] in slots)]:
            like = self.sent.pop(which)()
            self.copy(which[0], like, like, self.peer).wait_send()


def only(flag, body):
    pl.when(flag[0] == flag[1])(body)


TREE = 60


def slots_of(c, f):
    return range((c * 2 + f) * 15, (c * 2 + f) * 15 + 15)


def slot_of(c, f, phase, j, d):
    base = (c * 2 + f) * 15
    if phase == 0:
        return base + {1: 0, -1: 1, 0: 2}[d]
    return base + 3 + OFFS.index(j) * 3 + {1: 0, -1: 1, 0: 2}[d]


class Gather:
    def __init__(self, at, link, g, c, f):
        half = g.shape[2] // 2 // 128 * 128
        self.cols = pl.ds(0, half) if f == 0 else pl.ds(half, g.shape[2] - half)
        self.at, self.link, self.g, self.c, self.f = at, link, g, c, f
        self.s = 1 if (c ^ f) == 0 else -1

    def ref(self, p, q):
        return self.g.at[self.at.block(self.c, self.f, p, q), :, self.cols]

    def send(self, phase, j, d, p, q, sgn):
        r = self.ref(p, q)
        slot = slot_of(self.c, self.f, phase, j, d)
        self.link.send(slot, r, r, self.at.neighbour(self.f, phase, sgn))

    def wait(self, phase, j, d, p, q, sgn):
        slot = slot_of(self.c, self.f, phase, j, d)
        self.link.wait(slot, self.ref(p, q), self.at.neighbour(self.f, phase, sgn))

    def way(self, j):
        return self.s if j in (0, -self.s) else -self.s

    def spread(self, j):
        self.send(1, j, self.s, j, 0, self.s)
        self.send(1, j, -self.s, j, 0, -self.s)

    def start(self):
        self.send(0, 0, self.s, 0, 0, self.s)
        self.send(0, 0, -self.s, 0, 0, -self.s)
        self.send(0, 0, 0, 0, 0, 2)
        self.spread(0)

    def first(self):
        s = self.s
        self.wait(0, 0, s, -s, 0, s)
        self.spread(-s)

    def second(self):
        s = self.s
        self.wait(0, 0, -s, s, 0, -s)
        self.spread(s)

    def third(self):
        self.wait(0, 0, 0, 2, 0, 2)
        self.spread(2)

    def relay(self, j):
        s = self.way(j)
        self.wait(1, j, s, j, -s, s)
        self.send(1, j, 0, j, -s, s)

    def end(self):
        for j in OFFS:
            s = self.way(j)
            self.wait(1, j, -s, j, s, -s)
        for j in OFFS:
            self.wait(1, j, 0, j, 2, self.way(j))

    def tasks(self, add, name):
        add(f"{name}.start", self.start)
        add(f"{name}.first", self.first)
        add(f"{name}.second", self.second)
        add(f"{name}.third", self.third)
        for j in (0, -self.s, self.s, 2):
            add(f"{name}.relay{j}", functools.partial(self.relay, j))


class Scatter:
    def __init__(self, at, link, acc, sbuf, rbuf, c, f):
        half = acc.shape[2] // 2
        self.cols = pl.ds(f * half, half)
        self.at, self.link, self.acc, self.sbuf, self.rbuf, self.c, self.f = at, link, acc, sbuf, rbuf, c, f
        self.s = 1 if (c ^ f) == 0 else -1

    def own(self, p, q):
        return self.acc[self.at.block(self.c, self.f, p, q), :, self.cols]

    def send(self, phase, j, d, sgn, value):
        slot = slot_of(self.c, self.f, phase, j, d)
        self.sbuf[slot] = value.astype(BF16)
        self.link.send(slot, self.sbuf.at[slot], self.rbuf.at[slot], self.at.neighbour(self.f, phase, sgn))

    def take(self, phase, j, d, sgn):
        slot = slot_of(self.c, self.f, phase, j, d)
        self.link.wait(slot, self.rbuf.at[slot], self.at.neighbour(self.f, phase, sgn))
        return self.rbuf[slot].astype(F32)

    def way(self, j):
        return self.s if j in (0, -self.s) else -self.s

    def column(self, j):
        s = self.way(j)
        return self.own(j, 0) + self.take(1, j, s, s) + self.take(1, j, -s, -s)

    def far(self, j):
        self.send(1, j, 0, self.way(j), self.own(j, 2))

    def back(self, j):
        s = self.way(j)
        self.send(1, j, -s, -s, self.own(j, -s))

    def on(self, j):
        s = self.way(j)
        self.send(1, j, s, s, self.own(j, s) + self.take(1, j, 0, s))

    def line_far(self):
        self.send(0, 0, 0, 2, self.column(2))

    def line_back(self):
        self.send(0, 0, -self.s, -self.s, self.column(-self.s))

    def line_on(self):
        self.send(0, 0, self.s, self.s, self.column(self.s))

    def total(self):
        value = self.column(0)
        for d, sgn in ((self.s, self.s), (-self.s, -self.s), (0, 2)):
            value = value + self.take(0, 0, d, sgn)
        return value

    def tasks(self, add, name):
        order = (2, -self.s, self.s, 0)
        for j in order:
            add(f"{name}.far{j}", functools.partial(self.far, j), 0.06)
        for j in order:
            add(f"{name}.back{j}", functools.partial(self.back, j), 0.06)
        for j in order:
            add(f"{name}.on{j}", functools.partial(self.on, j), 0.08)
        add(f"{name}.line_far", self.line_far, 0.1)
        add(f"{name}.line_back", self.line_back, 0.1)
        add(f"{name}.line_on", self.line_on, 0.1)


def dot_nn(a, b):
    return jnp.dot(a, b, preferred_element_type=F32)


def dot_nt(a, b):
    return lax.dot_general(a, b, (((1,), (1,)), ((), ())), preferred_element_type=F32)


SS = 96


def split_sum(total, lanes, rest):
    high = total.astype(BF16).astype(F32)
    return jnp.where(lanes == SS, high, jnp.where(lanes == SS + 1, total - high, rest))


def joined_sum(tile, lanes):
    return jnp.sum(jnp.where((lanes == SS) | (lanes == SS + 1), tile, 0.0), axis=1, keepdims=True)


def lane_ids(rows):
    return lax.broadcasted_iota(jnp.int32, (rows, 128), 1)


def fill_own(g, block, values, gain, f):
    width = values.shape[1]
    tiles = width // 256
    for i in range(f * tiles, (f + 1) * tiles):
        cols = pl.ds(i * 128, 128)
        g[block, :, cols] = (values[:, i * 128 : (i + 1) * 128] * gain[i : i + 1]).astype(BF16)
    if f == 1:
        part = jnp.sum(values * values, axis=1, keepdims=True)
        lanes = lane_ids(values.shape[0])
        tail = split_sum(part, lanes, jnp.zeros(lanes.shape, F32))
        g[block, :, pl.ds(width, 128)] = tail.astype(BF16)


def exchange(at, link, src, dst, key, like):
    for i in range(1, 32):
        peer = at.along(i)
        link.send(0, src(peer[1]), dst(at.h), peer, key, like)


def exchanged(at, link, blocks):
    link.wait(0, blocks, at.partner)


def turn(values, cosine, sine):
    return values * cosine + pltpu.roll(values, HD // 2, 1) * sine


def attend(lengths, rqf, kc, vc, out):
    pairs = HEADS // 2
    lane = lax.broadcasted_iota(jnp.int32, (1, HD), 1)
    entry = lax.rem(lane, HD // 2).astype(F32)
    frequency = jnp.exp(entry * (-2.0 * math.log(rope_base) / HD))
    count = kc.shape[1]
    place = lax.broadcasted_iota(jnp.int32, (HEADS, count), 1)
    head_group = lax.rem(lax.broadcasted_iota(jnp.int32, (HEADS, count), 0), pairs) // (pairs // KV)
    same_group = lax.rem(place, KV) == head_group
    slot = place // KV
    factor = HD ** (-0.5)

    def widen(fresh):
        each = jnp.broadcast_to(fresh[:, None, :], (KV, pairs // KV, HD)).reshape(pairs, HD)
        return jnp.concatenate([each, each], axis=0)

    for r in range(4):
        def piece(t):
            return rqf[pl.ds(4 * t + r, pairs, stride=16), :]

        position = lengths[r]
        angle = frequency * position.astype(F32)
        cosine = jnp.cos(angle)
        sine = jnp.where(lane < HD // 2, -1.0, 1.0) * jnp.sin(angle)
        q = turn(jnp.concatenate([piece(0), piece(1)], axis=0), cosine, sine).astype(BF16)
        k_fresh = jnp.sum(piece(2).reshape(KV, pairs // KV, HD), axis=1)
        v_fresh = jnp.sum(piece(3).reshape(KV, pairs // KV, HD), axis=1)
        k_turned = turn(k_fresh, cosine, sine).astype(BF16).astype(F32)
        own = jnp.sum(q.astype(F32) * widen(k_turned), axis=1, keepdims=True) * factor
        visible = same_group & (slot < position)
        scores = jnp.where(visible, dot_nt(q, kc[r]) * factor, -jnp.inf)
        highest = jnp.maximum(jnp.max(scores, axis=1, keepdims=True), own)
        raised = jnp.exp(scores - highest)
        own_raised = jnp.exp(own - highest)
        total = jnp.sum(raised, axis=1, keepdims=True) + own_raised
        weights = (raised / total).astype(BF16)
        own_weight = (own_raised / total).astype(BF16).astype(F32)
        mixed = dot_nn(weights, vc[r]) + own_weight * widen(v_fresh)
        mixed = mixed.astype(BF16).astype(F32)
        for t in (0, 1):
            out[pl.ds(4 * t + r, pairs, stride=8), :] = mixed[t * pairs : (t + 1) * pairs]


def layer_kernel(
    hidden_ref, gain0, gain1, lengths, wq_hbm, wk_hbm, wv_hbm, wo_hbm, wg_hbm, wu_hbm, wd_hbm, kc_hbm, vc_hbm,
    out_ref,
    g, wq, wkv, wo, wgu, wd, kc, vc, acc, sbuf, rbuf, near, ysend, yrecv, res, hid,
    qkv, qkv_s, qkv_r, qkv_y, heads, msgf, msg, rq, rqf, msg2, rq2, attf, att,
    pg, s1, r1, s2, r2, act, scale,
    lsem, gss, grs, ssem, rsem, yss, yrs, wss, wrs, ass, ars, bss, brs,
):
    at = Place()
    width = hidden_ref.shape[1]
    units = wd_hbm.shape[0]
    half = width // 2
    loads = [
        pltpu.make_async_copy(src, dst, lsem.at[i])
        for i, (src, dst) in enumerate(
            (
                (wq_hbm, wq),
                (wk_hbm, wkv.at[pl.ds(0, 16)]),
                (wv_hbm, wkv.at[pl.ds(16, 16)]),
                (kc_hbm, kc),
                (vc_hbm, vc),
                (wo_hbm, wo),
                (wg_hbm, wgu.at[0, pl.ds(0, units)]),
                (wu_hbm, wgu.at[1, pl.ds(0, units)]),
                (wd_hbm, wd.at[pl.ds(0, units)]),
            )
        )
    ]
    for load in loads:
        load.start()
    hid[at.yh] = hidden_ref[...]
    for f in (0, 1):
        fill_own(g, at.h, hidden_ref[...].astype(F32), gain0[...].astype(F32), f)
    enter(at)
    pairs = ((gss, grs), (ssem, rsem), (yss, yrs), (wss, wrs), (ass, ars), (bss, brs))
    glink, link, ylink, wlink, alink, blink = (Link(a, b, at.partner) for a, b in pairs)
    c_, yl = at.core, at.yl
    tasks = {}

    def add(name, body, cost=0.0):
        tasks[name] = (body, cost)

    def here(c):
        return (at.yh, c)

    def there(c):
        return (at.yh, 1 - c)

    def fresh_zeros():
        wkv[pl.ds(32, 96), :] = jnp.zeros((96, width), BF16)
        for k in (0, 1):
            wgu[k, pl.ds(units, 64), :] = jnp.zeros((64, width), BF16)
        wd[pl.ds(units, 64), :] = jnp.zeros((64, width), BF16)

    add("zeros", fresh_zeros, 0.6)

    def swap_hidden():
        mine = hid.at[at.yh]
        ylink.send(8, mine, mine, at.partner)

    def hidden_there():
        theirs = hid.at[1 - at.yh]
        ylink.wait(8, theirs, at.partner)

    add("zh_send", swap_hidden)
    add("zh_wait", hidden_there)

    def add_loaded(name, which):
        def body():
            for load in which:
                load.wait()

        add(name, body)

    add_loaded("load_qkv", loads[:3])
    add_loaded("load_cache", loads[3:5])
    add_loaded("load_out", loads[5:6])
    add_loaded("load_mlp", loads[6:])

    def add_gather(turn, c):
        name = f"g{turn}{c}"
        halves = [Gather(at, glink, g, c, f) for f in (0, 1)]

        def slot(f):
            return c * 2 + f

        def own_rows():
            for f in (0, 1):
                mine = g.at[at.h, :, halves[f].cols]
                like = lambda f=f: g.at[0, :, halves[f].cols]
                ylink.send(slot(f), mine, mine, at.partner, c, like)

        def new_rows(f):
            fill_own(g, at.block(c, 0, 0, 0), res[c].astype(F32), gain1[...].astype(F32), f)

        if turn == 0:
            add(f"{name}.own", lambda: only(here(c), own_rows))
        else:
            for f in (0, 1):
                add(f"{name}.{f}.own", functools.partial(new_rows, f), 0.2)
        for f in (0, 1):
            def arrive(f=f):
                theirs = g.at[at.partner[1], :, halves[f].cols]
                only(there(c), lambda: ylink.wait(slot(f), theirs, at.partner))

            if turn == 0:
                add(f"{name}.{f}.arrive", arrive)
            halves[f].tasks(add, f"{name}.{f}")

        def finish():
            for f in (0, 1):
                glink.finish(slots_of(c, f))
            only(here(c), lambda: ylink.finish([slot(0), slot(1)], c))

        for f in (0, 1):
            add(f"{name}.{f}.end", halves[f].end)
        if turn == 0:
            add(f"{name}.finish", finish)

    def add_scatter(turn, c):
        name = f"s{turn}{c}"
        for f in (0, 1):
            one = Scatter(at, link, acc, sbuf, rbuf, c, f)
            one.tasks(add, f"{name}.{f}")
            slot = 4 + c * 2 + f if turn == 0 else 9 + f
            buf = c * 2 + f if turn == 0 else 4 + f
            cols = pl.ds(f * half, half)

            def total(one=one, f=f, slot=slot, buf=buf):
                near[c, f] = one.total()

                def pass_over():
                    ysend[buf] = near[c, f].astype(BF16)
                    ylink.send(slot, ysend.at[buf], yrecv.at[buf], at.partner, 1 - c, lambda: ysend.at[buf])

                if turn == 0:
                    ysend[buf] = near[c, f].astype(BF16)
                    ylink.send(slot, ysend.at[buf], yrecv.at[buf], at.partner)
                else:
                    only(there(c), pass_over)

            def last(f=f, slot=slot, buf=buf, cols=cols):
                def body():
                    ylink.wait(slot, yrecv.at[buf], at.partner)
                    value = near[c, f] + yrecv[buf].astype(F32)
                    out_ref[:, cols] = (res[c, :, cols].astype(F32) + value).astype(BF16)

                if turn == 0:
                    ylink.wait(slot, yrecv.at[buf], at.partner)
                    value = ysend[buf].astype(F32) + yrecv[buf].astype(F32)
                    res[c, :, cols] = (hid[c, :, cols].astype(F32) + value).astype(BF16)
                else:
                    only(here(c), body)

            add(f"{name}.{f}.total", total, 0.15)
            add(f"{name}.{f}.last", last, 0.1)
            if turn == 0:
                add(f"{name}.{f}.finish", functools.partial(link.finish, slots_of(c, f)))

    def add_attention(c):
        active, passive = (at.yl, c), (at.yl, 1 - c)

        def project(f):
            cols = pl.ds(f * half, half)
            rows = g[pl.ds(c * 16, 16), :, cols].reshape(256, half)
            query = dot_nn(rows, wq[cols, :]).reshape(2, 128, 256)
            fresh = dot_nt(rows, wkv[:, cols]).reshape(2, 128, 128)
            if f == 0:
                qkv[c, :, :, pl.ds(0, 256)] = query
                qkv[c, :, :, pl.ds(256, 128)] = fresh
                return
            extra = g[pl.ds(c * 16, 16), :, pl.ds(width, 128)].reshape(2, 128, 128).astype(F32)
            qkv[c, :, :, pl.ds(0, 256)] += query
            qkv[c, :, :, pl.ds(256, 128)] += fresh + extra
            qkv_s[c] = qkv[c, 1 - c_].astype(BF16)
            wlink.send(2 * c, qkv_s.at[c], qkv_r.at[2 * c], at.core_peer)

        def over_y():
            def across():
                wlink.wait(2 * c, qkv_r.at[2 * c], at.core_peer)
                total = qkv[c, c_] + qkv_r[2 * c].astype(F32)
                lanes = lane_ids(128)
                tile = total[:, 256:]
                qkv_y[:, pl.ds(0, 256)] = total[:, :256].astype(BF16)
                qkv_y[:, pl.ds(256, 128)] = split_sum(joined_sum(tile, lanes), lanes, tile).astype(BF16)
                wlink.send(1, qkv_y, qkv_r.at[1], at.y_peer, 1 - c, lambda: qkv_y)

            only(passive, across)

        def sum_up():
            total = qkv[c, c_]
            for i, peer in ((2 * c, at.core_peer), (1, at.y_peer)):
                wlink.wait(i, qkv_r.at[i], peer)
                total = total + qkv_r[i].astype(F32)
            norm = lax.rsqrt(joined_sum(total[:, 256:], lane_ids(128)) / D + norm_eps)
            scaled = (total * norm).astype(BF16)
            row = lax.broadcasted_iota(jnp.int32, (128, 256), 0)
            col = lax.broadcasted_iota(jnp.int32, (128, 256), 1)
            wanted = 16 * (col // 128) + lax.rem(col, 16)
            placed = (row == wanted) & (lax.rem(col, 128) // 16 == lax.rem(at.h, 8))
            fresh = dot_nn(scaled[:, 256:], jnp.where(placed, 1.0, 0.0).astype(BF16))
            heads[0] = scaled[:, :128].astype(F32)
            heads[1] = scaled[:, 128:256].astype(F32)
            heads[2] = fresh[:, :128]
            heads[3] = fresh[:, 128:]
            for t in range(4):
                for r in range(4):
                    msgf[pl.ds(4 * t + r, 32, stride=16), :] = heads[t, pl.ds(r, 32, stride=4), :]
            msg[...] = msgf[...].astype(BF16).reshape(32, 16, 128)
            exchange(at, alink, lambda d: msg.at[d], lambda d: rq.at[d], c, lambda: msg.at[pl.ds(0, 31)])

        def eight(ref):
            return lambda d: ref.at[pl.ds(pl.multiple_of(d * 8, 8), 8)]

        def attention():
            exchanged(at, alink, rq.at[pl.ds(0, 31)])
            rq[at.h] = msg[at.h]
            rqf[...] = rq[...].astype(F32).reshape(512, 128)
            attend(lengths, rqf, kc, vc, msg2)
            exchange(at, blink, eight(msg2), eight(rq2), c, lambda: msg2.at[pl.ds(0, 248)])

        def hand_out():
            exchanged(at, blink, rq2.at[pl.ds(0, 248)])
            own8 = pl.ds(pl.multiple_of(at.h * 8, 8), 8)
            rq2[own8, :] = msg2[own8, :]
            for t in (0, 1):
                for r in range(4):
                    attf[t, pl.ds(r, 32, stride=4), :] = rq2[pl.ds(4 * t + r, 32, stride=8), :]
                att[at.w, :, pl.ds(t * 128, 128)] = attf[t].astype(BF16)
            for i, peer in enumerate((at.core_peer, at.y_peer)):
                wlink.send(3 + i, att.at[at.w], att.at[at.w], peer, c, lambda: att.at[0])
            alink.finish(None, c)
            blink.finish(None, c)

        def take_in():
            only(active, lambda: wlink.wait(3, att.at[at.core_peer[0]], at.core_peer))

            def across():
                part = att.at[at.y_peer[0]]
                wlink.wait(4, part, at.y_peer)
                wlink.send(5, part, part, at.core_peer, 1 - c, lambda: att.at[0])

            only(passive, across)

        def take_other():
            only(passive, lambda: wlink.wait(5, att.at[at.far_peer[0]], at.core_peer))

        def out_product(f):
            rows = att[pl.ds(2 * c, 2)].reshape(256, 256)
            for i in (2 * f, 2 * f + 1):
                cols = pl.ds(i * 1024, 1024)
                acc[pl.ds(c * 16, 16), :, cols] = dot_nn(rows, wo[:, cols]).reshape(16, 16, 1024)

        for f in (0, 1):
            add(f"a{c}.project{f}", functools.partial(project, f), 0.1 * f)
        add(f"a{c}.over", over_y, 0.25)
        add(f"a{c}.sum", lambda: only(active, sum_up), 1.0)
        add(f"a{c}.attend", lambda: only(active, attention), 1.2)
        add(f"a{c}.hand", lambda: only(active, hand_out), 0.3)
        add(f"a{c}.take", take_in)
        add(f"a{c}.other", take_other)
        for f in (0, 1):
            add(f"a{c}.out{f}", functools.partial(out_product, f))

    def add_mlp(c):
        cuts = ((0, 256), (256, 256), (512, 384))

        def slot(i, which):
            return 6 + (c * 3 + i) * 7 + which

        def gate_up(k, i, f):
            cols, depth = pl.ds(*cuts[i]), pl.ds(f * half, half)
            rows = g[pl.ds(c * 16, 16), :, depth].reshape(256, half)
            value = dot_nt(rows, wgu[k, cols, depth]).reshape(4, 64, cuts[i][1])
            if f == 0:
                pg[k, c, :, :, cols] = value
                return
            pg[k, c, :, :, cols] += value
            if i == 2 and k == 0:
                extra = g[pl.ds(c * 16, 16), :, pl.ds(width, 128)].reshape(4, 64, 128).astype(F32)
                pg[0, c, :, :, pl.ds(768, 128)] += extra
            s1[c, k, :, :, cols] = pg[k, c, pl.ds(2 * (1 - c_), 2), :, cols].astype(BF16)
            wlink.send(slot(i, k), s1.at[c, k, :, :, cols], r1.at[c, k, :, :, cols], at.core_peer)

        def over_y(k, i):
            cols = pl.ds(*cuts[i])
            wlink.wait(slot(i, k), r1.at[c, k, :, :, cols], at.core_peer)
            value = pg[k, c, 2 * c_ + 1 - yl, :, cols] + r1[c, k, 1 - yl, :, cols].astype(F32)
            s2[c, k, :, cols] = value.astype(BF16)
            if i == 2 and k == 0:
                lanes = lane_ids(64)
                tile = value[:, 256:]
                s2[c, k, :, pl.ds(768, 128)] = split_sum(joined_sum(tile, lanes), lanes, tile).astype(BF16)
            wlink.send(slot(i, 2 + k), s2.at[c, k, :, cols], r2.at[c, k, :, cols], at.y_peer)

        def activate(i):
            cols = pl.ds(*cuts[i])
            sums = []
            for k in (0, 1):
                wlink.wait(slot(i, 2 + k), r2.at[c, k, :, cols], at.y_peer)
                total = pg[k, c, 2 * c_ + yl, :, cols] + r1[c, k, yl, :, cols].astype(F32)
                sums.append(total + r2[c, k, :, cols].astype(F32))
            if i == 2:
                norm = lax.rsqrt(joined_sum(sums[0][:, 256:], lane_ids(64)) / D + norm_eps)
                scale[c] = jnp.broadcast_to(norm, (64, 128))
            norm = scale[c, :, 0:1]
            gate, up = sums[0] * norm, sums[1] * norm
            mine = act.at[c, 2 * c_ + yl, :, cols]
            act[c, 2 * c_ + yl, :, cols] = (gate / (1.0 + jnp.exp(-gate)) * up).astype(BF16)
            wlink.send(slot(i, 4), mine, mine, at.y_peer)
            wlink.send(slot(i, 5), mine, mine, at.core_peer)

        def pass_on(i):
            other = act.at[c, 2 * c_ + 1 - yl, :, pl.ds(*cuts[i])]
            wlink.wait(slot(i, 4), other, at.y_peer)
            wlink.send(slot(i, 6), other, other, at.core_peer)

        def complete():
            for i in range(3):
                cols = pl.ds(*cuts[i])
                wlink.wait(slot(i, 5), act.at[c, 2 * (1 - c_) + yl, :, cols], at.core_peer)
                wlink.wait(slot(i, 6), act.at[c, 2 * (1 - c_) + 1 - yl, :, cols], at.core_peer)

        def down(i):
            rows = act[c].reshape(256, act.shape[3])
            cols = pl.ds(i * 1024, 1024)
            acc[pl.ds(c * 16, 16), :, cols] = dot_nn(rows, wd[:, cols]).reshape(16, 16, 1024)

        for i in (2, 0, 1):
            for k in (0, 1):
                for f in (0, 1):
                    add(f"m{c}.gu{k}{i}{f}", functools.partial(gate_up, k, i, f), 0.03 + 0.06 * f)
                add(f"m{c}.y{k}{i}", functools.partial(over_y, k, i), 0.07)
            add(f"m{c}.act{i}", functools.partial(activate, i), 0.2)
            add(f"m{c}.pass{i}", functools.partial(pass_on, i))
        add(f"m{c}.complete", complete)
        for i in range(4):
            add(f"m{c}.down{i}", functools.partial(down, i))

    for c in (0, 1):
        add_gather(0, c)
        add_attention(c)
        add_scatter(0, c)
        add_gather(1, c)
        add_mlp(c)
        add_scatter(1, c)

    for name in order_of(tasks):
        enter_task(name, tasks[name][1])
        tasks[name][0]()
    for each in (glink, link, ylink, wlink):
        each.finish()
    for c in (0, 1):
        only(here(c), lambda c=c: ylink.finish(None, c))
        only((at.yl, c), lambda c=c: wlink.finish(None, c))


def enter_task(name, cost):
    pass


ORDER = [
    "load_qkv", "g01.own", "load_cache", "g00.own", "g00.0.arrive", "g00.0.start", "g00.1.arrive",
    "g00.1.start", "g01.0.arrive", "g01.0.start", "g00.0.first", "g00.1.second", "g00.0.second",
    "g00.1.first", "g00.0.third", "g00.0.relay0", "g00.0.relay-1", "g00.1.third", "g01.1.arrive",
    "g01.1.start", "g00.1.relay-1", "g00.0.relay1", "g00.1.relay0", "g00.0.relay2", "g00.1.relay1",
    "g01.0.third", "g00.1.relay2", "zeros", "g01.1.relay0", "g01.1.first", "load_mlp", "g01.0.second",
    "g01.1.second", "g01.0.first", "g00.0.end", "a0.project0", "g00.1.end", "a0.project1", "g01.1.third",
    "a0.over", "g01.0.relay0", "g01.0.relay2", "zh_send", "g01.0.relay-1", "g01.1.relay1", "g01.0.relay1",
    "load_out", "g01.1.relay-1", "g01.1.relay2", "a0.sum", "g00.finish", "g01.0.end", "a1.project0",
    "g01.1.end", "a1.project1", "a1.over", "a0.attend", "a1.sum", "a0.hand", "a1.attend", "a0.take",
    "a0.other", "a0.out0", "s00.0.far2", "a0.out1", "s00.1.far0", "s00.1.far2", "s00.0.far1", "s00.0.back-1",
    "g01.finish", "s00.1.back0", "s00.0.far-1", "s00.1.far1", "s00.0.far0", "a1.hand", "s00.1.far-1",
    "s00.0.back1", "s00.1.back2", "s00.0.on2", "s00.1.on0", "s00.1.on2", "s00.0.back2", "s00.1.back1",
    "s00.0.on1", "s00.1.on1", "s00.0.on-1", "s00.1.back-1", "s00.0.back0", "s00.0.on0", "s00.1.on-1",
    "a1.take", "a1.other", "a1.out0", "s01.0.far1", "a1.out1", "s00.0.line_far", "s01.1.far2", "s01.0.far2",
    "s01.0.far-1", "s00.0.line_on", "s00.1.line_far", "s01.1.far-1", "s00.1.line_back", "s00.0.line_back",
    "s00.1.line_on", "s01.1.far1", "s01.1.far0", "s01.1.back2", "s01.0.back0", "s01.0.far0", "s01.1.back-1",
    "s01.1.on2", "s01.0.on2", "s01.0.back1", "s01.0.back2", "s01.0.on1", "s00.0.total", "s01.0.on-1",
    "s01.1.on1", "s01.1.back0", "s01.1.on-1", "s00.1.total", "s01.1.back1", "s01.0.back-1", "s01.0.on0",
    "s01.1.on0", "s01.0.line_far", "s01.1.line_far", "zh_wait", "s01.0.line_back", "s01.1.line_back",
    "s01.0.line_on", "s01.1.line_on", "s00.0.last", "g10.0.own", "g10.0.start", "s00.1.last", "g10.1.own",
    "g10.1.start", "s01.0.total", "g10.0.second", "g10.0.first", "s01.1.total", "g10.1.first", "g10.0.third",
    "g10.1.second", "g10.0.relay0", "g10.1.third", "g10.0.relay-1", "s01.0.last", "g11.0.own", "g11.0.start",
    "g10.0.relay1", "s01.1.last", "g10.1.relay0", "g11.1.own", "g10.1.relay1", "g10.0.relay2", "g11.1.start",
    "g10.1.relay-1", "g10.1.relay2", "g11.0.second", "g10.0.end", "g11.0.third", "g11.1.relay0",
    "g11.0.first", "m0.gu120", "m0.gu000", "g11.1.first", "g11.1.second", "m0.gu020", "s00.1.finish",
    "m0.gu100", "g10.1.end", "m0.gu121", "g11.1.third", "s00.0.finish", "m0.gu021", "g11.0.relay-1",
    "g11.0.relay0", "m0.y12", "m0.gu101", "m0.gu001", "g11.0.relay2", "m0.y02", "g11.0.relay1", "m0.gu110",
    "m0.gu010", "m0.gu011", "s01.0.finish", "m0.y10", "m0.gu111", "g11.1.relay1", "m0.y00", "m0.y01",
    "g11.1.relay-1", "m0.y11", "g11.1.relay2", "m0.act2", "g11.0.end", "m1.gu110", "m1.gu010", "m1.gu000",
    "m1.gu020", "m0.act0", "m1.gu120", "m0.act1", "g11.1.end", "m1.gu111", "m1.gu021", "m1.gu121", "m1.y11",
    "m1.gu011", "m1.y02", "m1.gu001", "m0.pass1", "m0.pass2", "m0.pass0", "s01.1.finish", "m1.y12",
    "m1.gu100", "m1.gu101", "m1.y01", "m1.y00", "m0.complete", "m0.down1", "m1.y10", "m0.down0", "s10.0.far1",
    "s10.0.far0", "m0.down2", "m0.down3", "s10.1.far2", "m1.act2", "s10.0.far-1", "s10.1.far0", "s10.0.far2",
    "s10.1.far-1", "m1.act1", "s10.1.far1", "s10.0.back2", "s10.0.back-1", "s10.0.back1", "m1.act0",
    "s10.1.back-1", "s10.1.back1", "s10.1.back2", "s10.0.on1", "s10.1.back0", "m1.pass1", "s10.0.on-1",
    "s10.1.on2", "s10.0.back0", "m1.pass0", "m1.pass2", "s10.1.on0", "s10.0.on0", "s10.1.on1", "s10.0.on2",
    "s10.1.on-1", "m1.complete", "m1.down0", "m1.down1", "s11.0.far2", "s11.0.far1", "m1.down3", "m1.down2",
    "s11.1.far2", "s11.1.far-1", "s11.0.far-1", "s11.0.back2", "s11.0.back0", "s11.1.far0", "s11.0.far0",
    "s10.1.line_far", "s11.1.back2", "s11.1.far1", "s11.1.back-1", "s10.1.line_on", "s10.1.line_back",
    "s11.0.back-1", "s11.0.back1", "s11.0.on1", "s10.0.line_on", "s11.0.on2", "s11.1.on2", "s11.1.on-1",
    "s11.1.on1", "s11.1.back1", "s10.0.line_far", "s10.0.line_back", "s11.1.on0", "s11.1.back0", "s11.0.on0",
    "s11.0.on-1", "s11.1.line_far", "s11.0.line_far", "s10.1.total", "s11.1.line_on", "s11.1.line_back",
    "s11.0.line_on", "s11.0.line_back", "s10.0.total", "s11.1.total", "s11.0.total", "s10.1.last",
    "s11.1.last", "s10.0.last", "s11.0.last",
]


def order_of(tasks):
    assert sorted(ORDER) == sorted(tasks)
    return ORDER


VM = pl.BlockSpec(memory_space=pltpu.VMEM)
ANY = pl.BlockSpec(memory_space=pl.ANY)
DMA = pltpu.SemaphoreType.DMA


def on_device(
    hidden_in,
    attn_gain,
    mlp_gain,
    w_query,
    w_key,
    w_value,
    w_out,
    w_gate,
    w_up,
    w_down,
    key_cache,
    value_cache,
    lengths,
):
    width = hidden_in.shape[1]
    units = w_gate.shape[1]
    padded = units + 64
    slots = key_cache.shape[1] * KV
    return pl.pallas_call(
        layer_kernel,
        out_shape=jax.ShapeDtypeStruct(hidden_in.shape, BF16),
        in_specs=[VM, VM, VM, pl.BlockSpec(memory_space=pltpu.SMEM)] + [ANY] * 9,
        out_specs=VM,
        scratch_shapes=[
            pltpu.VMEM((32, 16, width + 128), BF16),
            pltpu.VMEM((width, 256), BF16),
            pltpu.VMEM((128, width), BF16),
            pltpu.VMEM((256, width), BF16),
            pltpu.VMEM((2, padded, width), BF16),
            pltpu.VMEM((padded, width), BF16),
            pltpu.VMEM((4, slots, HD), BF16),
            pltpu.VMEM((4, slots, HD), BF16),
            pltpu.VMEM((32, 16, width), F32),
            pltpu.VMEM((TREE, 16, width // 2), BF16),
            pltpu.VMEM((TREE, 16, width // 2), BF16),
            pltpu.VMEM((2, 2, 16, width // 2), F32),
            pltpu.VMEM((6, 16, width // 2), BF16),
            pltpu.VMEM((6, 16, width // 2), BF16),
            pltpu.VMEM((2, 16, width), BF16),
            pltpu.VMEM((2, 16, width), BF16),
            pltpu.VMEM((2, 2, 128, 384), F32),
            pltpu.VMEM((2, 128, 384), BF16),
            pltpu.VMEM((3, 128, 384), BF16),
            pltpu.VMEM((128, 384), BF16),
            pltpu.VMEM((4, 128, 128), F32),
            pltpu.VMEM((512, 128), F32),
            pltpu.VMEM((32, 16, 128), BF16),
            pltpu.VMEM((32, 16, 128), BF16),
            pltpu.VMEM((512, 128), F32),
            pltpu.VMEM((256, 128), F32),
            pltpu.VMEM((256, 128), F32),
            pltpu.VMEM((2, 128, 128), F32),
            pltpu.VMEM((4, 128, 256), BF16),
            pltpu.VMEM((2, 2, 4, 64, padded), F32),
            pltpu.VMEM((2, 2, 2, 64, padded), BF16),
            pltpu.VMEM((2, 2, 2, 64, padded), BF16),
            pltpu.VMEM((2, 2, 64, padded), BF16),
            pltpu.VMEM((2, 2, 64, padded), BF16),
            pltpu.VMEM((2, 4, 64, padded), BF16),
            pltpu.VMEM((2, 64, 128), F32),
            DMA((9,)),
            DMA((TREE,)), DMA((TREE,)),
            DMA((TREE,)), DMA((TREE,)),
            DMA((16,)), DMA((16,)),
            DMA((48,)), DMA((48,)),
            DMA((1,)), DMA((1,)),
            DMA((1,)), DMA((1,)),
        ],
        compiler_params=pltpu.CompilerParams(
            collective_id=0, has_side_effects=True, vmem_limit_bytes=63 * 2**20
        ),
    )(
        hidden_in,
        attn_gain.reshape(-1, 128),
        mlp_gain.reshape(-1, 128),
        lengths,
        w_query,
        w_key.T,
        w_value.T,
        w_out,
        w_gate.T,
        w_up.T,
        w_down,
        key_cache.reshape(4, slots, HD),
        value_cache.reshape(4, slots, HD),
    )


def solution(mesh):
    return jax.shard_map(
        on_device,
        mesh=mesh,
        in_specs=(
            P("hidden", "width"),
            P("width"),
            P("width"),
            P("width", "hidden"),
            P("width", "hidden"),
            P("width", "hidden"),
            P("hidden", "width"),
            P("width", "hidden"),
            P("width", "hidden"),
            P("hidden", "width"),
            P(("width", "hidden"), None, None, None),
            P(("width", "hidden"), None, None, None),
            P(("width", "hidden")),
        ),
        out_specs=P("hidden", "width"),
        check_vma=False,
    )
```

```python
import functools
import math

import jax
import jax.numpy as jnp
from jax import lax
from jax.experimental import pallas as pl
from jax.experimental.pallas import tpu as pltpu
from jax.sharding import PartitionSpec as P

D = 16384
HEADS = 64
KV = 4
HD = 128
MESH = pl.DeviceIdType.MESH
F32 = jnp.float32
BF16 = jnp.bfloat16

rope_base = 500000.0
norm_eps = 1e-05

OFFS = (0, -1, 1, 2)


class Place:
    def __init__(self):
        self.w = lax.axis_index("width")
        self.h = lax.axis_index("hidden")
        self.x = lax.rem(self.h, 4)
        self.z = lax.rem(self.h // 4, 4)
        self.yh = self.h // 16
        self.core = lax.rem(self.w, 2)
        self.yl = self.w // 2
        self.partner = (self.w, lax.rem(self.h + 16, 32))
        self.core_peer = (self.w + 1 - 2 * self.core, self.h)
        self.y_peer = (lax.rem(self.w + 2, 4), self.h)
        self.far_peer = (lax.rem(self.w + 2, 4) + 1 - 2 * self.core, self.h)

    def block(self, c, f, p, q):
        dx, dz = (p, q) if f == 0 else (q, p)
        return c * 16 + lax.rem(self.z + (dz + 4), 4) * 4 + lax.rem(self.x + (dx + 4), 4)

    def neighbour(self, f, phase, sgn):
        p, q = (sgn, 0) if phase == 0 else (0, sgn)
        return (self.w, self.yh * 16 + self.block(0, f, p, q))

    def along(self, i):
        return (self.w, lax.rem(self.h + i, 32))


def enter(at):
    barrier = pltpu.get_barrier_semaphore()
    peers = [at.core_peer, at.y_peer, at.partner]
    peers += [at.neighbour(f, 0, places) for f in (0, 1) for places in (1, -1, 2)]
    for peer in peers:
        pl.semaphore_signal(barrier, inc=1, device_id=peer, device_id_type=MESH)
    pl.semaphore_wait(barrier, len(peers))


class Link:
    def __init__(self, ssem, rsem, peer):
        self.ssem, self.rsem, self.peer, self.sent = ssem, rsem, peer, {}

    def copy(self, slot, src, dst, peer):
        return pltpu.make_async_remote_copy(
            src_ref=src,
            dst_ref=dst,
            send_sem=self.ssem.at[slot],
            recv_sem=self.rsem.at[slot],
            device_id=peer,
            device_id_type=MESH,
        )

    def send(self, slot, src, dst, peer, key=None, like=None):
        self.copy(slot, src, dst, peer).start()
        self.sent[(slot, key)] = like or (lambda: src)

    def wait(self, slot, dst, peer):
        self.copy(slot, dst, dst, peer).wait_recv()

    def finish(self, slots=None, key=None):
        for which in [w for w in self.sent if w[1] == key and (slots is None or w[0] in slots)]:
            like = self.sent.pop(which)()
            self.copy(which[0], like, like, self.peer).wait_send()


def only(flag, body):
    pl.when(flag[0] == flag[1])(body)


TREE = 60


def slots_of(c, f):
    return range((c * 2 + f) * 15, (c * 2 + f) * 15 + 15)


def slot_of(c, f, phase, j, d):
    base = (c * 2 + f) * 15
    if phase == 0:
        return base + {1: 0, -1: 1, 0: 2}[d]
    return base + 3 + OFFS.index(j) * 3 + {1: 0, -1: 1, 0: 2}[d]


class Gather:
    def __init__(self, at, link, g, c, f):
        half = g.shape[2] // 2 // 128 * 128
        self.cols = pl.ds(0, half) if f == 0 else pl.ds(half, g.shape[2] - half)
        self.at, self.link, self.g, self.c, self.f = at, link, g, c, f
        self.s = 1 if (c ^ f) == 0 else -1

    def ref(self, p, q):
        return self.g.at[self.at.block(self.c, self.f, p, q), :, self.cols]

    def send(self, phase, j, d, p, q, sgn):
        r = self.ref(p, q)
        slot = slot_of(self.c, self.f, phase, j, d)
        self.link.send(slot, r, r, self.at.neighbour(self.f, phase, sgn))

    def wait(self, phase, j, d, p, q, sgn):
        slot = slot_of(self.c, self.f, phase, j, d)
        self.link.wait(slot, self.ref(p, q), self.at.neighbour(self.f, phase, sgn))

    def way(self, j):
        return self.s if j in (0, -self.s) else -self.s

    def spread(self, j):
        self.send(1, j, self.s, j, 0, self.s)
        self.send(1, j, -self.s, j, 0, -self.s)

    def start(self):
        self.send(0, 0, self.s, 0, 0, self.s)
        self.send(0, 0, -self.s, 0, 0, -self.s)
        self.send(0, 0, 0, 0, 0, 2)
        self.spread(0)

    def first(self):
        s = self.s
        self.wait(0, 0, s, -s, 0, s)
        self.spread(-s)

    def second(self):
        s = self.s
        self.wait(0, 0, -s, s, 0, -s)
        self.spread(s)

    def third(self):
        self.wait(0, 0, 0, 2, 0, 2)
        self.spread(2)

    def relay(self, j):
        s = self.way(j)
        self.wait(1, j, s, j, -s, s)
        self.send(1, j, 0, j, -s, s)

    def end(self):
        for j in OFFS:
            s = self.way(j)
            self.wait(1, j, -s, j, s, -s)
        for j in OFFS:
            self.wait(1, j, 0, j, 2, self.way(j))

    def tasks(self, add):
        add(self.start)
        add(self.first)
        add(self.second)
        add(self.third)
        for j in (0, -self.s, self.s, 2):
            add(functools.partial(self.relay, j))


class Scatter:
    def __init__(self, at, link, acc, sbuf, rbuf, c, f):
        half = acc.shape[2] // 2
        self.cols = pl.ds(f * half, half)
        self.at, self.link, self.acc, self.sbuf, self.rbuf, self.c, self.f = at, link, acc, sbuf, rbuf, c, f
        self.s = 1 if (c ^ f) == 0 else -1

    def own(self, p, q):
        return self.acc[self.at.block(self.c, self.f, p, q), :, self.cols]

    def send(self, phase, j, d, sgn, value):
        slot = slot_of(self.c, self.f, phase, j, d)
        self.sbuf[slot] = value.astype(BF16)
        self.link.send(slot, self.sbuf.at[slot], self.rbuf.at[slot], self.at.neighbour(self.f, phase, sgn))

    def take(self, phase, j, d, sgn):
        slot = slot_of(self.c, self.f, phase, j, d)
        self.link.wait(slot, self.rbuf.at[slot], self.at.neighbour(self.f, phase, sgn))
        return self.rbuf[slot].astype(F32)

    def way(self, j):
        return self.s if j in (0, -self.s) else -self.s

    def column(self, j):
        s = self.way(j)
        return self.own(j, 0) + self.take(1, j, s, s) + self.take(1, j, -s, -s)

    def far(self, j):
        self.send(1, j, 0, self.way(j), self.own(j, 2))

    def back(self, j):
        s = self.way(j)
        self.send(1, j, -s, -s, self.own(j, -s))

    def on(self, j):
        s = self.way(j)
        self.send(1, j, s, s, self.own(j, s) + self.take(1, j, 0, s))

    def line_far(self):
        self.send(0, 0, 0, 2, self.column(2))

    def line_back(self):
        self.send(0, 0, -self.s, -self.s, self.column(-self.s))

    def line_on(self):
        self.send(0, 0, self.s, self.s, self.column(self.s))

    def total(self):
        value = self.column(0)
        for d, sgn in ((self.s, self.s), (-self.s, -self.s), (0, 2)):
            value = value + self.take(0, 0, d, sgn)
        return value

    def tasks(self, add):
        order = (2, -self.s, self.s, 0)
        for j in order:
            add(functools.partial(self.far, j), 0.06)
        for j in order:
            add(functools.partial(self.back, j), 0.06)
        for j in order:
            add(functools.partial(self.on, j), 0.08)
        add(self.line_far, 0.1)
        add(self.line_back, 0.1)
        add(self.line_on, 0.1)


def dot_nn(a, b):
    return jnp.dot(a, b, preferred_element_type=F32)


def dot_nt(a, b):
    return lax.dot_general(a, b, (((1,), (1,)), ((), ())), preferred_element_type=F32)


SS = 96


def split_sum(total, lanes, rest):
    high = total.astype(BF16).astype(F32)
    return jnp.where(lanes == SS, high, jnp.where(lanes == SS + 1, total - high, rest))


def joined_sum(tile, lanes):
    return jnp.sum(jnp.where((lanes == SS) | (lanes == SS + 1), tile, 0.0), axis=1, keepdims=True)


def lane_ids(rows):
    return lax.broadcasted_iota(jnp.int32, (rows, 128), 1)


def fill_own(g, block, values, gain, f):
    width = values.shape[1]
    tiles = width // 256
    for i in range(f * tiles, (f + 1) * tiles):
        cols = pl.ds(i * 128, 128)
        g[block, :, cols] = (values[:, i * 128 : (i + 1) * 128] * gain[i : i + 1]).astype(BF16)
    if f == 1:
        part = jnp.sum(values * values, axis=1, keepdims=True)
        lanes = lane_ids(values.shape[0])
        tail = split_sum(part, lanes, jnp.zeros(lanes.shape, F32))
        g[block, :, pl.ds(width, 128)] = tail.astype(BF16)


def exchange(at, link, src, dst, key, like):
    for i in range(1, 32):
        peer = at.along(i)
        link.send(0, src(peer[1]), dst(at.h), peer, key, like)


def exchanged(at, link, blocks):
    link.wait(0, blocks, at.partner)


def turn(values, cosine, sine):
    return values * cosine + pltpu.roll(values, HD // 2, 1) * sine


def attend(lengths, rqf, kc, vc, out):
    pairs = HEADS // 2
    lane = lax.broadcasted_iota(jnp.int32, (1, HD), 1)
    entry = lax.rem(lane, HD // 2).astype(F32)
    frequency = jnp.exp(entry * (-2.0 * math.log(rope_base) / HD))
    count = kc.shape[1]
    place = lax.broadcasted_iota(jnp.int32, (HEADS, count), 1)
    head_group = lax.rem(lax.broadcasted_iota(jnp.int32, (HEADS, count), 0), pairs) // (pairs // KV)
    same_group = lax.rem(place, KV) == head_group
    slot = place // KV
    factor = HD ** (-0.5)

    def widen(fresh):
        each = jnp.broadcast_to(fresh[:, None, :], (KV, pairs // KV, HD)).reshape(pairs, HD)
        return jnp.concatenate([each, each], axis=0)

    for r in range(4):
        def piece(t):
            return rqf[pl.ds(4 * t + r, pairs, stride=16), :]

        position = lengths[r]
        angle = frequency * position.astype(F32)
        cosine = jnp.cos(angle)
        sine = jnp.where(lane < HD // 2, -1.0, 1.0) * jnp.sin(angle)
        q = turn(jnp.concatenate([piece(0), piece(1)], axis=0), cosine, sine).astype(BF16)
        k_fresh = jnp.sum(piece(2).reshape(KV, pairs // KV, HD), axis=1)
        v_fresh = jnp.sum(piece(3).reshape(KV, pairs // KV, HD), axis=1)
        k_turned = turn(k_fresh, cosine, sine).astype(BF16).astype(F32)
        own = jnp.sum(q.astype(F32) * widen(k_turned), axis=1, keepdims=True) * factor
        visible = same_group & (slot < position)
        scores = jnp.where(visible, dot_nt(q, kc[r]) * factor, -jnp.inf)
        highest = jnp.maximum(jnp.max(scores, axis=1, keepdims=True), own)
        raised = jnp.exp(scores - highest)
        own_raised = jnp.exp(own - highest)
        total = jnp.sum(raised, axis=1, keepdims=True) + own_raised
        weights = (raised / total).astype(BF16)
        own_weight = (own_raised / total).astype(BF16).astype(F32)
        mixed = dot_nn(weights, vc[r]) + own_weight * widen(v_fresh)
        mixed = mixed.astype(BF16).astype(F32)
        for t in (0, 1):
            out[pl.ds(4 * t + r, pairs, stride=8), :] = mixed[t * pairs : (t + 1) * pairs]


def layer_kernel(
    hidden_ref, gain0, gain1, lengths, wq_hbm, wk_hbm, wv_hbm, wo_hbm, wg_hbm, wu_hbm, wd_hbm, kc_hbm, vc_hbm,
    out_ref,
    g, wq, wkv, wo, wgu, wd, kc, vc, acc, sbuf, rbuf, near, ysend, yrecv, res, hid,
    qkv, qkv_s, qkv_r, qkv_y, heads, msgf, msg, rq, rqf, msg2, rq2, attf, att,
    pg, s1, r1, s2, r2, act, scale,
    lsem, gss, grs, ssem, rsem, yss, yrs, wss, wrs, ass, ars, bss, brs,
):
    at = Place()
    width = hidden_ref.shape[1]
    units = wd_hbm.shape[0]
    half = width // 2
    loads = [
        pltpu.make_async_copy(src, dst, lsem.at[i])
        for i, (src, dst) in enumerate(
            (
                (wq_hbm, wq),
                (wk_hbm, wkv.at[pl.ds(0, 16)]),
                (wv_hbm, wkv.at[pl.ds(16, 16)]),
                (kc_hbm, kc),
                (vc_hbm, vc),
                (wo_hbm, wo),
                (wg_hbm, wgu.at[0, pl.ds(0, units)]),
                (wu_hbm, wgu.at[1, pl.ds(0, units)]),
                (wd_hbm, wd.at[pl.ds(0, units)]),
            )
        )
    ]
    for load in loads:
        load.start()
    hid[at.yh] = hidden_ref[...]
    for f in (0, 1):
        fill_own(g, at.h, hidden_ref[...].astype(F32), gain0[...].astype(F32), f)
    enter(at)
    pairs = ((gss, grs), (ssem, rsem), (yss, yrs), (wss, wrs), (ass, ars), (bss, brs))
    glink, link, ylink, wlink, alink, blink = (Link(a, b, at.partner) for a, b in pairs)
    c_, yl = at.core, at.yl
    tasks = []

    def add(body, cost=0.0):
        tasks.append((body, cost))

    def here(c):
        return (at.yh, c)

    def there(c):
        return (at.yh, 1 - c)

    def fresh_zeros():
        wkv[pl.ds(32, 96), :] = jnp.zeros((96, width), BF16)
        for k in (0, 1):
            wgu[k, pl.ds(units, 64), :] = jnp.zeros((64, width), BF16)
        wd[pl.ds(units, 64), :] = jnp.zeros((64, width), BF16)

    add(fresh_zeros, 0.6)

    def swap_hidden():
        mine = hid.at[at.yh]
        ylink.send(8, mine, mine, at.partner)

    def hidden_there():
        theirs = hid.at[1 - at.yh]
        ylink.wait(8, theirs, at.partner)

    add(swap_hidden)
    add(hidden_there)

    def add_loaded(which):
        def body():
            for load in which:
                load.wait()

        add(body)

    add_loaded(loads[:3])
    add_loaded(loads[3:5])
    add_loaded(loads[5:6])
    add_loaded(loads[6:])

    def add_gather(turn, c):
        halves = [Gather(at, glink, g, c, f) for f in (0, 1)]

        def slot(f):
            return c * 2 + f

        def own_rows():
            for f in (0, 1):
                mine = g.at[at.h, :, halves[f].cols]
                like = lambda f=f: g.at[0, :, halves[f].cols]
                ylink.send(slot(f), mine, mine, at.partner, c, like)

        def new_rows(f):
            fill_own(g, at.block(c, 0, 0, 0), res[c].astype(F32), gain1[...].astype(F32), f)

        if turn == 0:
            add(lambda: only(here(c), own_rows))
        else:
            for f in (0, 1):
                add(functools.partial(new_rows, f), 0.2)
        for f in (0, 1):
            def arrive(f=f):
                theirs = g.at[at.partner[1], :, halves[f].cols]
                only(there(c), lambda: ylink.wait(slot(f), theirs, at.partner))

            if turn == 0:
                add(arrive)
            halves[f].tasks(add)

        def finish():
            for f in (0, 1):
                glink.finish(slots_of(c, f))
            only(here(c), lambda: ylink.finish([slot(0), slot(1)], c))

        for f in (0, 1):
            add(halves[f].end)
        if turn == 0:
            add(finish)

    def add_scatter(turn, c):
        for f in (0, 1):
            one = Scatter(at, link, acc, sbuf, rbuf, c, f)
            one.tasks(add)
            slot = 4 + c * 2 + f if turn == 0 else 9 + f
            buf = c * 2 + f if turn == 0 else 4 + f
            cols = pl.ds(f * half, half)

            def total(one=one, f=f, slot=slot, buf=buf):
                near[c, f] = one.total()

                def pass_over():
                    ysend[buf] = near[c, f].astype(BF16)
                    ylink.send(slot, ysend.at[buf], yrecv.at[buf], at.partner, 1 - c, lambda: ysend.at[buf])

                if turn == 0:
                    ysend[buf] = near[c, f].astype(BF16)
                    ylink.send(slot, ysend.at[buf], yrecv.at[buf], at.partner)
                else:
                    only(there(c), pass_over)

            def last(f=f, slot=slot, buf=buf, cols=cols):
                def body():
                    ylink.wait(slot, yrecv.at[buf], at.partner)
                    value = near[c, f] + yrecv[buf].astype(F32)
                    out_ref[:, cols] = (res[c, :, cols].astype(F32) + value).astype(BF16)

                if turn == 0:
                    ylink.wait(slot, yrecv.at[buf], at.partner)
                    value = ysend[buf].astype(F32) + yrecv[buf].astype(F32)
                    res[c, :, cols] = (hid[c, :, cols].astype(F32) + value).astype(BF16)
                else:
                    only(here(c), body)

            add(total, 0.15)
            add(last, 0.1)
            if turn == 0:
                add(functools.partial(link.finish, slots_of(c, f)))

    def add_attention(c):
        active, passive = (at.yl, c), (at.yl, 1 - c)

        def project(f):
            cols = pl.ds(f * half, half)
            rows = g[pl.ds(c * 16, 16), :, cols].reshape(256, half)
            query = dot_nn(rows, wq[cols, :]).reshape(2, 128, 256)
            fresh = dot_nt(rows, wkv[:, cols]).reshape(2, 128, 128)
            if f == 0:
                qkv[c, :, :, pl.ds(0, 256)] = query
                qkv[c, :, :, pl.ds(256, 128)] = fresh
                return
            extra = g[pl.ds(c * 16, 16), :, pl.ds(width, 128)].reshape(2, 128, 128).astype(F32)
            qkv[c, :, :, pl.ds(0, 256)] += query
            qkv[c, :, :, pl.ds(256, 128)] += fresh + extra
            qkv_s[c] = qkv[c, 1 - c_].astype(BF16)
            wlink.send(2 * c, qkv_s.at[c], qkv_r.at[2 * c], at.core_peer)

        def over_y():
            def across():
                wlink.wait(2 * c, qkv_r.at[2 * c], at.core_peer)
                total = qkv[c, c_] + qkv_r[2 * c].astype(F32)
                lanes = lane_ids(128)
                tile = total[:, 256:]
                qkv_y[:, pl.ds(0, 256)] = total[:, :256].astype(BF16)
                qkv_y[:, pl.ds(256, 128)] = split_sum(joined_sum(tile, lanes), lanes, tile).astype(BF16)
                wlink.send(1, qkv_y, qkv_r.at[1], at.y_peer, 1 - c, lambda: qkv_y)

            only(passive, across)

        def sum_up():
            total = qkv[c, c_]
            for i, peer in ((2 * c, at.core_peer), (1, at.y_peer)):
                wlink.wait(i, qkv_r.at[i], peer)
                total = total + qkv_r[i].astype(F32)
            norm = lax.rsqrt(joined_sum(total[:, 256:], lane_ids(128)) / D + norm_eps)
            scaled = (total * norm).astype(BF16)
            row = lax.broadcasted_iota(jnp.int32, (128, 256), 0)
            col = lax.broadcasted_iota(jnp.int32, (128, 256), 1)
            wanted = 16 * (col // 128) + lax.rem(col, 16)
            placed = (row == wanted) & (lax.rem(col, 128) // 16 == lax.rem(at.h, 8))
            fresh = dot_nn(scaled[:, 256:], jnp.where(placed, 1.0, 0.0).astype(BF16))
            heads[0] = scaled[:, :128].astype(F32)
            heads[1] = scaled[:, 128:256].astype(F32)
            heads[2] = fresh[:, :128]
            heads[3] = fresh[:, 128:]
            for t in range(4):
                for r in range(4):
                    msgf[pl.ds(4 * t + r, 32, stride=16), :] = heads[t, pl.ds(r, 32, stride=4), :]
            msg[...] = msgf[...].astype(BF16).reshape(32, 16, 128)
            exchange(at, alink, lambda d: msg.at[d], lambda d: rq.at[d], c, lambda: msg.at[pl.ds(0, 31)])

        def eight(ref):
            return lambda d: ref.at[pl.ds(pl.multiple_of(d * 8, 8), 8)]

        def attention():
            exchanged(at, alink, rq.at[pl.ds(0, 31)])
            rq[at.h] = msg[at.h]
            rqf[...] = rq[...].astype(F32).reshape(512, 128)
            attend(lengths, rqf, kc, vc, msg2)
            exchange(at, blink, eight(msg2), eight(rq2), c, lambda: msg2.at[pl.ds(0, 248)])

        def hand_out():
            exchanged(at, blink, rq2.at[pl.ds(0, 248)])
            own8 = pl.ds(pl.multiple_of(at.h * 8, 8), 8)
            rq2[own8, :] = msg2[own8, :]
            for t in (0, 1):
                for r in range(4):
                    attf[t, pl.ds(r, 32, stride=4), :] = rq2[pl.ds(4 * t + r, 32, stride=8), :]
                att[at.w, :, pl.ds(t * 128, 128)] = attf[t].astype(BF16)
            for i, peer in enumerate((at.core_peer, at.y_peer)):
                wlink.send(3 + i, att.at[at.w], att.at[at.w], peer, c, lambda: att.at[0])
            alink.finish(None, c)
            blink.finish(None, c)

        def take_in():
            only(active, lambda: wlink.wait(3, att.at[at.core_peer[0]], at.core_peer))

            def across():
                part = att.at[at.y_peer[0]]
                wlink.wait(4, part, at.y_peer)
                wlink.send(5, part, part, at.core_peer, 1 - c, lambda: att.at[0])

            only(passive, across)

        def take_other():
            only(passive, lambda: wlink.wait(5, att.at[at.far_peer[0]], at.core_peer))

        def out_product(f):
            rows = att[pl.ds(2 * c, 2)].reshape(256, 256)
            for i in (2 * f, 2 * f + 1):
                cols = pl.ds(i * 1024, 1024)
                acc[pl.ds(c * 16, 16), :, cols] = dot_nn(rows, wo[:, cols]).reshape(16, 16, 1024)

        for f in (0, 1):
            add(functools.partial(project, f), 0.1 * f)
        add(over_y, 0.25)
        add(lambda: only(active, sum_up), 1.0)
        add(lambda: only(active, attention), 1.2)
        add(lambda: only(active, hand_out), 0.3)
        add(take_in)
        add(take_other)
        for f in (0, 1):
            add(functools.partial(out_product, f))

    def add_mlp(c):
        cuts = ((0, 256), (256, 256), (512, 384))

        def slot(i, which):
            return 6 + (c * 3 + i) * 7 + which

        def gate_up(k, i, f):
            cols, depth = pl.ds(*cuts[i]), pl.ds(f * half, half)
            rows = g[pl.ds(c * 16, 16), :, depth].reshape(256, half)
            value = dot_nt(rows, wgu[k, cols, depth]).reshape(4, 64, cuts[i][1])
            if f == 0:
                pg[k, c, :, :, cols] = value
                return
            pg[k, c, :, :, cols] += value
            if i == 2 and k == 0:
                extra = g[pl.ds(c * 16, 16), :, pl.ds(width, 128)].reshape(4, 64, 128).astype(F32)
                pg[0, c, :, :, pl.ds(768, 128)] += extra
            s1[c, k, :, :, cols] = pg[k, c, pl.ds(2 * (1 - c_), 2), :, cols].astype(BF16)
            wlink.send(slot(i, k), s1.at[c, k, :, :, cols], r1.at[c, k, :, :, cols], at.core_peer)

        def over_y(k, i):
            cols = pl.ds(*cuts[i])
            wlink.wait(slot(i, k), r1.at[c, k, :, :, cols], at.core_peer)
            value = pg[k, c, 2 * c_ + 1 - yl, :, cols] + r1[c, k, 1 - yl, :, cols].astype(F32)
            s2[c, k, :, cols] = value.astype(BF16)
            if i == 2 and k == 0:
                lanes = lane_ids(64)
                tile = value[:, 256:]
                s2[c, k, :, pl.ds(768, 128)] = split_sum(joined_sum(tile, lanes), lanes, tile).astype(BF16)
            wlink.send(slot(i, 2 + k), s2.at[c, k, :, cols], r2.at[c, k, :, cols], at.y_peer)

        def activate(i):
            cols = pl.ds(*cuts[i])
            sums = []
            for k in (0, 1):
                wlink.wait(slot(i, 2 + k), r2.at[c, k, :, cols], at.y_peer)
                total = pg[k, c, 2 * c_ + yl, :, cols] + r1[c, k, yl, :, cols].astype(F32)
                sums.append(total + r2[c, k, :, cols].astype(F32))
            if i == 2:
                norm = lax.rsqrt(joined_sum(sums[0][:, 256:], lane_ids(64)) / D + norm_eps)
                scale[c] = jnp.broadcast_to(norm, (64, 128))
            norm = scale[c, :, 0:1]
            gate, up = sums[0] * norm, sums[1] * norm
            mine = act.at[c, 2 * c_ + yl, :, cols]
            act[c, 2 * c_ + yl, :, cols] = (gate / (1.0 + jnp.exp(-gate)) * up).astype(BF16)
            wlink.send(slot(i, 4), mine, mine, at.y_peer)
            wlink.send(slot(i, 5), mine, mine, at.core_peer)

        def pass_on(i):
            other = act.at[c, 2 * c_ + 1 - yl, :, pl.ds(*cuts[i])]
            wlink.wait(slot(i, 4), other, at.y_peer)
            wlink.send(slot(i, 6), other, other, at.core_peer)

        def complete():
            for i in range(3):
                cols = pl.ds(*cuts[i])
                wlink.wait(slot(i, 5), act.at[c, 2 * (1 - c_) + yl, :, cols], at.core_peer)
                wlink.wait(slot(i, 6), act.at[c, 2 * (1 - c_) + 1 - yl, :, cols], at.core_peer)

        def down(i):
            rows = act[c].reshape(256, act.shape[3])
            cols = pl.ds(i * 1024, 1024)
            acc[pl.ds(c * 16, 16), :, cols] = dot_nn(rows, wd[:, cols]).reshape(16, 16, 1024)

        for i in (2, 0, 1):
            for k in (0, 1):
                for f in (0, 1):
                    add(functools.partial(gate_up, k, i, f), 0.03 + 0.06 * f)
                add(functools.partial(over_y, k, i), 0.07)
            add(functools.partial(activate, i), 0.2)
            add(functools.partial(pass_on, i))
        add(complete)
        for i in range(4):
            add(functools.partial(down, i))

    for c in (0, 1):
        add_gather(0, c)
        add_attention(c)
        add_scatter(0, c)
        add_gather(1, c)
        add_mlp(c)
        add_scatter(1, c)

    for place in ORDER:
        tasks[place][0]()
    for each in (glink, link, ylink, wlink):
        each.finish()
    for c in (0, 1):
        only(here(c), lambda c=c: ylink.finish(None, c))
        only((at.yl, c), lambda c=c: wlink.finish(None, c))


ORDER = [
    7, 158, 8, 9, 17, 18, 159, 160, 1, 10, 11, 6, 19, 12, 20, 21, 168, 13, 14, 169, 15, 23, 5, 24, 0, 16, 22,
    3, 162, 25, 161, 171, 163, 173, 170, 164, 26, 29, 27, 30, 172, 175, 31, 165, 166, 4, 167, 174, 176, 32,
    177, 180, 178, 181, 182, 33, 183, 28, 34, 184, 35, 36, 37, 41, 38, 57, 60, 40, 58, 61, 179, 39, 42, 46,
    59, 63, 45, 43, 62, 185, 49, 65, 47, 44, 64, 67, 66, 48, 68, 50, 53, 186, 187, 69, 188, 189, 192, 208,
    190, 51, 52, 71, 209, 210, 193, 213, 191, 211, 70, 216, 2, 212, 200, 196, 198, 54, 215, 72, 194, 195, 217,
    197, 218, 214, 219, 199, 201, 204, 220, 202, 221, 203, 222, 55, 75, 77, 73, 76, 85, 205, 223, 79, 78, 86,
    87, 81, 80, 89, 88, 83, 82, 206, 226, 228, 224, 227, 90, 84, 91, 236, 230, 92, 93, 237, 95, 111, 231, 106,
    98, 238, 229, 94, 96, 103, 99, 239, 97, 234, 232, 74, 225, 112, 104, 100, 235, 114, 233, 107, 105, 241,
    242, 115, 113, 240, 108, 243, 116, 101, 244, 246, 249, 254, 109, 117, 245, 250, 262, 247, 265, 251, 255,
    102, 263, 110, 248, 257, 118, 258, 256, 207, 266, 264, 119, 122, 259, 123, 267, 143, 147, 56, 121, 120,
    126, 252, 124, 141, 144, 127, 260, 125, 148, 142, 268, 129, 146, 151, 145, 128, 131, 253, 261, 135, 152,
    149, 269, 134, 132, 130, 150, 133, 270, 274, 273, 294, 298, 271, 272, 275, 276, 296, 292, 293, 277, 297,
    282, 295, 278, 138, 279, 155, 302, 281, 137, 283, 136, 284, 153, 300, 285, 301, 280, 154, 286, 299, 303,
    287, 306, 304, 289, 288, 139, 305, 156, 290, 291, 307, 140, 157, 308,
]


VM = pl.BlockSpec(memory_space=pltpu.VMEM)
ANY = pl.BlockSpec(memory_space=pl.ANY)
DMA = pltpu.SemaphoreType.DMA


def on_device(
    hidden_in,
    attn_gain,
    mlp_gain,
    w_query,
    w_key,
    w_value,
    w_out,
    w_gate,
    w_up,
    w_down,
    key_cache,
    value_cache,
    lengths,
):
    width = hidden_in.shape[1]
    units = w_gate.shape[1]
    padded = units + 64
    slots = key_cache.shape[1] * KV
    return pl.pallas_call(
        layer_kernel,
        out_shape=jax.ShapeDtypeStruct(hidden_in.shape, BF16),
        in_specs=[VM, VM, VM, pl.BlockSpec(memory_space=pltpu.SMEM)] + [ANY] * 9,
        out_specs=VM,
        scratch_shapes=[
            pltpu.VMEM((32, 16, width + 128), BF16),
            pltpu.VMEM((width, 256), BF16),
            pltpu.VMEM((128, width), BF16),
            pltpu.VMEM((256, width), BF16),
            pltpu.VMEM((2, padded, width), BF16),
            pltpu.VMEM((padded, width), BF16),
            pltpu.VMEM((4, slots, HD), BF16),
            pltpu.VMEM((4, slots, HD), BF16),
            pltpu.VMEM((32, 16, width), F32),
            pltpu.VMEM((TREE, 16, width // 2), BF16),
            pltpu.VMEM((TREE, 16, width // 2), BF16),
            pltpu.VMEM((2, 2, 16, width // 2), F32),
            pltpu.VMEM((6, 16, width // 2), BF16),
            pltpu.VMEM((6, 16, width // 2), BF16),
            pltpu.VMEM((2, 16, width), BF16),
            pltpu.VMEM((2, 16, width), BF16),
            pltpu.VMEM((2, 2, 128, 384), F32),
            pltpu.VMEM((2, 128, 384), BF16),
            pltpu.VMEM((3, 128, 384), BF16),
            pltpu.VMEM((128, 384), BF16),
            pltpu.VMEM((4, 128, 128), F32),
            pltpu.VMEM((512, 128), F32),
            pltpu.VMEM((32, 16, 128), BF16),
            pltpu.VMEM((32, 16, 128), BF16),
            pltpu.VMEM((512, 128), F32),
            pltpu.VMEM((256, 128), F32),
            pltpu.VMEM((256, 128), F32),
            pltpu.VMEM((2, 128, 128), F32),
            pltpu.VMEM((4, 128, 256), BF16),
            pltpu.VMEM((2, 2, 4, 64, padded), F32),
            pltpu.VMEM((2, 2, 2, 64, padded), BF16),
            pltpu.VMEM((2, 2, 2, 64, padded), BF16),
            pltpu.VMEM((2, 2, 64, padded), BF16),
            pltpu.VMEM((2, 2, 64, padded), BF16),
            pltpu.VMEM((2, 4, 64, padded), BF16),
            pltpu.VMEM((2, 64, 128), F32),
            DMA((9,)),
            DMA((TREE,)), DMA((TREE,)),
            DMA((TREE,)), DMA((TREE,)),
            DMA((16,)), DMA((16,)),
            DMA((48,)), DMA((48,)),
            DMA((1,)), DMA((1,)),
            DMA((1,)), DMA((1,)),
        ],
        compiler_params=pltpu.CompilerParams(
            collective_id=0, has_side_effects=True, vmem_limit_bytes=63 * 2**20
        ),
    )(
        hidden_in,
        attn_gain.reshape(-1, 128),
        mlp_gain.reshape(-1, 128),
        lengths,
        w_query,
        w_key.T,
        w_value.T,
        w_out,
        w_gate.T,
        w_up.T,
        w_down,
        key_cache.reshape(4, slots, HD),
        value_cache.reshape(4, slots, HD),
    )


def solution(mesh):
    return jax.shard_map(
        on_device,
        mesh=mesh,
        in_specs=(
            P("hidden", "width"),
            P("width"),
            P("width"),
            P("width", "hidden"),
            P("width", "hidden"),
            P("width", "hidden"),
            P("hidden", "width"),
            P("width", "hidden"),
            P("width", "hidden"),
            P("hidden", "width"),
            P(("width", "hidden"), None, None, None),
            P(("width", "hidden"), None, None, None),
            P(("width", "hidden")),
        ),
        out_specs=P("hidden", "width"),
        check_vma=False,
    )
```

```python
import functools
import math

import jax
import jax.numpy as jnp
from jax import lax
from jax.experimental import pallas as pl
from jax.experimental.pallas import tpu as pltpu
from jax.sharding import PartitionSpec as P

D = 16384
HEADS = 64
KV = 4
HD = 128
MESH = pl.DeviceIdType.MESH
F32 = jnp.float32
BF16 = jnp.bfloat16

rope_base = 500000.0
norm_eps = 1e-05

OFFS = (0, -1, 1, 2)


class Place:
    def __init__(self):
        self.w = lax.axis_index("width")
        self.h = lax.axis_index("hidden")
        self.x = lax.rem(self.h, 4)
        self.z = lax.rem(self.h // 4, 4)
        self.yh = self.h // 16
        self.core = lax.rem(self.w, 2)
        self.yl = self.w // 2
        self.partner = (self.w, lax.rem(self.h + 16, 32))
        self.core_peer = (self.w + 1 - 2 * self.core, self.h)
        self.y_peer = (lax.rem(self.w + 2, 4), self.h)
        self.far_peer = (lax.rem(self.w + 2, 4) + 1 - 2 * self.core, self.h)

    def block(self, c, f, p, q):
        dx, dz = (p, q) if f == 0 else (q, p)
        return c * 16 + lax.rem(self.z + (dz + 4), 4) * 4 + lax.rem(self.x + (dx + 4), 4)

    def neighbour(self, f, phase, sgn):
        p, q = (sgn, 0) if phase == 0 else (0, sgn)
        return (self.w, self.yh * 16 + self.block(0, f, p, q))

    def along(self, i):
        return (self.w, lax.rem(self.h + i, 32))


def greet(at):
    barrier = pltpu.get_barrier_semaphore()
    peers = [at.core_peer, at.y_peer, at.partner]
    peers += [at.neighbour(f, 0, places) for f in (0, 1) for places in (1, -1, 2)]
    for peer in peers:
        pl.semaphore_signal(barrier, inc=1, device_id=peer, device_id_type=MESH)
    return lambda: pl.semaphore_wait(barrier, len(peers))


class Link:
    def __init__(self, ssem, rsem, peer):
        self.ssem, self.rsem, self.peer, self.sent = ssem, rsem, peer, {}

    def copy(self, slot, src, dst, peer):
        return pltpu.make_async_remote_copy(
            src_ref=src,
            dst_ref=dst,
            send_sem=self.ssem.at[slot],
            recv_sem=self.rsem.at[slot],
            device_id=peer,
            device_id_type=MESH,
        )

    def send(self, slot, src, dst, peer, key=None, like=None):
        self.copy(slot, src, dst, peer).start()
        self.sent[(slot, key)] = like or (lambda: src)

    def wait(self, slot, dst, peer):
        self.copy(slot, dst, dst, peer).wait_recv()

    def finish(self, slots=None, key=None):
        for which in [w for w in self.sent if w[1] == key and (slots is None or w[0] in slots)]:
            like = self.sent.pop(which)()
            self.copy(which[0], like, like, self.peer).wait_send()


def only(flag, body):
    pl.when(flag[0] == flag[1])(body)


TREE = 60


def slots_of(c, f):
    return range((c * 2 + f) * 15, (c * 2 + f) * 15 + 15)


def slot_of(c, f, phase, j, d):
    base = (c * 2 + f) * 15
    if phase == 0:
        return base + {1: 0, -1: 1, 0: 2}[d]
    return base + 3 + OFFS.index(j) * 3 + {1: 0, -1: 1, 0: 2}[d]


class Gather:
    def __init__(self, at, link, g, c, f):
        half = g.shape[2] // 2 // 128 * 128
        self.cols = pl.ds(0, half) if f == 0 else pl.ds(half, g.shape[2] - half)
        self.at, self.link, self.g, self.c, self.f = at, link, g, c, f
        self.s = 1 if (c ^ f) == 0 else -1

    def ref(self, p, q):
        return self.g.at[self.at.block(self.c, self.f, p, q), :, self.cols]

    def send(self, phase, j, d, p, q, sgn):
        r = self.ref(p, q)
        slot = slot_of(self.c, self.f, phase, j, d)
        self.link.send(slot, r, r, self.at.neighbour(self.f, phase, sgn))

    def wait(self, phase, j, d, p, q, sgn):
        slot = slot_of(self.c, self.f, phase, j, d)
        self.link.wait(slot, self.ref(p, q), self.at.neighbour(self.f, phase, sgn))

    def way(self, j):
        return self.s if j in (0, -self.s) else -self.s

    def spread(self, j):
        self.send(1, j, self.s, j, 0, self.s)
        self.send(1, j, -self.s, j, 0, -self.s)

    def start(self):
        self.send(0, 0, self.s, 0, 0, self.s)
        self.send(0, 0, -self.s, 0, 0, -self.s)
        self.send(0, 0, 0, 0, 0, 2)
        self.spread(0)

    def first(self):
        s = self.s
        self.wait(0, 0, s, -s, 0, s)
        self.spread(-s)

    def second(self):
        s = self.s
        self.wait(0, 0, -s, s, 0, -s)
        self.spread(s)

    def third(self):
        self.wait(0, 0, 0, 2, 0, 2)
        self.spread(2)

    def relay(self, j):
        s = self.way(j)
        self.wait(1, j, s, j, -s, s)
        self.send(1, j, 0, j, -s, s)

    def end(self):
        for j in OFFS:
            s = self.way(j)
            self.wait(1, j, -s, j, s, -s)
        for j in OFFS:
            self.wait(1, j, 0, j, 2, self.way(j))

    def tasks(self, add):
        add(self.start)
        add(self.first)
        add(self.second)
        add(self.third)
        for j in (0, -self.s, self.s, 2):
            add(functools.partial(self.relay, j))


class Scatter:
    def __init__(self, at, link, acc, sbuf, rbuf, c, f):
        half = acc.shape[2] // 2
        self.cols = pl.ds(f * half, half)
        self.at, self.link, self.acc, self.sbuf, self.rbuf, self.c, self.f = at, link, acc, sbuf, rbuf, c, f
        self.s = 1 if (c ^ f) == 0 else -1

    def own(self, p, q):
        return self.acc[self.at.block(self.c, self.f, p, q), :, self.cols]

    def send(self, phase, j, d, sgn, value):
        slot = slot_of(self.c, self.f, phase, j, d)
        self.sbuf[slot] = value.astype(BF16)
        self.link.send(slot, self.sbuf.at[slot], self.rbuf.at[slot], self.at.neighbour(self.f, phase, sgn))

    def take(self, phase, j, d, sgn):
        slot = slot_of(self.c, self.f, phase, j, d)
        self.link.wait(slot, self.rbuf.at[slot], self.at.neighbour(self.f, phase, sgn))
        return self.rbuf[slot].astype(F32)

    def way(self, j):
        return self.s if j in (0, -self.s) else -self.s

    def column(self, j):
        s = self.way(j)
        return self.own(j, 0) + self.take(1, j, s, s) + self.take(1, j, -s, -s)

    def far(self, j):
        self.send(1, j, 0, self.way(j), self.own(j, 2))

    def back(self, j):
        s = self.way(j)
        self.send(1, j, -s, -s, self.own(j, -s))

    def on(self, j):
        s = self.way(j)
        self.send(1, j, s, s, self.own(j, s) + self.take(1, j, 0, s))

    def line_far(self):
        self.send(0, 0, 0, 2, self.column(2))

    def line_back(self):
        self.send(0, 0, -self.s, -self.s, self.column(-self.s))

    def line_on(self):
        self.send(0, 0, self.s, self.s, self.column(self.s))

    def total(self):
        value = self.column(0)
        for d, sgn in ((self.s, self.s), (-self.s, -self.s), (0, 2)):
            value = value + self.take(0, 0, d, sgn)
        return value

    def tasks(self, add):
        order = (2, -self.s, self.s, 0)
        for j in order:
            add(functools.partial(self.far, j), 0.06)
        for j in order:
            add(functools.partial(self.back, j), 0.06)
        for j in order:
            add(functools.partial(self.on, j), 0.08)
        add(self.line_far, 0.1)
        add(self.line_back, 0.1)
        add(self.line_on, 0.1)


def dot_nn(a, b):
    return jnp.dot(a, b, preferred_element_type=F32)


def dot_nt(a, b):
    return lax.dot_general(a, b, (((1,), (1,)), ((), ())), preferred_element_type=F32)


SS = 96


def split_sum(total, lanes, rest):
    high = total.astype(BF16).astype(F32)
    return jnp.where(lanes == SS, high, jnp.where(lanes == SS + 1, total - high, rest))


def joined_sum(tile, lanes):
    return jnp.sum(jnp.where((lanes == SS) | (lanes == SS + 1), tile, 0.0), axis=1, keepdims=True)


def lane_ids(rows):
    return lax.broadcasted_iota(jnp.int32, (rows, 128), 1)


def fill_own(g, block, values, gain, f):
    width = values.shape[1]
    tiles = width // 256
    for i in range(f * tiles, (f + 1) * tiles):
        cols = pl.ds(i * 128, 128)
        g[block, :, cols] = (values[:, i * 128 : (i + 1) * 128] * gain[i : i + 1]).astype(BF16)
    if f == 1:
        part = jnp.sum(values * values, axis=1, keepdims=True)
        lanes = lane_ids(values.shape[0])
        tail = split_sum(part, lanes, jnp.zeros(lanes.shape, F32))
        g[block, :, pl.ds(width, 128)] = tail.astype(BF16)


def exchange(at, link, src, dst, key, like):
    for i in range(1, 32):
        peer = at.along(i)
        link.send(0, src(peer[1]), dst(at.h), peer, key, like)


def exchanged(at, link, blocks):
    link.wait(0, blocks, at.partner)


def turn(values, cosine, sine):
    return values * cosine + pltpu.roll(values, HD // 2, 1) * sine


def attend(lengths, rqf, kc, vc, out):
    pairs = HEADS // 2
    lane = lax.broadcasted_iota(jnp.int32, (1, HD), 1)
    entry = lax.rem(lane, HD // 2).astype(F32)
    frequency = jnp.exp(entry * (-2.0 * math.log(rope_base) / HD))
    count = kc.shape[1]
    place = lax.broadcasted_iota(jnp.int32, (HEADS, count), 1)
    head_group = lax.rem(lax.broadcasted_iota(jnp.int32, (HEADS, count), 0), pairs) // (pairs // KV)
    same_group = lax.rem(place, KV) == head_group
    slot = place // KV
    factor = HD ** (-0.5)

    def widen(fresh):
        each = jnp.broadcast_to(fresh[:, None, :], (KV, pairs // KV, HD)).reshape(pairs, HD)
        return jnp.concatenate([each, each], axis=0)

    for r in range(4):
        def piece(t):
            return rqf[pl.ds(4 * t + r, pairs, stride=16), :]

        position = lengths[r]
        angle = frequency * position.astype(F32)
        cosine = jnp.cos(angle)
        sine = jnp.where(lane < HD // 2, -1.0, 1.0) * jnp.sin(angle)
        q = turn(jnp.concatenate([piece(0), piece(1)], axis=0), cosine, sine).astype(BF16)
        k_fresh = jnp.sum(piece(2).reshape(KV, pairs // KV, HD), axis=1)
        v_fresh = jnp.sum(piece(3).reshape(KV, pairs // KV, HD), axis=1)
        k_turned = turn(k_fresh, cosine, sine).astype(BF16).astype(F32)
        own = jnp.sum(q.astype(F32) * widen(k_turned), axis=1, keepdims=True) * factor
        visible = same_group & (slot < position)
        scores = jnp.where(visible, dot_nt(q, kc[r]) * factor, -jnp.inf)
        highest = jnp.maximum(jnp.max(scores, axis=1, keepdims=True), own)
        raised = jnp.exp(scores - highest)
        own_raised = jnp.exp(own - highest)
        total = jnp.sum(raised, axis=1, keepdims=True) + own_raised
        weights = (raised / total).astype(BF16)
        own_weight = (own_raised / total).astype(BF16).astype(F32)
        mixed = dot_nn(weights, vc[r]) + own_weight * widen(v_fresh)
        mixed = mixed.astype(BF16).astype(F32)
        for t in (0, 1):
            out[pl.ds(4 * t + r, pairs, stride=8), :] = mixed[t * pairs : (t + 1) * pairs]


def layer_kernel(
    hidden_ref, gain0, gain1, lengths, wq_hbm, wk_hbm, wv_hbm, wo_hbm, wg_hbm, wu_hbm, wd_hbm, kc_hbm, vc_hbm,
    out_ref,
    g, wq, wkv, wo, wgu, wd, kc, vc, acc, sbuf, rbuf, near, ysend, yrecv, res, hid,
    qkv, qkv_s, qkv_r, qkv_y, heads, msgf, msg, rq, rqf, msg2, rq2, attf, att,
    pg, s1, r1, s2, r2, act, scale,
    lsem, gss, grs, ssem, rsem, yss, yrs, wss, wrs, ass, ars, bss, brs,
):
    at = Place()
    enter = greet(at)
    width = hidden_ref.shape[1]
    units = wd_hbm.shape[0]
    half = width // 2
    loads = [
        pltpu.make_async_copy(src, dst, lsem.at[i])
        for i, (src, dst) in enumerate(
            (
                (wq_hbm, wq),
                (wk_hbm, wkv.at[pl.ds(0, 16)]),
                (wv_hbm, wkv.at[pl.ds(16, 16)]),
                (kc_hbm, kc),
                (vc_hbm, vc),
                (wo_hbm, wo),
                (wg_hbm, wgu.at[0, pl.ds(0, units)]),
                (wu_hbm, wgu.at[1, pl.ds(0, units)]),
                (wd_hbm, wd.at[pl.ds(0, units)]),
            )
        )
    ]
    for load in loads:
        load.start()
    hid[at.yh] = hidden_ref[...]
    for f in (0, 1):
        fill_own(g, at.h, hidden_ref[...].astype(F32), gain0[...].astype(F32), f)
    enter()
    pairs = ((gss, grs), (ssem, rsem), (yss, yrs), (wss, wrs), (ass, ars), (bss, brs))
    glink, link, ylink, wlink, alink, blink = (Link(a, b, at.partner) for a, b in pairs)
    c_, yl = at.core, at.yl
    tasks = []

    def add(body, cost=0.0):
        tasks.append((body, cost))

    def here(c):
        return (at.yh, c)

    def there(c):
        return (at.yh, 1 - c)

    def fresh_zeros():
        wkv[pl.ds(32, 96), :] = jnp.zeros((96, width), BF16)
        for k in (0, 1):
            wgu[k, pl.ds(units, 64), :] = jnp.zeros((64, width), BF16)
        wd[pl.ds(units, 64), :] = jnp.zeros((64, width), BF16)

    add(fresh_zeros, 0.6)

    def swap_hidden():
        mine = hid.at[at.yh]
        ylink.send(8, mine, mine, at.partner)

    def hidden_there():
        theirs = hid.at[1 - at.yh]
        ylink.wait(8, theirs, at.partner)

    add(swap_hidden)
    add(hidden_there)

    def add_loaded(which):
        def body():
            for load in which:
                load.wait()

        add(body)

    add_loaded(loads[:3])
    add_loaded(loads[3:5])
    add_loaded(loads[5:6])
    add_loaded(loads[6:])

    def add_gather(turn, c):
        halves = [Gather(at, glink, g, c, f) for f in (0, 1)]

        def slot(f):
            return c * 2 + f

        def own_rows():
            for f in (0, 1):
                mine = g.at[at.h, :, halves[f].cols]
                like = lambda f=f: g.at[0, :, halves[f].cols]
                ylink.send(slot(f), mine, mine, at.partner, c, like)

        def new_rows(f):
            fill_own(g, at.block(c, 0, 0, 0), res[c].astype(F32), gain1[...].astype(F32), f)

        if turn == 0:
            add(lambda: only(here(c), own_rows))
        else:
            for f in (0, 1):
                add(functools.partial(new_rows, f), 0.2)
        for f in (0, 1):
            def arrive(f=f):
                theirs = g.at[at.partner[1], :, halves[f].cols]
                only(there(c), lambda: ylink.wait(slot(f), theirs, at.partner))

            if turn == 0:
                add(arrive)
            halves[f].tasks(add)

        def finish():
            for f in (0, 1):
                glink.finish(slots_of(c, f))
            only(here(c), lambda: ylink.finish([slot(0), slot(1)], c))

        for f in (0, 1):
            add(halves[f].end)
        if turn == 0:
            add(finish)

    def add_scatter(turn, c):
        for f in (0, 1):
            one = Scatter(at, link, acc, sbuf, rbuf, c, f)
            one.tasks(add)
            slot = 4 + c * 2 + f if turn == 0 else 9 + f
            buf = c * 2 + f if turn == 0 else 4 + f
            cols = pl.ds(f * half, half)

            def total(one=one, f=f, slot=slot, buf=buf):
                near[c, f] = one.total()

                def pass_over():
                    ysend[buf] = near[c, f].astype(BF16)
                    ylink.send(slot, ysend.at[buf], yrecv.at[buf], at.partner, 1 - c, lambda: ysend.at[buf])

                if turn == 0:
                    ysend[buf] = near[c, f].astype(BF16)
                    ylink.send(slot, ysend.at[buf], yrecv.at[buf], at.partner)
                else:
                    only(there(c), pass_over)

            def last(f=f, slot=slot, buf=buf, cols=cols):
                def body():
                    ylink.wait(slot, yrecv.at[buf], at.partner)
                    value = near[c, f] + yrecv[buf].astype(F32)
                    out_ref[:, cols] = (res[c, :, cols].astype(F32) + value).astype(BF16)

                if turn == 0:
                    ylink.wait(slot, yrecv.at[buf], at.partner)
                    value = ysend[buf].astype(F32) + yrecv[buf].astype(F32)
                    res[c, :, cols] = (hid[c, :, cols].astype(F32) + value).astype(BF16)
                else:
                    only(here(c), body)

            add(total, 0.15)
            add(last, 0.1)
            if turn == 0:
                add(functools.partial(link.finish, slots_of(c, f)))

    def add_attention(c):
        active, passive = (at.yl, c), (at.yl, 1 - c)

        def project(f):
            cols = pl.ds(f * half, half)
            rows = g[pl.ds(c * 16, 16), :, cols].reshape(256, half)
            query = dot_nn(rows, wq[cols, :]).reshape(2, 128, 256)
            fresh = dot_nt(rows, wkv[:, cols]).reshape(2, 128, 128)
            if f == 0:
                qkv[c, :, :, pl.ds(0, 256)] = query
                qkv[c, :, :, pl.ds(256, 128)] = fresh
                return
            extra = g[pl.ds(c * 16, 16), :, pl.ds(width, 128)].reshape(2, 128, 128).astype(F32)
            qkv[c, :, :, pl.ds(0, 256)] += query
            qkv[c, :, :, pl.ds(256, 128)] += fresh + extra
            qkv_s[c] = qkv[c, 1 - c_].astype(BF16)
            wlink.send(2 * c, qkv_s.at[c], qkv_r.at[2 * c], at.core_peer)

        def over_y():
            def across():
                wlink.wait(2 * c, qkv_r.at[2 * c], at.core_peer)
                total = qkv[c, c_] + qkv_r[2 * c].astype(F32)
                lanes = lane_ids(128)
                tile = total[:, 256:]
                qkv_y[:, pl.ds(0, 256)] = total[:, :256].astype(BF16)
                qkv_y[:, pl.ds(256, 128)] = split_sum(joined_sum(tile, lanes), lanes, tile).astype(BF16)
                wlink.send(1, qkv_y, qkv_r.at[1], at.y_peer, 1 - c, lambda: qkv_y)

            only(passive, across)

        def sum_up():
            total = qkv[c, c_]
            for i, peer in ((2 * c, at.core_peer), (1, at.y_peer)):
                wlink.wait(i, qkv_r.at[i], peer)
                total = total + qkv_r[i].astype(F32)
            norm = lax.rsqrt(joined_sum(total[:, 256:], lane_ids(128)) / D + norm_eps)
            scaled = (total * norm).astype(BF16)
            row = lax.broadcasted_iota(jnp.int32, (128, 256), 0)
            col = lax.broadcasted_iota(jnp.int32, (128, 256), 1)
            wanted = 16 * (col // 128) + lax.rem(col, 16)
            placed = (row == wanted) & (lax.rem(col, 128) // 16 == lax.rem(at.h, 8))
            fresh = dot_nn(scaled[:, 256:], jnp.where(placed, 1.0, 0.0).astype(BF16))
            heads[0] = scaled[:, :128].astype(F32)
            heads[1] = scaled[:, 128:256].astype(F32)
            heads[2] = fresh[:, :128]
            heads[3] = fresh[:, 128:]
            for t in range(4):
                for r in range(4):
                    msgf[pl.ds(4 * t + r, 32, stride=16), :] = heads[t, pl.ds(r, 32, stride=4), :]
            msg[...] = msgf[...].astype(BF16).reshape(32, 16, 128)
            exchange(at, alink, lambda d: msg.at[d], lambda d: rq.at[d], c, lambda: msg.at[pl.ds(0, 31)])

        def eight(ref):
            return lambda d: ref.at[pl.ds(pl.multiple_of(d * 8, 8), 8)]

        def attention():
            exchanged(at, alink, rq.at[pl.ds(0, 31)])
            rq[at.h] = msg[at.h]
            rqf[...] = rq[...].astype(F32).reshape(512, 128)
            attend(lengths, rqf, kc, vc, msg2)
            exchange(at, blink, eight(msg2), eight(rq2), c, lambda: msg2.at[pl.ds(0, 248)])

        def hand_out():
            exchanged(at, blink, rq2.at[pl.ds(0, 248)])
            own8 = pl.ds(pl.multiple_of(at.h * 8, 8), 8)
            rq2[own8, :] = msg2[own8, :]
            for t in (0, 1):
                for r in range(4):
                    attf[t, pl.ds(r, 32, stride=4), :] = rq2[pl.ds(4 * t + r, 32, stride=8), :]
                att[at.w, :, pl.ds(t * 128, 128)] = attf[t].astype(BF16)
            for i, peer in enumerate((at.core_peer, at.y_peer)):
                wlink.send(3 + i, att.at[at.w], att.at[at.w], peer, c, lambda: att.at[0])
            alink.finish(None, c)
            blink.finish(None, c)

        def take_in():
            only(active, lambda: wlink.wait(3, att.at[at.core_peer[0]], at.core_peer))

            def across():
                part = att.at[at.y_peer[0]]
                wlink.wait(4, part, at.y_peer)
                wlink.send(5, part, part, at.core_peer, 1 - c, lambda: att.at[0])

            only(passive, across)

        def take_other():
            only(passive, lambda: wlink.wait(5, att.at[at.far_peer[0]], at.core_peer))

        def out_product(f):
            rows = att[pl.ds(2 * c, 2)].reshape(256, 256)
            for i in (2 * f, 2 * f + 1):
                cols = pl.ds(i * 1024, 1024)
                acc[pl.ds(c * 16, 16), :, cols] = dot_nn(rows, wo[:, cols]).reshape(16, 16, 1024)

        for f in (0, 1):
            add(functools.partial(project, f), 0.1 * f)
        add(over_y, 0.25)
        add(lambda: only(active, sum_up), 1.0)
        add(lambda: only(active, attention), 1.2)
        add(lambda: only(active, hand_out), 0.3)
        add(take_in)
        add(take_other)
        for f in (0, 1):
            add(functools.partial(out_product, f))

    def add_mlp(c):
        cuts = ((0, 256), (256, 256), (512, 384))

        def slot(i, which):
            return 6 + (c * 3 + i) * 7 + which

        def gate_up(k, i, f):
            cols, depth = pl.ds(*cuts[i]), pl.ds(f * half, half)
            rows = g[pl.ds(c * 16, 16), :, depth].reshape(256, half)
            value = dot_nt(rows, wgu[k, cols, depth]).reshape(4, 64, cuts[i][1])
            if f == 0:
                pg[k, c, :, :, cols] = value
                return
            pg[k, c, :, :, cols] += value
            if i == 2 and k == 0:
                extra = g[pl.ds(c * 16, 16), :, pl.ds(width, 128)].reshape(4, 64, 128).astype(F32)
                pg[0, c, :, :, pl.ds(768, 128)] += extra
            s1[c, k, :, :, cols] = pg[k, c, pl.ds(2 * (1 - c_), 2), :, cols].astype(BF16)
            wlink.send(slot(i, k), s1.at[c, k, :, :, cols], r1.at[c, k, :, :, cols], at.core_peer)

        def over_y(k, i):
            cols = pl.ds(*cuts[i])
            wlink.wait(slot(i, k), r1.at[c, k, :, :, cols], at.core_peer)
            value = pg[k, c, 2 * c_ + 1 - yl, :, cols] + r1[c, k, 1 - yl, :, cols].astype(F32)
            s2[c, k, :, cols] = value.astype(BF16)
            if i == 2 and k == 0:
                lanes = lane_ids(64)
                tile = value[:, 256:]
                s2[c, k, :, pl.ds(768, 128)] = split_sum(joined_sum(tile, lanes), lanes, tile).astype(BF16)
            wlink.send(slot(i, 2 + k), s2.at[c, k, :, cols], r2.at[c, k, :, cols], at.y_peer)

        def activate(i):
            cols = pl.ds(*cuts[i])
            sums = []
            for k in (0, 1):
                wlink.wait(slot(i, 2 + k), r2.at[c, k, :, cols], at.y_peer)
                total = pg[k, c, 2 * c_ + yl, :, cols] + r1[c, k, yl, :, cols].astype(F32)
                sums.append(total + r2[c, k, :, cols].astype(F32))
            if i == 2:
                norm = lax.rsqrt(joined_sum(sums[0][:, 256:], lane_ids(64)) / D + norm_eps)
                scale[c] = jnp.broadcast_to(norm, (64, 128))
            norm = scale[c, :, 0:1]
            gate, up = sums[0] * norm, sums[1] * norm
            mine = act.at[c, 2 * c_ + yl, :, cols]
            act[c, 2 * c_ + yl, :, cols] = (gate / (1.0 + jnp.exp(-gate)) * up).astype(BF16)
            wlink.send(slot(i, 4), mine, mine, at.y_peer)
            wlink.send(slot(i, 5), mine, mine, at.core_peer)

        def pass_on(i):
            other = act.at[c, 2 * c_ + 1 - yl, :, pl.ds(*cuts[i])]
            wlink.wait(slot(i, 4), other, at.y_peer)
            wlink.send(slot(i, 6), other, other, at.core_peer)

        def complete():
            for i in range(3):
                cols = pl.ds(*cuts[i])
                wlink.wait(slot(i, 5), act.at[c, 2 * (1 - c_) + yl, :, cols], at.core_peer)
                wlink.wait(slot(i, 6), act.at[c, 2 * (1 - c_) + 1 - yl, :, cols], at.core_peer)

        def down(i):
            rows = act[c].reshape(256, act.shape[3])
            cols = pl.ds(i * 1024, 1024)
            acc[pl.ds(c * 16, 16), :, cols] = dot_nn(rows, wd[:, cols]).reshape(16, 16, 1024)

        for i in (2, 0, 1):
            for k in (0, 1):
                for f in (0, 1):
                    add(functools.partial(gate_up, k, i, f), 0.03 + 0.06 * f)
                add(functools.partial(over_y, k, i), 0.07)
            add(functools.partial(activate, i), 0.2)
            add(functools.partial(pass_on, i))
        add(complete)
        for i in range(4):
            add(functools.partial(down, i))

    for c in (0, 1):
        add_gather(0, c)
        add_attention(c)
        add_scatter(0, c)
        add_gather(1, c)
        add_mlp(c)
        add_scatter(1, c)

    for place in ORDER:
        tasks[place][0]()
    for each in (glink, link, ylink, wlink):
        each.finish()
    for c in (0, 1):
        only(here(c), lambda c=c: ylink.finish(None, c))
        only((at.yl, c), lambda c=c: wlink.finish(None, c))


ORDER = [
    7, 158, 8, 9, 17, 18, 159, 160, 1, 10, 11, 6, 19, 12, 20, 21, 168, 13, 14, 169, 15, 23, 5, 24, 0, 16, 22,
    3, 162, 25, 161, 171, 163, 173, 170, 164, 26, 29, 27, 30, 172, 175, 31, 165, 166, 4, 167, 174, 176, 32,
    177, 180, 178, 181, 182, 33, 183, 28, 34, 184, 35, 36, 37, 41, 38, 57, 60, 40, 58, 61, 179, 39, 42, 46,
    59, 63, 45, 43, 62, 185, 49, 65, 47, 44, 64, 67, 66, 48, 68, 50, 53, 186, 187, 69, 188, 189, 192, 208,
    190, 51, 52, 71, 209, 210, 193, 213, 191, 211, 70, 216, 2, 212, 200, 196, 198, 54, 215, 72, 194, 195, 217,
    197, 218, 214, 219, 199, 201, 204, 220, 202, 221, 203, 222, 55, 75, 77, 73, 76, 85, 205, 223, 79, 78, 86,
    87, 81, 80, 89, 88, 83, 82, 206, 226, 228, 224, 227, 90, 84, 91, 236, 230, 92, 93, 237, 95, 111, 231, 106,
    98, 238, 229, 94, 96, 103, 99, 239, 97, 234, 232, 74, 225, 112, 104, 100, 235, 114, 233, 107, 105, 241,
    242, 115, 113, 240, 108, 243, 116, 101, 244, 246, 249, 254, 109, 117, 245, 250, 262, 247, 265, 251, 255,
    102, 263, 110, 248, 257, 118, 258, 256, 207, 266, 264, 119, 122, 259, 123, 267, 143, 147, 56, 121, 120,
    126, 252, 124, 141, 144, 127, 260, 125, 148, 142, 268, 129, 146, 151, 145, 128, 131, 253, 261, 135, 152,
    149, 269, 134, 132, 130, 150, 133, 270, 274, 273, 294, 298, 271, 272, 275, 276, 296, 292, 293, 277, 297,
    282, 295, 278, 138, 279, 155, 302, 281, 137, 283, 136, 284, 153, 300, 285, 301, 280, 154, 286, 299, 303,
    287, 306, 304, 289, 288, 139, 305, 156, 290, 291, 307, 140, 157, 308,
]


VM = pl.BlockSpec(memory_space=pltpu.VMEM)
ANY = pl.BlockSpec(memory_space=pl.ANY)
DMA = pltpu.SemaphoreType.DMA


def on_device(
    hidden_in,
    attn_gain,
    mlp_gain,
    w_query,
    w_key,
    w_value,
    w_out,
    w_gate,
    w_up,
    w_down,
    key_cache,
    value_cache,
    lengths,
):
    width = hidden_in.shape[1]
    units = w_gate.shape[1]
    padded = units + 64
    slots = key_cache.shape[1] * KV
    return pl.pallas_call(
        layer_kernel,
        out_shape=jax.ShapeDtypeStruct(hidden_in.shape, BF16),
        in_specs=[VM, VM, VM, pl.BlockSpec(memory_space=pltpu.SMEM)] + [ANY] * 9,
        out_specs=VM,
        scratch_shapes=[
            pltpu.VMEM((32, 16, width + 128), BF16),
            pltpu.VMEM((width, 256), BF16),
            pltpu.VMEM((128, width), BF16),
            pltpu.VMEM((256, width), BF16),
            pltpu.VMEM((2, padded, width), BF16),
            pltpu.VMEM((padded, width), BF16),
            pltpu.VMEM((4, slots, HD), BF16),
            pltpu.VMEM((4, slots, HD), BF16),
            pltpu.VMEM((32, 16, width), F32),
            pltpu.VMEM((TREE, 16, width // 2), BF16),
            pltpu.VMEM((TREE, 16, width // 2), BF16),
            pltpu.VMEM((2, 2, 16, width // 2), F32),
            pltpu.VMEM((6, 16, width // 2), BF16),
            pltpu.VMEM((6, 16, width // 2), BF16),
            pltpu.VMEM((2, 16, width), BF16),
            pltpu.VMEM((2, 16, width), BF16),
            pltpu.VMEM((2, 2, 128, 384), F32),
            pltpu.VMEM((2, 128, 384), BF16),
            pltpu.VMEM((3, 128, 384), BF16),
            pltpu.VMEM((128, 384), BF16),
            pltpu.VMEM((4, 128, 128), F32),
            pltpu.VMEM((512, 128), F32),
            pltpu.VMEM((32, 16, 128), BF16),
            pltpu.VMEM((32, 16, 128), BF16),
            pltpu.VMEM((512, 128), F32),
            pltpu.VMEM((256, 128), F32),
            pltpu.VMEM((256, 128), F32),
            pltpu.VMEM((2, 128, 128), F32),
            pltpu.VMEM((4, 128, 256), BF16),
            pltpu.VMEM((2, 2, 4, 64, padded), F32),
            pltpu.VMEM((2, 2, 2, 64, padded), BF16),
            pltpu.VMEM((2, 2, 2, 64, padded), BF16),
            pltpu.VMEM((2, 2, 64, padded), BF16),
            pltpu.VMEM((2, 2, 64, padded), BF16),
            pltpu.VMEM((2, 4, 64, padded), BF16),
            pltpu.VMEM((2, 64, 128), F32),
            DMA((9,)),
            DMA((TREE,)), DMA((TREE,)),
            DMA((TREE,)), DMA((TREE,)),
            DMA((16,)), DMA((16,)),
            DMA((48,)), DMA((48,)),
            DMA((1,)), DMA((1,)),
            DMA((1,)), DMA((1,)),
        ],
        compiler_params=pltpu.CompilerParams(
            collective_id=0, has_side_effects=True, vmem_limit_bytes=63 * 2**20
        ),
    )(
        hidden_in,
        attn_gain.reshape(-1, 128),
        mlp_gain.reshape(-1, 128),
        lengths,
        w_query,
        w_key.T,
        w_value.T,
        w_out,
        w_gate.T,
        w_up.T,
        w_down,
        key_cache.reshape(4, slots, HD),
        value_cache.reshape(4, slots, HD),
    )


def solution(mesh):
    return jax.shard_map(
        on_device,
        mesh=mesh,
        in_specs=(
            P("hidden", "width"),
            P("width"),
            P("width"),
            P("width", "hidden"),
            P("width", "hidden"),
            P("width", "hidden"),
            P("hidden", "width"),
            P("width", "hidden"),
            P("width", "hidden"),
            P("hidden", "width"),
            P(("width", "hidden"), None, None, None),
            P(("width", "hidden"), None, None, None),
            P(("width", "hidden")),
        ),
        out_specs=P("hidden", "width"),
        check_vma=False,
    )
```
